256 devices in a mesh: row: 64 (over z, y_lo, x), dev: 4 (over y_hi, core).
Axes of the slice: x: 4, y: 4 (y_hi: 2, y_lo: 2; y = y_hi * 2 + y_lo), z: 8, core: 2. Of those that a mesh axis runs over, the one named last changes fastest.
Arguments:
- rider_emb: bfloat16 [16384, 128], P('row'), may hold values from -40 to 40
- driver_emb: bfloat16 [32768, 128], P(('row', 'dev')), may hold values from -5 to 5
- log_a: float32 [16384], P('row'), may hold values from -0.7 to 0.7
- log_b: float32 [32768], P(('row', 'dev')), may hold values from -0.7 to 0.7
- rider_zone: int32 [128], P('row'), may hold values from 0 to 15, as said below
- driver_zone: int32 [256], P(('row', 'dev')), may hold values from 0 to 15, as said below
- zone_table: int32 [16, 16], replicated, may hold values from 0 to 1, as said below
Outputs:
- rider_pot: float32 [16384], P('row')
- driver_pot: float32 [32768], P(('row', 'dev'))
The draws below stay inside these ranges and needn't reach their ends.
Inputs may be any that keep to these rules, and one draw needn't show every extreme that they name: `rider_zone`: every one of the 16 zones names at least one rider block. `driver_zone`: every one of the 16 zones names at least one driver block. `zone_table`: the diagonal is all ones.
All inputs are finite; a program needn't handle non-finite values.
Results may differ from the reference program's by a relative error of at most 0.00035.
Values may be sent and summed in bfloat16 or wider, within the bound.
No kernel may reach another device: no remote copies, remote signals or barrier semaphores. Data moves between devices by JAX's collectives and lax.ppermute only.
A program may use at most 64 MiB of HBM per device.

```python
import math
from functools import partial
import jax
import jax.numpy as jnp
from jax import lax

E = 128
BLOCK = 128
ZONES = 16
ITERS = 3
RIDERS = 16384
DRIVERS = 32768
RBLOCKS = 128
DBLOCKS = 256


def draw_rider_emb(key, part):
    noise_key = jax.random.fold_in(key, 0)
    noise_rows = jnp.clip(jax.random.normal(noise_key, (RIDERS, E), jnp.float32), -4.0, 4.0)
    scaled = jnp.clip(noise_rows * (1.5 / math.sqrt(E)), -40.0, 40.0)
    return scaled.astype(jnp.bfloat16)


def covering_labels(key, count):
    order_key, fill_key = jax.random.split(key)
    counter = jnp.arange(count, dtype=jnp.int32)
    filler = jax.random.randint(fill_key, (count,), 0, ZONES, dtype=jnp.int32)
    labels = jnp.where(counter < ZONES, counter, filler)
    return jax.random.permutation(order_key, labels)


def draw_rider_zone(key, part):
    return covering_labels(jax.random.fold_in(key, 11), RBLOCKS)


def draw_driver_zone(key, part):
    return covering_labels(jax.random.fold_in(key, 23), DBLOCKS)


def draw_zone_table(key, part):
    links = jax.random.randint(jax.random.fold_in(key, 37), (ZONES, ZONES), 0, 2, dtype=jnp.int32)
    counter = jnp.arange(ZONES, dtype=jnp.int32)
    return jnp.where(counter[:, None] == counter[None, :], 1, links).astype(jnp.int32)


def levels(own_key, shape, shards, least, high):
    gain, own = 1.0, jax.random.fold_in(own_key, 6)
    for dim, shards_of in shards:
        heights = jnp.exp(jax.random.uniform(jax.random.fold_in(own, dim), (shards_of,), jnp.float32, least / len(shards), high / len(shards)))
        gain = gain * jnp.repeat(heights, shape[dim] // shards_of).reshape([-1 if axis == dim else 1 for axis in range(len(shape))])
    return gain


def bell_draw(own_key, dims, width, limit, cuts=(), held_as=jnp.bfloat16):
    gain = levels(own_key, dims, cuts, -0.22, 0.18) if cuts else 1.0
    drawn = jax.random.normal(own_key, dims, jnp.float32) * width * gain
    return jnp.minimum(jnp.maximum(drawn, -limit), limit).astype(held_as)


def setup_inputs(seed: int = 0) -> dict:
    keys = jax.random.split(jax.random.key(seed), 8)
    return {
        "rider_emb": draw_rider_emb(jax.random.fold_in(keys[7], 71), 0),
        "driver_emb": bell_draw(keys[1], (DRIVERS, E), 1.0, 5.0, ((0, 256),)),
        "log_a": jnp.clip(jax.random.uniform(keys[2], (RIDERS,), jnp.float32, -0.7, 0.7) * levels(keys[2], (RIDERS,), ((0, 64),), -0.4, 0.0), -0.7, 0.7),
        "log_b": jnp.clip(jax.random.uniform(keys[3], (DRIVERS,), jnp.float32, -0.7, 0.7) * levels(keys[3], (DRIVERS,), ((0, 256),), -0.4, 0.0), -0.7, 0.7),
        "rider_zone": draw_rider_zone(jax.random.fold_in(keys[7], 71), 0),
        "driver_zone": draw_driver_zone(jax.random.fold_in(keys[7], 71), 0),
        "zone_table": draw_zone_table(jax.random.fold_in(keys[7], 71), 0),
    }


NEG_FILL = -1e30


def masked_logsum(scores, feasible):
    peak_val = jnp.max(jnp.where(feasible, scores, NEG_FILL), axis=1)
    mass_sum = jnp.sum(jnp.where(feasible, jnp.exp(scores - peak_val[:, None]), 0.0), axis=1)
    return peak_val + jnp.log(mass_sum)


def rider_block(driver_emb, driver_tags, driver_pot, group):
    emb_rows, table_rows, mass_rows = group
    eta_cost = jnp.dot(emb_rows, driver_emb.T, preferred_element_type=jnp.float32)
    feasible = jnp.take(table_rows, driver_tags, axis=1) == 1
    return mass_rows - (masked_logsum(driver_pot[None, :] - eta_cost, feasible) - math.log(DRIVERS))


def driver_block(rider_emb, rider_tags, rider_pot, group):
    emb_rows, table_rows, mass_rows = group
    eta_cost = jnp.dot(emb_rows, rider_emb.T, preferred_element_type=jnp.float32)
    feasible = jnp.take(table_rows, rider_tags, axis=1) == 1
    return mass_rows - (masked_logsum(rider_pot[None, :] - eta_cost, feasible) - math.log(RIDERS))


def reference(rider_emb, driver_emb, log_a, log_b, rider_zone, driver_zone, zone_table):
    rider_tags = jnp.repeat(rider_zone, BLOCK)
    driver_tags = jnp.repeat(driver_zone, BLOCK)
    rider_table = zone_table[rider_tags]
    driver_table = zone_table.T[driver_tags]
    row_block = math.gcd(RIDERS, 512)
    col_block = math.gcd(DRIVERS, 512)
    rider_sets = (rider_emb.reshape(RIDERS // row_block, row_block, E),
                  rider_table.reshape(RIDERS // row_block, row_block, ZONES),
                  log_a.reshape(RIDERS // row_block, row_block))
    driver_sets = (driver_emb.reshape(DRIVERS // col_block, col_block, E),
                   driver_table.reshape(DRIVERS // col_block, col_block, ZONES),
                   log_b.reshape(DRIVERS // col_block, col_block))
    driver_pot = jnp.zeros((DRIVERS,), jnp.float32)
    rider_pot = jnp.zeros((RIDERS,), jnp.float32)
    for iteration in range(ITERS):
        rider_pot = lax.map(partial(rider_block, driver_emb, driver_tags, driver_pot), rider_sets).reshape(RIDERS)
        driver_pot = lax.map(partial(driver_block, rider_emb, rider_tags, rider_pot), driver_sets).reshape(DRIVERS)
    return rider_pot, driver_pot
```

```python
import math

import jax
import jax.numpy as jnp
from jax import lax
from jax.experimental import pallas as pl
from jax.experimental.pallas import tpu as pltpu
from jax.sharding import Mesh, PartitionSpec as P

AXES = ("z", "yl", "x", "yh", "c")
SIZES = (8, 2, 4, 2, 2)
RGROUP = ("yl", "x", "yh")
DGROUP = ("z", "c")

B = 128
RB = 8
DB = 16
GROUP = 16
PAY = B + 16
ITERS = 3
LOG_DRIVERS = math.log(32768)
LOG_RIDERS = math.log(16384)
PENALTY = 1e30
FLOOR = -1e29

F32 = jnp.float32
BF16 = jnp.bfloat16
VM = pl.BlockSpec(memory_space=pltpu.VMEM)
SM = pl.BlockSpec(memory_space=pltpu.SMEM)


def call(body, outs, ins, scratch=(), limit=40):
    return pl.pallas_call(
        body,
        out_shape=outs,
        in_specs=ins,
        out_specs=[VM] * len(outs),
        scratch_shapes=list(scratch),
        compiler_params=pltpu.CompilerParams(vmem_limit_bytes=limit * 2**20),
    )


def f32(*shape):
    return jax.ShapeDtypeStruct(shape, F32)


def bf16(*shape):
    return jax.ShapeDtypeStruct(shape, BF16)


def product(left, right):
    return lax.dot_general(left, right, (((1,), (1,)), ((), ())), preferred_element_type=F32)


def fold(block, op):
    rows = [block[8 * k : 8 * k + 8] for k in range(B // 8)]
    while len(rows) > 1:
        rows = [op(rows[2 * k], rows[2 * k + 1]) for k in range(len(rows) // 2)]
    return rows[0]


def with_zone(message):
    return jnp.concatenate([message[:B], jnp.concatenate([message[B:]] * (B // 16), axis=0)], axis=1)


def column(row):
    return jnp.broadcast_to(row, (B, B)).T


def pack_body(rider, driver, rzone, dzone, table, rider_out, driver_out):
    c = lax.axis_index("c")
    lane = lax.broadcasted_iota(jnp.int32, (16, B), 1)
    hot = jnp.where(lane == rzone[c], 1.0, 0.0)
    zone = dzone[0]
    shut = jnp.zeros((16, B), F32)
    for k in range(16):
        shut = jnp.where((lane == k) & (table[k, zone] != 1), PENALTY, shut)
    mine = rider[c]
    for k in range(8):
        rider_out[k, :B, :] = mine
        rider_out[k, B:, :] = hot.astype(BF16)
        driver_out[k, :B, :] = driver[...]
        driver_out[k, B:, :] = shut.astype(BF16)


def rider_first_body(rider, own, other, log_a, out):
    c = lax.axis_index("c")

    def pair(p, carry):
        right = jnp.concatenate([with_zone(rider[2 * p]), with_zone(rider[2 * p + 1])], axis=0)
        peak = jnp.full((8, 2 * B), -3e38, F32)
        mass = jnp.zeros((8, 2 * B), F32)
        for z in range(8):
            for source in (own, other):
                cost = product(with_zone(source[z]), right)
                fresh = jnp.maximum(peak, -fold(cost, jnp.minimum))
                terms = jnp.exp(-cost - jnp.concatenate([fresh] * 16, axis=0))
                mass = mass * jnp.exp(peak - fresh) + fold(terms, jnp.add)
                peak = fresh
        top = jnp.max(peak, axis=0, keepdims=True)
        mass = jnp.sum(mass * jnp.exp(peak - top), axis=0, keepdims=True)
        for h in range(2):
            out[0, pl.ds(2 * p + h, 1), :] = top[:, h * B : (h + 1) * B]
            out[0, pl.ds(8 + 2 * p + h, 1), :] = mass[:, h * B : (h + 1) * B]
        return carry

    lax.fori_loop(0, RB // 2, pair, 0)
    out[0, 16:24, :] = jnp.broadcast_to(log_a[pl.ds(c, 1), :], (8, B))
    for k in range(1, GROUP):
        out[k] = out[0]


def driver_first_body(sums, rider, own, other, log_b, out, kernel, peaks, pots, ucol, right):
    c = lax.axis_index("c")
    peak = sums[0, 0:8]
    for k in range(1, GROUP):
        peak = jnp.maximum(peak, sums[k, 0:8])
    mass = jnp.zeros((8, B), F32)
    for k in range(GROUP):
        mass = mass + sums[k, 8:16] * jnp.exp(sums[k, 0:8] - peak)
    log_a = jnp.concatenate([sums[2 * k, 16:17] for k in range(RB)], axis=0)
    pot = log_a - (peak + jnp.log(mass) - LOG_DRIVERS)
    pots[0:8] = pot
    pots[8:16] = log_a
    for r in range(RB):
        ucol[r * B : (r + 1) * B, :] = column(pot[r : r + 1])

    def pair(z, carry):
        right[pl.ds(pl.multiple_of(c * B, B), B), :] = with_zone(own[z])
        right[pl.ds(pl.multiple_of((1 - c) * B, B), B), :] = with_zone(other[z])
        rhs = right[...]
        lanes = pl.ds(pl.multiple_of(z * 2 * B, 2 * B), 2 * B)
        high = jnp.full((8, 2 * B), FLOOR, F32)
        for r in range(RB):
            u = ucol[r * B : (r + 1) * B, :]
            score = jnp.concatenate([u, u], axis=1) - product(with_zone(rider[r]), rhs)
            kernel[r * B : (r + 1) * B, lanes] = score
            high = jnp.maximum(high, fold(score, jnp.maximum))
        top = jnp.max(high, axis=0, keepdims=True)
        total = jnp.zeros((8, 2 * B), F32)
        for r in range(RB):
            term = jnp.exp(kernel[r * B : (r + 1) * B, lanes] - top)
            kernel[r * B : (r + 1) * B, lanes] = term
            total = total + fold(term, jnp.add)
        total = jnp.sum(total, axis=0, keepdims=True)
        for h in range(2):
            out[0, pl.ds(2 * z + h, 1), :] = top[:, h * B : (h + 1) * B]
            out[0, pl.ds(16 + 2 * z + h, 1), :] = total[:, h * B : (h + 1) * B]
        return carry

    lax.fori_loop(0, DB // 2, pair, 0)
    out[0, 32:40, :] = jnp.broadcast_to(log_b[...], (8, B))
    peaks[...] = out[0, 0:16]
    for k in range(1, GROUP):
        out[k] = out[0]


def row_sums(kernel, weight, out):
    def block(r, carry):
        rows = pl.ds(pl.multiple_of(r * B, B), B)
        acc = kernel[rows, 0:B] * weight[0:1]
        for k in range(1, DB):
            acc = acc + kernel[rows, k * B : (k + 1) * B] * weight[k : k + 1]
        out[0, pl.ds(r, 1), :] = jnp.sum(acc.T, axis=0, keepdims=True)
        return carry

    lax.fori_loop(0, RB, block, 0)
    for k in range(1, GROUP):
        out[k] = out[0]


def column_sums(kernel, fcol):
    def block(r, acc):
        for k in range(B // 8):
            rows = pl.ds(pl.multiple_of(r * B + 8 * k, 8), 8)
            f = fcol[rows, :]
            acc = tuple(a + kernel[rows, j * B : (j + 1) * B] * f for j, a in enumerate(acc))
        return acc

    return lax.fori_loop(0, RB, block, tuple(jnp.zeros((8, B), F32) for _ in range(DB)))


def rider_second_body(sums, peaks, kernel, out, state, weight):
    peak = sums[0, 0:16]
    for k in range(1, GROUP):
        peak = jnp.maximum(peak, sums[k, 0:16])
    mass = jnp.zeros((DB, B), F32)
    for k in range(GROUP):
        mass = mass + sums[k, 16:32] * jnp.exp(sums[k, 0:16] - peak)
    log_b = jnp.concatenate([sums[k, 32:33] for k in range(GROUP)], axis=0)
    pot = log_b - (peak + jnp.log(mass) - LOG_RIDERS)
    scale = jnp.exp(pot + peaks[...])
    state[0:16] = pot
    state[16:32] = log_b
    state[32:48] = scale
    weight[...] = scale
    row_sums(kernel, weight, out)


def total_of(sums):
    parts = [sums[k] for k in range(GROUP)]
    while len(parts) > 1:
        parts = [parts[2 * k] + parts[2 * k + 1] for k in range(len(parts) // 2)]
    return parts[0]


def driver_next_body(sums, pots, state, kernel, out, fcol):
    f = jnp.exp(pots[8:16] + LOG_DRIVERS) / total_of(sums)
    for r in range(RB):
        fcol[r * B : (r + 1) * B, :] = column(f[r : r + 1])
    acc = column_sums(kernel, fcol)
    rows = jnp.concatenate([jnp.sum(a, axis=0, keepdims=True) for a in acc], axis=0)
    rows = rows * state[32:48]
    for k in range(GROUP):
        out[k] = rows


def rider_next_body(sums, state, kernel, out, weight):
    weight[...] = state[32:48] * (jnp.exp(state[16:32] + LOG_RIDERS) / total_of(sums))
    row_sums(kernel, weight, out)


def driver_last_body(sums, pots, state, kernel, out, mine, fcol):
    block = lax.axis_index("yl") * 4 + lax.axis_index("x")
    total = total_of(sums)
    log_a = pots[8:16]
    f = jnp.exp(log_a + LOG_DRIVERS) / total
    for r in range(RB):
        fcol[r * B : (r + 1) * B, :] = column(f[r : r + 1])
    pot = pots[0:8] + (log_a + LOG_DRIVERS - jnp.log(total))
    row = lax.broadcasted_iota(jnp.int32, (8, B), 0)
    mine[...] = jnp.broadcast_to(jnp.sum(jnp.where(row == block, pot, 0.0), axis=0, keepdims=True), (8, B))
    acc = column_sums(kernel, fcol)
    for k in range(DB):
        out[k] = jnp.broadcast_to(jnp.sum(acc[k], axis=0, keepdims=True) * state[32 + k : 33 + k], (8, B))


def finish_body(sums, state, mine, other, rider_pot, driver_pot):
    c = lax.axis_index("c")
    block = lax.axis_index("z") * 2 + c
    total = total_of(sums)[0:1]
    pot = state[pl.ds(block, 1), :]
    log_b = state[pl.ds(16 + block, 1), :]
    driver_pot[...] = pot + (log_b + LOG_RIDERS - jnp.log(total))
    rider_pot[pl.ds(c, 1), :] = mine[0:1]
    rider_pot[pl.ds(1 - c, 1), :] = other[0:1]


def exchange(message, axes):
    return lax.all_to_all(message, axes, 0, 0, tiled=True)


def swap_core(value):
    return lax.ppermute(value, "c", [(0, 1), (1, 0)])


def per_device(rider_emb, driver_emb, log_a, log_b, rider_zone, driver_zone, zone_table):
    rider_msg, driver_msg = call(
        pack_body, [bf16(8, PAY, B), bf16(8, PAY, B)], [VM, VM, SM, SM, SM]
    )(rider_emb.reshape(2, B, B), driver_emb, rider_zone, driver_zone, zone_table)
    own = exchange(driver_msg, ("z",))
    other = swap_core(own)
    rider = exchange(rider_msg, ("yl", "x"))
    (message,) = call(rider_first_body, [f32(GROUP, 24, B)], [VM] * 4)(
        rider, own, other, log_a.reshape(2, B)
    )
    sums = exchange(message, RGROUP)
    message, kernel, peaks, pots = call(
        driver_first_body,
        [f32(GROUP, 40, B), f32(RB * B, DB * B), f32(DB, B), f32(16, B)],
        [VM] * 5,
        [pltpu.VMEM((RB * B, B), F32), pltpu.VMEM((2 * B, 2 * B), BF16)],
    )(sums, rider, own, other, log_b.reshape(1, B))
    sums = exchange(message, DGROUP)
    weights = [pltpu.VMEM((DB, B), F32)]
    columns = [pltpu.VMEM((RB * B, B), F32)]
    message, state = call(
        rider_second_body, [f32(GROUP, 8, B), f32(48, B)], [VM] * 3, weights
    )(sums, peaks, kernel)
    sums = exchange(message, RGROUP)
    for _ in range(ITERS - 2):
        (message,) = call(driver_next_body, [f32(GROUP, DB, B)], [VM] * 4, columns)(
            sums, pots, state, kernel
        )
        sums = exchange(message, DGROUP)
        (message,) = call(rider_next_body, [f32(GROUP, 8, B)], [VM] * 3, weights)(
            sums, state, kernel
        )
        sums = exchange(message, RGROUP)
    message, mine = call(
        driver_last_body, [f32(GROUP, 8, B), f32(8, B)], [VM] * 4, columns
    )(sums, pots, state, kernel)
    theirs = swap_core(mine)
    sums = exchange(message, DGROUP)
    rider_pot, driver_pot = call(finish_body, [f32(2, B), f32(1, B)], [VM] * 4)(
        sums, state, mine, theirs
    )
    return rider_pot.reshape(2 * B), driver_pot.reshape(B)


def solution(mesh):
    fine = Mesh(mesh.devices.reshape(SIZES), AXES)
    row, every = ("z", "yl", "x"), AXES
    placed = (
        P(row, None),
        P(every, None),
        P(row),
        P(every),
        P(row),
        P(every),
        P(),
    )
    return jax.shard_map(
        per_device,
        mesh=fine,
        in_specs=placed,
        out_specs=(P(row), P(every)),
        check_vma=False,
    )
```

```python
import math

import jax
import jax.numpy as jnp
from jax import lax
from jax.experimental import pallas as pl
from jax.experimental.pallas import tpu as pltpu
from jax.sharding import Mesh, PartitionSpec as P

AXES = ("z", "yl", "x", "yh", "c")
SIZES = (8, 2, 4, 2, 2)
RGROUP = ("yl", "x", "yh", "c")
DGROUP = ("z",)
RPEERS = 32
DPEERS = 8

B = 128
RB = 16
DB = 8
PAY = B + 16
ITERS = 3
LOG_DRIVERS = math.log(32768)
LOG_RIDERS = math.log(16384)
PENALTY = 1e30
FLOOR = -1e29
TINY = 1e-37

F32 = jnp.float32
BF16 = jnp.bfloat16
VM = pl.BlockSpec(memory_space=pltpu.VMEM)
FAR = pl.BlockSpec(memory_space=pltpu.HBM)


def call(body, outs, ins, scratch=(), limit=40, to=VM):
    return pl.pallas_call(
        body,
        out_shape=outs,
        in_specs=ins,
        out_specs=[to] * len(outs),
        scratch_shapes=list(scratch),
        compiler_params=pltpu.CompilerParams(vmem_limit_bytes=limit * 2**20),
    )


def f32(*shape):
    return jax.ShapeDtypeStruct(shape, F32)


def bf16(*shape):
    return jax.ShapeDtypeStruct(shape, BF16)


def product(left, right):
    return lax.dot_general(left, right, (((1,), (1,)), ((), ())), preferred_element_type=F32)


def tree(parts, op):
    while len(parts) > 1:
        parts = [op(parts[2 * k], parts[2 * k + 1]) for k in range(len(parts) // 2)]
    return parts[0]


def fold(block, op):
    return tree([block[8 * k : 8 * k + 8] for k in range(B // 8)], op)


def column(row):
    return jnp.broadcast_to(row, (B, B)).T


def three_parts(value):
    high = value.astype(BF16)
    rest = value - high.astype(F32)
    middle = rest.astype(BF16)
    return high, middle, (rest - middle.astype(F32)).astype(BF16)


def zone_rows(message):
    return jnp.broadcast_to(message[B : B + 1].astype(F32), (16, B)).astype(BF16)


def weight_row(message):
    tail = message[B:].astype(F32)
    return (tail[1:2] + tail[2:3]) + tail[3:4]


def with_zone(message, zone):
    return jnp.concatenate([message[:B], jnp.concatenate([zone] * (B // 16), axis=0)], axis=1)


def tail_rows(zone_row, log_row):
    row = lax.broadcasted_iota(jnp.int32, (16, B), 0)
    tail = jnp.where(row == 0, zone_row, 0.0)
    for k, part in enumerate(three_parts(log_row)):
        tail = jnp.where(row == k + 1, part.astype(F32), tail)
    return tail.astype(BF16)


def pack_body(rider, driver, log_a, log_b, rzone, dzone, table, rider_out, driver_out,
              a_row, b_row, rz, dz, tab, tails, sems):
    c = lax.axis_index("c")
    small = [
        pltpu.make_async_copy(log_a.at[pl.ds(c, 1)], a_row, sems.at[0]),
        pltpu.make_async_copy(log_b, b_row, sems.at[1]),
        pltpu.make_async_copy(rzone, rz, sems.at[2]),
        pltpu.make_async_copy(dzone, dz, sems.at[3]),
        pltpu.make_async_copy(table, tab, sems.at[4]),
    ]
    for copy in small:
        copy.start()
    large = []
    for k in range(8):
        large.append(pltpu.make_async_copy(rider.at[c], rider_out.at[k, pl.ds(0, B)], sems.at[5 + k]))
        large.append(pltpu.make_async_copy(driver, driver_out.at[k, pl.ds(0, B)], sems.at[13 + k]))
    for copy in large:
        copy.start()
    for copy in small:
        copy.wait()
    lane = lax.broadcasted_iota(jnp.int32, (16, B), 1)
    hot = jnp.where(lane == rz[c], 1.0, 0.0)
    zone = dz[0]
    shut = jnp.zeros((16, B), F32)
    for k in range(16):
        shut = jnp.where((lane == k) & (tab[k, zone] != 1), PENALTY, shut)
    tails[0] = tail_rows(hot, a_row[...])
    tails[1] = tail_rows(shut, b_row[...])
    ends = []
    for k in range(8):
        ends.append(pltpu.make_async_copy(tails.at[0], rider_out.at[k, pl.ds(B, 16)], sems.at[21 + k]))
        ends.append(pltpu.make_async_copy(tails.at[1], driver_out.at[k, pl.ds(B, 16)], sems.at[29 + k]))
    for copy in ends:
        copy.start()
    for copy in large + ends:
        copy.wait()


def rider_first_body(own, other, driver, out, dzone):
    c = lax.axis_index("c")
    for z in range(DB):
        dzone[z] = zone_rows(driver[z])

    def pair(p, carry):
        mine, theirs = own[p], other[p]
        right = jnp.concatenate(
            [with_zone(mine, zone_rows(mine)), with_zone(theirs, zone_rows(theirs))], axis=0
        )
        peak = jnp.full((8, 2 * B), -3e38, F32)
        mass = jnp.zeros((8, 2 * B), F32)
        for z in range(DB):
            cost = product(with_zone(driver[z], dzone[z]), right)
            fresh = jnp.maximum(peak, -fold(cost, jnp.minimum))
            terms = jnp.exp(-cost - jnp.concatenate([fresh] * 16, axis=0))
            mass = mass * jnp.exp(peak - fresh) + fold(terms, jnp.add)
            peak = fresh
        top = jnp.max(peak, axis=0, keepdims=True)
        mass = jnp.sum(mass * jnp.exp(peak - top), axis=0, keepdims=True)
        total = top + jnp.log(mass)
        out[0, pl.ds(2 * p + c, 1), :] = total[:, :B]
        out[0, pl.ds(2 * p + 1 - c, 1), :] = total[:, B:]
        return carry

    lax.fori_loop(0, RB // 2, pair, 0)
    for k in range(1, RPEERS):
        out[k] = out[0]


def log_total(sums, peers):
    parts = [sums[k] for k in range(peers)]
    peak = tree(parts, jnp.maximum)
    return peak + jnp.log(tree([jnp.exp(part - peak) for part in parts], jnp.add))


def total_of(sums, peers):
    return tree([sums[k] for k in range(peers)], jnp.add)


def driver_first_body(sums, own, other, driver, out, kernel, peaks, pots, ucol):
    c = lax.axis_index("c")
    for p in range(RB // 2):
        pots[pl.ds(RB + 2 * p + c, 1), :] = weight_row(own[p])
        pots[pl.ds(RB + 2 * p + 1 - c, 1), :] = weight_row(other[p])
    pots[0:RB] = pots[RB:] - (log_total(sums, RPEERS) - LOG_DRIVERS)
    for p in range(RB // 2):
        ucol[2 * p * B : (2 * p + 1) * B, :] = column(pots[pl.ds(2 * p + c, 1), :])
        ucol[(2 * p + 1) * B : (2 * p + 2) * B, :] = column(pots[pl.ds(2 * p + 1 - c, 1), :])

    def pair(h, carry):
        one, two = driver[2 * h], driver[2 * h + 1]
        right = jnp.concatenate(
            [with_zone(one, zone_rows(one)), with_zone(two, zone_rows(two))], axis=0
        )
        lanes = pl.ds(pl.multiple_of(h * 2 * B, 2 * B), 2 * B)
        high = jnp.full((8, 2 * B), FLOOR, F32)
        for r in range(RB):
            u = ucol[r * B : (r + 1) * B, :]
            left = own[r // 2] if r % 2 == 0 else other[r // 2]
            score = jnp.concatenate([u, u], axis=1) - product(with_zone(left, zone_rows(left)), right)
            kernel[r * B : (r + 1) * B, lanes] = score
            high = jnp.maximum(high, fold(score, jnp.maximum))
        top = jnp.max(high, axis=0, keepdims=True)
        total = jnp.zeros((8, 2 * B), F32)
        for r in range(RB):
            term = jnp.exp(kernel[r * B : (r + 1) * B, lanes] - top)
            kernel[r * B : (r + 1) * B, lanes] = term
            total = total + fold(term, jnp.add)
        total = top + jnp.log(jnp.maximum(jnp.sum(total, axis=0, keepdims=True), TINY))
        for k in range(2):
            peaks[pl.ds(2 * h + k, 1), :] = top[:, k * B : (k + 1) * B]
            out[0, pl.ds(2 * h + k, 1), :] = total[:, k * B : (k + 1) * B]
        return carry

    lax.fori_loop(0, DB // 2, pair, 0)
    for k in range(1, DPEERS):
        out[k] = out[0]


def row_sums(kernel, weight, out):
    c = lax.axis_index("c")

    def block(r, carry):
        rows = pl.ds(pl.multiple_of(r * B, B), B)
        acc = kernel[rows, 0:B] * weight[0:1]
        for k in range(1, DB):
            acc = acc + kernel[rows, k * B : (k + 1) * B] * weight[k : k + 1]
        place = r + c - 2 * c * (r % 2)
        out[0, pl.ds(place, 1), :] = jnp.sum(acc.T, axis=0, keepdims=True)
        return carry

    lax.fori_loop(0, RB, block, 0)
    for k in range(1, RPEERS):
        out[k] = out[0]


def column_sums(kernel, fcol, state):
    def block(r, acc):
        for k in range(B // 8):
            rows = pl.ds(pl.multiple_of(r * B + 8 * k, 8), 8)
            f = fcol[rows, :]
            acc = tuple(a + kernel[rows, j * B : (j + 1) * B] * f for j, a in enumerate(acc))
        return acc

    acc = lax.fori_loop(0, RB, block, tuple(jnp.zeros((8, B), F32) for _ in range(DB)))
    rows = jnp.concatenate([jnp.sum(a, axis=0, keepdims=True) for a in acc], axis=0)
    return rows * state[2 * DB : 3 * DB]


def rider_second_body(sums, peaks, driver, kernel, out, state, weight):
    log_b = jnp.concatenate([weight_row(driver[k]) for k in range(DB)], axis=0)
    pot = log_b - (log_total(sums, DPEERS) - LOG_RIDERS)
    scale = jnp.exp(pot + peaks[...])
    state[0:DB] = pot
    state[DB : 2 * DB] = log_b
    state[2 * DB : 3 * DB] = scale
    weight[...] = scale
    row_sums(kernel, weight, out)


def spread_columns(f, fcol, hold):
    c = lax.axis_index("c")
    hold[...] = f
    for p in range(RB // 2):
        fcol[2 * p * B : (2 * p + 1) * B, :] = column(hold[pl.ds(2 * p + c, 1), :])
        fcol[(2 * p + 1) * B : (2 * p + 2) * B, :] = column(hold[pl.ds(2 * p + 1 - c, 1), :])


def driver_next_body(sums, pots, state, kernel, out, fcol, hold):
    f = jnp.exp(pots[RB:] + LOG_DRIVERS) / total_of(sums, RPEERS)
    spread_columns(f, fcol, hold)
    rows = column_sums(kernel, fcol, state)
    for k in range(DPEERS):
        out[k] = rows


def rider_next_body(sums, state, kernel, out, weight):
    g = jnp.exp(state[DB : 2 * DB] + LOG_RIDERS) / total_of(sums, DPEERS)
    weight[...] = state[2 * DB : 3 * DB] * g
    row_sums(kernel, weight, out)


def driver_last_body(sums, pots, state, kernel, out, rider_pot, fcol, hold):
    total = total_of(sums, RPEERS)
    log_a = pots[RB:]
    hold[...] = pots[0:RB] + (log_a + LOG_DRIVERS - jnp.log(total))
    block = lax.axis_index("yl") * 4 + lax.axis_index("x")
    rider_pot[0:1] = hold[pl.ds(2 * block, 1), :]
    rider_pot[1:2] = hold[pl.ds(2 * block + 1, 1), :]
    spread_columns(jnp.exp(log_a + LOG_DRIVERS) / total, fcol, hold)
    rows = column_sums(kernel, fcol, state)
    for k in range(DPEERS):
        out[k] = jnp.broadcast_to(rows[k : k + 1], (8, B))


def finish_body(sums, state, driver_pot):
    z = lax.axis_index("z")
    pot = state[pl.ds(z, 1), :]
    log_b = state[pl.ds(DB + z, 1), :]
    driver_pot[...] = pot + (log_b + LOG_RIDERS - jnp.log(total_of(sums, DPEERS)[0:1]))


def exchange(message, axes):
    return lax.all_to_all(message, axes, 0, 0, tiled=True)


def swap_core(value):
    return lax.ppermute(value, "c", [(0, 1), (1, 0)])


def per_device(rider_emb, driver_emb, log_a, log_b, rider_zone, driver_zone, zone_table):
    rider_msg, driver_msg = call(
        pack_body,
        [bf16(8, PAY, B), bf16(8, PAY, B)],
        [FAR] * 7,
        [
            pltpu.VMEM((1, B), F32),
            pltpu.VMEM((1, B), F32),
            pltpu.SMEM((2,), jnp.int32),
            pltpu.SMEM((1,), jnp.int32),
            pltpu.SMEM((16, 16), jnp.int32),
            pltpu.VMEM((2, 16, B), BF16),
            pltpu.SemaphoreType.DMA((37,)),
        ],
        limit=60,
        to=FAR,
    )(
        rider_emb.reshape(2, B, B), driver_emb, log_a.reshape(2, B), log_b.reshape(1, B),
        rider_zone, driver_zone, zone_table,
    )
    own = exchange(rider_msg, ("yl", "x"))
    other = swap_core(own)
    driver = exchange(driver_msg, ("z",))
    (message,) = call(
        rider_first_body, [f32(RPEERS, RB, B)], [VM] * 3, [pltpu.VMEM((DB, 16, B), BF16)]
    )(own, other, driver)
    sums = exchange(message, RGROUP)
    columns = pltpu.VMEM((RB * B, B), F32)
    message, kernel, peaks, pots = call(
        driver_first_body,
        [f32(DPEERS, DB, B), f32(RB * B, DB * B), f32(DB, B), f32(2 * RB, B)],
        [VM] * 4,
        [columns],
    )(sums, own, other, driver)
    sums = exchange(message, DGROUP)
    weights = [pltpu.VMEM((DB, B), F32)]
    columns = [columns, pltpu.VMEM((RB, B), F32)]
    message, state = call(
        rider_second_body, [f32(RPEERS, RB, B), f32(3 * DB, B)], [VM] * 4, weights
    )(sums, peaks, driver, kernel)
    sums = exchange(message, RGROUP)
    for _ in range(ITERS - 2):
        (message,) = call(driver_next_body, [f32(DPEERS, DB, B)], [VM] * 4, columns)(
            sums, pots, state, kernel
        )
        sums = exchange(message, DGROUP)
        (message,) = call(rider_next_body, [f32(RPEERS, RB, B)], [VM] * 3, weights)(
            sums, state, kernel
        )
        sums = exchange(message, RGROUP)
    message, rider_pot = call(
        driver_last_body, [f32(DPEERS, 8, B), f32(2, B)], [VM] * 4, columns
    )(sums, pots, state, kernel)
    sums = exchange(message, DGROUP)
    (driver_pot,) = call(finish_body, [f32(1, B)], [VM] * 2)(sums, state)
    return rider_pot.reshape(2 * B), driver_pot.reshape(B)


def solution(mesh):
    fine = Mesh(mesh.devices.reshape(SIZES), AXES)
    row, every = ("z", "yl", "x"), AXES
    placed = (
        P(row, None),
        P(every, None),
        P(row),
        P(every),
        P(row),
        P(every),
        P(),
    )
    return jax.shard_map(
        per_device,
        mesh=fine,
        in_specs=placed,
        out_specs=(P(row), P(every)),
        check_vma=False,
    )
```

```python
import math

import jax
import jax.numpy as jnp
from jax import lax
from jax.experimental import pallas as pl
from jax.experimental.pallas import tpu as pltpu
from jax.sharding import Mesh, PartitionSpec as P

AXES = ("z", "yl", "x", "yh", "c")
SIZES = (8, 2, 4, 2, 2)
RGROUP = ("yl", "x", "yh", "c")
DGROUP = ("z",)
RPEERS = 32
DPEERS = 8

B = 128
RB = 16
DB = 8
PAY = B + 16
ITERS = 3
LOG_DRIVERS = math.log(32768)
LOG_RIDERS = math.log(16384)
PENALTY = 1e30
FLOOR = -1e29
TINY = 1e-37

F32 = jnp.float32
BF16 = jnp.bfloat16
VM = pl.BlockSpec(memory_space=pltpu.VMEM)
FAR = pl.BlockSpec(memory_space=pltpu.HBM)


def call(body, outs, ins, scratch=(), limit=40, to=VM):
    return pl.pallas_call(
        body,
        out_shape=outs,
        in_specs=ins,
        out_specs=[to] * len(outs),
        scratch_shapes=list(scratch),
        compiler_params=pltpu.CompilerParams(vmem_limit_bytes=limit * 2**20),
    )


def f32(*shape):
    return jax.ShapeDtypeStruct(shape, F32)


def bf16(*shape):
    return jax.ShapeDtypeStruct(shape, BF16)


def product(left, right):
    return lax.dot_general(left, right, (((1,), (1,)), ((), ())), preferred_element_type=F32)


def tree(parts, op):
    while len(parts) > 1:
        parts = [op(parts[2 * k], parts[2 * k + 1]) for k in range(len(parts) // 2)]
    return parts[0]


def fold(block, op):
    return tree([block[8 * k : 8 * k + 8] for k in range(B // 8)], op)


def column(row):
    return jnp.broadcast_to(row, (B, B)).T


def three_parts(value):
    high = value.astype(BF16)
    rest = value - high.astype(F32)
    middle = rest.astype(BF16)
    return high, middle, (rest - middle.astype(F32)).astype(BF16)


def zone_rows(message):
    return jnp.broadcast_to(message[B : B + 1].astype(F32), (16, B)).astype(BF16)


def weight_row(message):
    tail = message[B:].astype(F32)
    return (tail[1:2] + tail[2:3]) + tail[3:4]


def with_zone(message, zone):
    return jnp.concatenate([message[:B], jnp.concatenate([zone] * (B // 16), axis=0)], axis=1)


def tail_rows(zone_row, log_row):
    row = lax.broadcasted_iota(jnp.int32, (16, B), 0)
    tail = jnp.where(row == 0, zone_row, 0.0)
    for k, part in enumerate(three_parts(log_row)):
        tail = jnp.where(row == k + 1, part.astype(F32), tail)
    return tail.astype(BF16)


def pack_body(rider, driver, log_a, log_b, rzone, dzone, table, rider_out, driver_out,
              a_row, b_row, rz, dz, tab, message, sems):
    c = lax.axis_index("c")
    copies = [
        pltpu.make_async_copy(rider.at[c], message.at[0, pl.ds(0, B)], sems.at[0]),
        pltpu.make_async_copy(driver, message.at[1, pl.ds(0, B)], sems.at[1]),
        pltpu.make_async_copy(log_a.at[pl.ds(c, 1)], a_row, sems.at[2]),
        pltpu.make_async_copy(log_b, b_row, sems.at[3]),
        pltpu.make_async_copy(rzone, rz, sems.at[4]),
        pltpu.make_async_copy(dzone, dz, sems.at[5]),
        pltpu.make_async_copy(table, tab, sems.at[6]),
    ]
    for copy in copies:
        copy.start()
    for copy in copies:
        copy.wait()
    lane = lax.broadcasted_iota(jnp.int32, (16, B), 1)
    hot = jnp.where(lane == rz[c], 1.0, 0.0)
    zone = dz[0]
    shut = jnp.zeros((16, B), F32)
    for k in range(16):
        shut = jnp.where((lane == k) & (tab[k, zone] != 1), PENALTY, shut)
    message[0, B:, :] = tail_rows(hot, a_row[...])
    message[1, B:, :] = tail_rows(shut, b_row[...])
    copies = [pltpu.make_async_copy(message.at[0], rider_out.at[0], sems.at[7])]
    for k in range(8):
        copies.append(pltpu.make_async_copy(message.at[1], driver_out.at[k], sems.at[8 + k]))
    for copy in copies:
        copy.start()
    for copy in copies:
        copy.wait()


def place(far, slot):
    yl, x = lax.axis_index("yl"), lax.axis_index("x")
    first, second = slot % 2, slot // 2
    x = x + far * (3 - 2 * x)
    x = x + second * (1 - 2 * (x % 2))
    return (yl + first * (1 - 2 * yl)) * 4 + x


def rider_first_body(own_near, own_far, other_near, other_far, driver, out, dzone):
    c = lax.axis_index("c")
    for z in range(DB):
        dzone[z] = zone_rows(driver[z])

    def pair(slot, carry):
        for far, (own, other) in enumerate(((own_near, other_near), (own_far, other_far))):
            mine, theirs = own[slot], other[slot]
            right = jnp.concatenate(
                [with_zone(mine, zone_rows(mine)), with_zone(theirs, zone_rows(theirs))], axis=0
            )
            peak = jnp.full((8, 2 * B), -3e38, F32)
            mass = jnp.zeros((8, 2 * B), F32)
            for z in range(DB):
                cost = product(with_zone(driver[z], dzone[z]), right)
                fresh = jnp.maximum(peak, -fold(cost, jnp.minimum))
                terms = jnp.exp(-cost - jnp.concatenate([fresh] * 16, axis=0))
                mass = mass * jnp.exp(peak - fresh) + fold(terms, jnp.add)
                peak = fresh
            top = jnp.max(peak, axis=0, keepdims=True)
            mass = jnp.sum(mass * jnp.exp(peak - top), axis=0, keepdims=True)
            total = top + jnp.log(mass)
            p = place(far, slot)
            out[0, pl.ds(2 * p + c, 1), :] = total[:, :B]
            out[0, pl.ds(2 * p + 1 - c, 1), :] = total[:, B:]
        return carry

    lax.fori_loop(0, RB // 4, pair, 0)
    for k in range(1, RPEERS):
        out[k] = out[0]


def log_total(sums, peers):
    parts = [sums[k] for k in range(peers)]
    peak = tree(parts, jnp.maximum)
    return peak + jnp.log(tree([jnp.exp(part - peak) for part in parts], jnp.add))


def total_of(sums, peers):
    return tree([sums[k] for k in range(peers)], jnp.add)


def block_of(r):
    c = lax.axis_index("c")
    other = r % 2
    return 2 * place(r // 8, r // 2 % 4) + c + other * (1 - 2 * c)


def driver_first_body(sums, own_near, own_far, other_near, other_far, driver, out, kernel, peaks, pots, ucol):
    own = [own_near[k] for k in range(4)] + [own_far[k] for k in range(4)]
    other = [other_near[k] for k in range(4)] + [other_far[k] for k in range(4)]
    for r in range(RB):
        pots[pl.ds(RB + block_of(r), 1), :] = weight_row((other if r % 2 else own)[r // 2])
    pots[0:RB] = pots[RB:] - (log_total(sums, RPEERS) - LOG_DRIVERS)
    for r in range(RB):
        ucol[r * B : (r + 1) * B, :] = column(pots[pl.ds(block_of(r), 1), :])

    def pair(h, carry):
        one, two = driver[2 * h], driver[2 * h + 1]
        right = jnp.concatenate(
            [with_zone(one, zone_rows(one)), with_zone(two, zone_rows(two))], axis=0
        )
        lanes = pl.ds(pl.multiple_of(h * 2 * B, 2 * B), 2 * B)
        high = jnp.full((8, 2 * B), FLOOR, F32)
        for r in range(RB):
            u = ucol[r * B : (r + 1) * B, :]
            left = (other if r % 2 else own)[r // 2]
            score = jnp.concatenate([u, u], axis=1) - product(with_zone(left, zone_rows(left)), right)
            kernel[r * B : (r + 1) * B, lanes] = score
            high = jnp.maximum(high, fold(score, jnp.maximum))
        top = jnp.max(high, axis=0, keepdims=True)
        total = jnp.zeros((8, 2 * B), F32)
        for r in range(RB):
            term = jnp.exp(kernel[r * B : (r + 1) * B, lanes] - top)
            kernel[r * B : (r + 1) * B, lanes] = term
            total = total + fold(term, jnp.add)
        total = top + jnp.log(jnp.maximum(jnp.sum(total, axis=0, keepdims=True), TINY))
        for k in range(2):
            peaks[pl.ds(2 * h + k, 1), :] = top[:, k * B : (k + 1) * B]
            out[0, pl.ds(2 * h + k, 1), :] = total[:, k * B : (k + 1) * B]
        return carry

    lax.fori_loop(0, DB // 2, pair, 0)
    for k in range(1, DPEERS):
        out[k] = out[0]


def row_sums(kernel, weight, out):
    def block(r, carry):
        rows = pl.ds(pl.multiple_of(r * B, B), B)
        acc = kernel[rows, 0:B] * weight[0:1]
        for k in range(1, DB):
            acc = acc + kernel[rows, k * B : (k + 1) * B] * weight[k : k + 1]
        out[0, pl.ds(block_of(r), 1), :] = jnp.sum(acc.T, axis=0, keepdims=True)
        return carry

    lax.fori_loop(0, RB, block, 0)
    for k in range(1, RPEERS):
        out[k] = out[0]


def column_sums(kernel, fcol, state):
    def block(r, acc):
        for k in range(B // 8):
            rows = pl.ds(pl.multiple_of(r * B + 8 * k, 8), 8)
            f = fcol[rows, :]
            acc = tuple(a + kernel[rows, j * B : (j + 1) * B] * f for j, a in enumerate(acc))
        return acc

    acc = lax.fori_loop(0, RB, block, tuple(jnp.zeros((8, B), F32) for _ in range(DB)))
    rows = jnp.concatenate([jnp.sum(a, axis=0, keepdims=True) for a in acc], axis=0)
    return rows * state[2 * DB : 3 * DB]


def rider_second_body(sums, peaks, driver, kernel, out, state, weight):
    log_b = jnp.concatenate([weight_row(driver[k]) for k in range(DB)], axis=0)
    pot = log_b - (log_total(sums, DPEERS) - LOG_RIDERS)
    scale = jnp.exp(pot + peaks[...])
    state[0:DB] = pot
    state[DB : 2 * DB] = log_b
    state[2 * DB : 3 * DB] = scale
    weight[...] = scale
    row_sums(kernel, weight, out)


def spread_columns(f, fcol, hold):
    hold[...] = f
    for r in range(RB):
        fcol[r * B : (r + 1) * B, :] = column(hold[pl.ds(block_of(r), 1), :])


def driver_next_body(sums, pots, state, kernel, out, fcol, hold):
    f = jnp.exp(pots[RB:] + LOG_DRIVERS) / total_of(sums, RPEERS)
    spread_columns(f, fcol, hold)
    rows = column_sums(kernel, fcol, state)
    for k in range(DPEERS):
        out[k] = rows


def rider_next_body(sums, state, kernel, out, weight):
    g = jnp.exp(state[DB : 2 * DB] + LOG_RIDERS) / total_of(sums, DPEERS)
    weight[...] = state[2 * DB : 3 * DB] * g
    row_sums(kernel, weight, out)


def driver_last_body(sums, pots, state, kernel, out, rider_pot, fcol, hold):
    total = total_of(sums, RPEERS)
    log_a = pots[RB:]
    hold[...] = pots[0:RB] + (log_a + LOG_DRIVERS - jnp.log(total))
    block = lax.axis_index("yl") * 4 + lax.axis_index("x")
    rider_pot[0:1] = hold[pl.ds(2 * block, 1), :]
    rider_pot[1:2] = hold[pl.ds(2 * block + 1, 1), :]
    spread_columns(jnp.exp(log_a + LOG_DRIVERS) / total, fcol, hold)
    rows = column_sums(kernel, fcol, state)
    for k in range(DPEERS):
        out[k] = jnp.broadcast_to(rows[k : k + 1], (8, B))


def finish_body(sums, state, driver_pot):
    z = lax.axis_index("z")
    pot = state[pl.ds(z, 1), :]
    log_b = state[pl.ds(DB + z, 1), :]
    driver_pot[...] = pot + (log_b + LOG_RIDERS - jnp.log(total_of(sums, DPEERS)[0:1]))


def exchange(message, axes):
    return lax.all_to_all(message, axes, 0, 0, tiled=True)


def swap(value, axis, partner):
    return lax.ppermute(value, axis, [(k, partner(k)) for k in range(SIZES[AXES.index(axis)])])


def gather_riders(message):
    near = jnp.concatenate([message, swap(message, "yl", lambda k: 1 - k)], axis=0)
    near = jnp.concatenate([near, swap(near, "x", lambda k: k ^ 1)], axis=0)
    far = swap(near, "x", lambda k: 3 - k)
    return near, far, swap(near, "c", lambda k: 1 - k), swap(far, "c", lambda k: 1 - k)


def per_device(rider_emb, driver_emb, log_a, log_b, rider_zone, driver_zone, zone_table):
    rider_msg, driver_msg = call(
        pack_body,
        [bf16(1, PAY, B), bf16(8, PAY, B)],
        [FAR] * 7,
        [
            pltpu.VMEM((1, B), F32),
            pltpu.VMEM((1, B), F32),
            pltpu.SMEM((2,), jnp.int32),
            pltpu.SMEM((1,), jnp.int32),
            pltpu.SMEM((16, 16), jnp.int32),
            pltpu.VMEM((2, PAY, B), BF16),
            pltpu.SemaphoreType.DMA((16,)),
        ],
        limit=60,
        to=FAR,
    )(
        rider_emb.reshape(2, B, B), driver_emb, log_a.reshape(2, B), log_b.reshape(1, B),
        rider_zone, driver_zone, zone_table,
    )
    riders = gather_riders(rider_msg)
    driver = exchange(driver_msg, ("z",))
    (message,) = call(
        rider_first_body, [f32(RPEERS, RB, B)], [VM] * 5, [pltpu.VMEM((DB, 16, B), BF16)]
    )(*riders, driver)
    sums = exchange(message, RGROUP)
    columns = pltpu.VMEM((RB * B, B), F32)
    message, kernel, peaks, pots = call(
        driver_first_body,
        [f32(DPEERS, DB, B), f32(RB * B, DB * B), f32(DB, B), f32(2 * RB, B)],
        [VM] * 6,
        [columns],
    )(sums, *riders, driver)
    sums = exchange(message, DGROUP)
    weights = [pltpu.VMEM((DB, B), F32)]
    columns = [columns, pltpu.VMEM((RB, B), F32)]
    message, state = call(
        rider_second_body, [f32(RPEERS, RB, B), f32(3 * DB, B)], [VM] * 4, weights
    )(sums, peaks, driver, kernel)
    sums = exchange(message, RGROUP)
    for _ in range(ITERS - 2):
        (message,) = call(driver_next_body, [f32(DPEERS, DB, B)], [VM] * 4, columns)(
            sums, pots, state, kernel
        )
        sums = exchange(message, DGROUP)
        (message,) = call(rider_next_body, [f32(RPEERS, RB, B)], [VM] * 3, weights)(
            sums, state, kernel
        )
        sums = exchange(message, RGROUP)
    message, rider_pot = call(
        driver_last_body, [f32(DPEERS, 8, B), f32(2, B)], [VM] * 4, columns
    )(sums, pots, state, kernel)
    sums = exchange(message, DGROUP)
    (driver_pot,) = call(finish_body, [f32(1, B)], [VM] * 2)(sums, state)
    return rider_pot.reshape(2 * B), driver_pot.reshape(B)


def solution(mesh):
    fine = Mesh(mesh.devices.reshape(SIZES), AXES)
    row, every = ("z", "yl", "x"), AXES
    placed = (
        P(row, None),
        P(every, None),
        P(row),
        P(every),
        P(row),
        P(every),
        P(),
    )
    return jax.shard_map(
        per_device,
        mesh=fine,
        in_specs=placed,
        out_specs=(P(row), P(every)),
        check_vma=False,
    )
```

```python
import math

import jax
import jax.numpy as jnp
from jax import lax
from jax.experimental import pallas as pl
from jax.experimental.pallas import tpu as pltpu
from jax.sharding import Mesh, PartitionSpec as P

AXES = ("z", "yl", "x", "yh", "c")
SIZES = (8, 2, 4, 2, 2)
RGROUP = ("yl", "x", "yh", "c")
DGROUP = ("z",)
RPEERS = 32
DPEERS = 8

B = 128
RB = 16
DB = 8
PAY = B + 16
ITERS = 3
LOG_DRIVERS = math.log(32768)
LOG_RIDERS = math.log(16384)
PENALTY = 1e30
FLOOR = -1e29
TINY = 1e-37

F32 = jnp.float32
BF16 = jnp.bfloat16
VM = pl.BlockSpec(memory_space=pltpu.VMEM)
FAR = pl.BlockSpec(memory_space=pltpu.HBM)


def call(body, outs, ins, scratch=(), limit=40, to=None, cost=None):
    return pl.pallas_call(
        body,
        out_shape=outs,
        in_specs=ins,
        out_specs=to or [VM] * len(outs),
        cost_estimate=cost,
        scratch_shapes=list(scratch),
        compiler_params=pltpu.CompilerParams(vmem_limit_bytes=limit * 2**20),
    )


def f32(*shape):
    return jax.ShapeDtypeStruct(shape, F32)


def bf16(*shape):
    return jax.ShapeDtypeStruct(shape, BF16)


def product(left, right):
    return lax.dot_general(left, right, (((1,), (1,)), ((), ())), preferred_element_type=F32)


def tree(parts, op):
    while len(parts) > 1:
        parts = [op(parts[2 * k], parts[2 * k + 1]) for k in range(len(parts) // 2)]
    return parts[0]


def fold(block, op):
    return tree([block[8 * k : 8 * k + 8] for k in range(B // 8)], op)


def column(row):
    return jnp.broadcast_to(row, (B, B)).T


def three_parts(value):
    high = value.astype(BF16)
    rest = value - high.astype(F32)
    middle = rest.astype(BF16)
    return high, middle, (rest - middle.astype(F32)).astype(BF16)


def zone_rows(message):
    return jnp.broadcast_to(message[B : B + 1].astype(F32), (16, B)).astype(BF16)


def weight_row(message):
    tail = message[B:].astype(F32)
    return (tail[1:2] + tail[2:3]) + tail[3:4]


def with_zone(message, zone):
    return jnp.concatenate([message[:B], jnp.concatenate([zone] * (B // 16), axis=0)], axis=1)


def tail_rows(zone_row, log_row):
    row = lax.broadcasted_iota(jnp.int32, (16, B), 0)
    tail = jnp.where(row == 0, zone_row, 0.0)
    for k, part in enumerate(three_parts(log_row)):
        tail = jnp.where(row == k + 1, part.astype(F32), tail)
    return tail.astype(BF16)


def pack_body(rider, driver, log_a, log_b, rzone, dzone, table, rider_out, driver_out,
              a_row, b_row, rz, dz, tab, message, sems):
    c = lax.axis_index("c")
    copies = [
        pltpu.make_async_copy(rider.at[c], rider_out.at[0, pl.ds(0, B)], sems.at[0]),
        pltpu.make_async_copy(driver, message.at[pl.ds(0, B)], sems.at[1]),
        pltpu.make_async_copy(log_a.at[pl.ds(c, 1)], a_row, sems.at[2]),
        pltpu.make_async_copy(log_b, b_row, sems.at[3]),
        pltpu.make_async_copy(rzone, rz, sems.at[4]),
        pltpu.make_async_copy(dzone, dz, sems.at[5]),
        pltpu.make_async_copy(table, tab, sems.at[6]),
    ]
    for copy in copies:
        copy.start()
    for copy in copies:
        copy.wait()
    lane = lax.broadcasted_iota(jnp.int32, (16, B), 1)
    hot = jnp.where(lane == rz[c], 1.0, 0.0)
    zone = dz[0]
    shut = jnp.zeros((16, B), F32)
    for k in range(16):
        shut = jnp.where((lane == k) & (tab[k, zone] != 1), PENALTY, shut)
    rider_out[0, B:, :] = tail_rows(hot, a_row[...])
    message[B:, :] = tail_rows(shut, b_row[...])
    copies = [pltpu.make_async_copy(message, driver_out.at[k], sems.at[7 + k]) for k in range(8)]
    for copy in copies:
        copy.start()
    for copy in copies:
        copy.wait()


def place(far, slot):
    yl, x = lax.axis_index("yl"), lax.axis_index("x")
    first, second = slot % 2, slot // 2
    x = x + far * (3 - 2 * x)
    x = x + second * (1 - 2 * (x % 2))
    return (yl + first * (1 - 2 * yl)) * 4 + x


def block_of(r):
    c = lax.axis_index("c")
    other = r % 2
    return 2 * place(r // 8, r // 2 % 4) + c + other * (1 - 2 * c)


def rider_part(own, other, driver, rows, left):
    for z in range(DB):
        left[z * B : (z + 1) * B] = with_zone(driver[z], zone_rows(driver[z]))

    def pair(slot, carry):
        mine, theirs = own[slot], other[slot]
        right = jnp.concatenate(
            [with_zone(mine, zone_rows(mine)), with_zone(theirs, zone_rows(theirs))], axis=0
        )
        cost = product(left[...], right)
        pieces = [cost[z * B : (z + 1) * B] for z in range(DB)]
        low = tree([fold(piece, jnp.minimum) for piece in pieces], jnp.minimum)
        low = jnp.min(low, axis=0, keepdims=True)
        mass = tree([fold(jnp.exp(low - piece), jnp.add) for piece in pieces], jnp.add)
        total = jnp.log(jnp.sum(mass, axis=0, keepdims=True)) - low
        rows[pl.ds(2 * slot, 1), :] = total[:, :B]
        rows[pl.ds(2 * slot + 1, 1), :] = total[:, B:]
        return carry

    lax.fori_loop(0, 4, pair, 0)


def rider_near_body(own, other, driver, rows, left):
    rider_part(own, other, driver, rows, left)


def rider_far_body(own, other, driver, near, out, rows, left):
    rider_part(own, other, driver, rows, left)
    for r in range(RB):
        out[0, pl.ds(block_of(r), 1), :] = (rows if r >= 8 else near)[r % 8 : r % 8 + 1]
    for k in range(1, RPEERS):
        out[k] = out[0]


def log_total(sums, peers):
    parts = [sums[k] for k in range(peers)]
    peak = tree(parts, jnp.maximum)
    return peak + jnp.log(tree([jnp.exp(part - peak) for part in parts], jnp.add))


def total_of(sums, peers):
    return tree([sums[k] for k in range(peers)], jnp.add)


def driver_first_body(sums, own_near, own_far, other_near, other_far, driver, out, kernel, peaks, pots, ucol, left):
    riders = ((own_near, other_near), (own_far, other_far))
    for r in range(RB):
        message = riders[r // 8][r % 2][r // 2 % 4]
        left[r * B : (r + 1) * B] = with_zone(message, zone_rows(message))
        pots[pl.ds(RB + block_of(r), 1), :] = weight_row(message)
    pots[0:RB] = pots[RB:] - (log_total(sums, RPEERS) - LOG_DRIVERS)
    for r in range(RB):
        ucol[r * B : (r + 1) * B, :] = column(pots[pl.ds(block_of(r), 1), :])

    def pair(h, carry):
        one, two = driver[2 * h], driver[2 * h + 1]
        right = jnp.concatenate(
            [with_zone(one, zone_rows(one)), with_zone(two, zone_rows(two))], axis=0
        )
        lanes = pl.ds(pl.multiple_of(h * 2 * B, 2 * B), 2 * B)
        cost = product(left[...], right)
        high = jnp.full((8, 2 * B), FLOOR, F32)
        for r in range(RB):
            u = ucol[r * B : (r + 1) * B, :]
            score = jnp.concatenate([u, u], axis=1) - cost[r * B : (r + 1) * B]
            kernel[r * B : (r + 1) * B, lanes] = score
            high = jnp.maximum(high, fold(score, jnp.maximum))
        top = jnp.max(high, axis=0, keepdims=True)
        total = jnp.zeros((8, 2 * B), F32)
        for r in range(RB):
            term = jnp.exp(kernel[r * B : (r + 1) * B, lanes] - top)
            kernel[r * B : (r + 1) * B, lanes] = term
            total = total + fold(term, jnp.add)
        total = top + jnp.log(jnp.maximum(jnp.sum(total, axis=0, keepdims=True), TINY))
        for k in range(2):
            peaks[pl.ds(2 * h + k, 1), :] = top[:, k * B : (k + 1) * B]
            out[0, pl.ds(2 * h + k, 1), :] = total[:, k * B : (k + 1) * B]
        return carry

    lax.fori_loop(0, DB // 2, pair, 0)
    for k in range(1, DPEERS):
        out[k] = out[0]


def row_sums(kernel, weight, out):
    for r in range(RB):
        rows = slice(r * B, (r + 1) * B)
        acc = kernel[rows, 0:B] * weight[0:1]
        for k in range(1, DB):
            acc = acc + kernel[rows, k * B : (k + 1) * B] * weight[k : k + 1]
        out[0, pl.ds(block_of(r), 1), :] = jnp.sum(acc.T, axis=0, keepdims=True)
    for k in range(1, RPEERS):
        out[k] = out[0]


def column_sums(kernel, fcol, state):
    def block(r, acc):
        for k in range(B // 8):
            rows = pl.ds(pl.multiple_of(r * B + 8 * k, 8), 8)
            f = fcol[rows, :]
            acc = tuple(a + kernel[rows, j * B : (j + 1) * B] * f for j, a in enumerate(acc))
        return acc

    acc = lax.fori_loop(0, RB, block, tuple(jnp.zeros((8, B), F32) for _ in range(DB)))
    rows = jnp.concatenate([jnp.sum(a, axis=0, keepdims=True) for a in acc], axis=0)
    return rows * state[2 * DB : 3 * DB]


def rider_second_body(sums, peaks, driver, kernel, out, state, weight):
    log_b = jnp.concatenate([weight_row(driver[k]) for k in range(DB)], axis=0)
    pot = log_b - (log_total(sums, DPEERS) - LOG_RIDERS)
    scale = jnp.exp(pot + peaks[...])
    state[0:DB] = pot
    state[DB : 2 * DB] = log_b
    state[2 * DB : 3 * DB] = scale
    weight[...] = scale
    row_sums(kernel, weight, out)


def spread_columns(f, fcol, hold):
    hold[...] = f
    for r in range(RB):
        fcol[r * B : (r + 1) * B, :] = column(hold[pl.ds(block_of(r), 1), :])


def driver_next_body(sums, pots, state, kernel, out, fcol, hold):
    f = jnp.exp(pots[RB:] + LOG_DRIVERS) / total_of(sums, RPEERS)
    spread_columns(f, fcol, hold)
    rows = column_sums(kernel, fcol, state)
    for k in range(DPEERS):
        out[k] = rows


def rider_next_body(sums, state, kernel, out, weight):
    g = jnp.exp(state[DB : 2 * DB] + LOG_RIDERS) / total_of(sums, DPEERS)
    weight[...] = state[2 * DB : 3 * DB] * g
    row_sums(kernel, weight, out)


def driver_last_body(sums, pots, state, kernel, out, rider_pot, fcol, hold):
    total = total_of(sums, RPEERS)
    log_a = pots[RB:]
    hold[...] = pots[0:RB] + (log_a + LOG_DRIVERS - jnp.log(total))
    block = lax.axis_index("yl") * 4 + lax.axis_index("x")
    rider_pot[0:1] = hold[pl.ds(2 * block, 1), :]
    rider_pot[1:2] = hold[pl.ds(2 * block + 1, 1), :]
    spread_columns(jnp.exp(log_a + LOG_DRIVERS) / total, fcol, hold)
    rows = column_sums(kernel, fcol, state)
    for k in range(DPEERS):
        out[k] = jnp.broadcast_to(rows[k : k + 1], (8, B))


def finish_body(sums, state, driver_pot):
    z = lax.axis_index("z")
    pot = state[pl.ds(z, 1), :]
    log_b = state[pl.ds(DB + z, 1), :]
    driver_pot[...] = pot + (log_b + LOG_RIDERS - jnp.log(total_of(sums, DPEERS)[0:1]))


def exchange(message, axes):
    return lax.all_to_all(message, axes, 0, 0, tiled=True)


def swap(value, axis, partner):
    return lax.ppermute(value, axis, [(k, partner(k)) for k in range(SIZES[AXES.index(axis)])])


def gather(message, drivers):
    near = jnp.concatenate([message, swap(message, "yl", lambda k: 1 - k)], axis=0)
    near, drivers = lax.optimization_barrier((near, drivers))
    drivers = exchange(drivers, ("z",))
    near = jnp.concatenate([near, swap(near, "x", lambda k: k ^ 1)], axis=0)
    far = swap(near, "x", lambda k: 3 - k)
    return near, far, swap(near, "c", lambda k: 1 - k), swap(far, "c", lambda k: 1 - k), drivers


def matmul_cost(riders, drivers):
    return pl.CostEstimate(flops=2 * riders * drivers * 2 * B, transcendentals=riders * drivers,
                           bytes_accessed=4 * riders * drivers)


def per_device(rider_emb, driver_emb, log_a, log_b, rider_zone, driver_zone, zone_table):
    rider_msg, driver_msg = call(
        pack_body,
        [pltpu.VMEM((1, PAY, B), BF16), bf16(8, PAY, B)],
        [FAR] * 7,
        [
            pltpu.VMEM((1, B), F32),
            pltpu.VMEM((1, B), F32),
            pltpu.SMEM((2,), jnp.int32),
            pltpu.SMEM((1,), jnp.int32),
            pltpu.SMEM((16, 16), jnp.int32),
            pltpu.VMEM((PAY, B), BF16),
            pltpu.SemaphoreType.DMA((15,)),
        ],
        limit=60,
        to=[VM, FAR],
    )(
        rider_emb.reshape(2, B, B), driver_emb, log_a.reshape(2, B), log_b.reshape(1, B),
        rider_zone, driver_zone, zone_table,
    )
    own_near, own_far, other_near, other_far, driver = gather(rider_msg, driver_msg)
    riders = own_near, own_far, other_near, other_far
    half = matmul_cost(RB * B // 2, DB * B)
    left = pltpu.VMEM((DB * B, 2 * B), BF16)
    (near_rows,) = call(rider_near_body, [f32(8, B)], [VM] * 3, [left], cost=half)(
        own_near, other_near, driver
    )
    (message,) = call(
        rider_far_body, [f32(RPEERS, RB, B)], [VM] * 4, [pltpu.VMEM((8, B), F32), left], cost=half
    )(own_far, other_far, driver, near_rows)
    sums = exchange(message, RGROUP)
    columns = pltpu.VMEM((RB * B, B), F32)
    message, kernel, peaks, pots = call(
        driver_first_body,
        [f32(DPEERS, DB, B), f32(RB * B, DB * B), f32(DB, B), f32(2 * RB, B)],
        [VM] * 6,
        [columns, pltpu.VMEM((RB * B, 2 * B), BF16)],
    )(sums, *riders, driver)
    sums = exchange(message, DGROUP)
    weights = [pltpu.VMEM((DB, B), F32)]
    columns = [columns, pltpu.VMEM((RB, B), F32)]
    message, state = call(
        rider_second_body, [f32(RPEERS, RB, B), f32(3 * DB, B)], [VM] * 4, weights
    )(sums, peaks, driver, kernel)
    sums = exchange(message, RGROUP)
    for _ in range(ITERS - 2):
        (message,) = call(driver_next_body, [f32(DPEERS, DB, B)], [VM] * 4, columns)(
            sums, pots, state, kernel
        )
        sums = exchange(message, DGROUP)
        (message,) = call(rider_next_body, [f32(RPEERS, RB, B)], [VM] * 3, weights)(
            sums, state, kernel
        )
        sums = exchange(message, RGROUP)
    message, rider_pot = call(
        driver_last_body, [f32(DPEERS, 8, B), f32(2, B)], [VM] * 4, columns
    )(sums, pots, state, kernel)
    sums = exchange(message, DGROUP)
    (driver_pot,) = call(finish_body, [f32(1, B)], [VM] * 2)(sums, state)
    return rider_pot.reshape(2 * B), driver_pot.reshape(B)


def solution(mesh):
    fine = Mesh(mesh.devices.reshape(SIZES), AXES)
    row, every = ("z", "yl", "x"), AXES
    placed = (
        P(row, None),
        P(every, None),
        P(row),
        P(every),
        P(row),
        P(every),
        P(),
    )
    return jax.shard_map(
        per_device,
        mesh=fine,
        in_specs=placed,
        out_specs=(P(row), P(every)),
        check_vma=False,
    )
```

```python
import math

import jax
import jax.numpy as jnp
from jax import lax
from jax.experimental import pallas as pl
from jax.experimental.pallas import tpu as pltpu
from jax.sharding import Mesh, PartitionSpec as P

AXES = ("z", "yl", "x", "yh", "c")
SIZES = (8, 2, 4, 2, 2)

B = 128
RB = 16
DB = 8
PAY = B + 16
ITERS = 3
LOG_DRIVERS = math.log(32768)
LOG_RIDERS = math.log(16384)
PENALTY = 1e30
FLOOR = -1e29
TINY = 1e-37

F32 = jnp.float32
BF16 = jnp.bfloat16
VM = pl.BlockSpec(memory_space=pltpu.VMEM)
FAR = pl.BlockSpec(memory_space=pltpu.HBM)


def call(body, outs, ins, scratch=(), limit=40, cost=None):
    return pl.pallas_call(
        body,
        out_shape=outs,
        in_specs=ins,
        out_specs=[VM] * len(outs),
        cost_estimate=cost,
        scratch_shapes=list(scratch),
        compiler_params=pltpu.CompilerParams(vmem_limit_bytes=limit * 2**20),
    )


def f32(*shape):
    return jax.ShapeDtypeStruct(shape, F32)


def bf16(*shape):
    return jax.ShapeDtypeStruct(shape, BF16)


def product(left, right):
    return lax.dot_general(left, right, (((1,), (1,)), ((), ())), preferred_element_type=F32)


def tree(parts, op):
    while len(parts) > 1:
        parts = [op(parts[2 * k], parts[2 * k + 1]) for k in range(len(parts) // 2)]
    return parts[0]


def fold(block, op):
    return tree([block[8 * k : 8 * k + 8] for k in range(B // 8)], op)


def column(row):
    return jnp.broadcast_to(row, (B, B)).T


def three_parts(value):
    high = value.astype(BF16)
    rest = value - high.astype(F32)
    middle = rest.astype(BF16)
    return high, middle, (rest - middle.astype(F32)).astype(BF16)


def zone_rows(message):
    return jnp.broadcast_to(message[B : B + 1].astype(F32), (16, B)).astype(BF16)


def weight_row(message):
    tail = message[B:].astype(F32)
    return (tail[1:2] + tail[2:3]) + tail[3:4]


def with_zone(message, zone):
    return jnp.concatenate([message[:B], jnp.concatenate([zone] * (B // 16), axis=0)], axis=1)


def tail_rows(zone_row, log_row):
    row = lax.broadcasted_iota(jnp.int32, (16, B), 0)
    tail = jnp.where(row == 0, zone_row, 0.0)
    for k, part in enumerate(three_parts(log_row)):
        tail = jnp.where(row == k + 1, part.astype(F32), tail)
    return tail.astype(BF16)


def pack_body(rider, driver, log_a, log_b, rzone, dzone, table, rider_out, driver_out,
              a_row, b_row, rz, dz, tab, sems):
    c = lax.axis_index("c")
    copies = [
        pltpu.make_async_copy(rider.at[c], rider_out.at[0, pl.ds(0, B)], sems.at[0]),
        pltpu.make_async_copy(driver, driver_out.at[0, pl.ds(0, B)], sems.at[1]),
        pltpu.make_async_copy(log_a.at[pl.ds(c, 1)], a_row, sems.at[2]),
        pltpu.make_async_copy(log_b, b_row, sems.at[3]),
        pltpu.make_async_copy(rzone, rz, sems.at[4]),
        pltpu.make_async_copy(dzone, dz, sems.at[5]),
        pltpu.make_async_copy(table, tab, sems.at[6]),
    ]
    for copy in copies:
        copy.start()
    for copy in copies:
        copy.wait()
    lane = lax.broadcasted_iota(jnp.int32, (16, B), 1)
    hot = jnp.where(lane == rz[c], 1.0, 0.0)
    zone = dz[0]
    shut = jnp.zeros((16, B), F32)
    for k in range(16):
        shut = jnp.where((lane == k) & (tab[k, zone] != 1), PENALTY, shut)
    rider_out[0, B:, :] = tail_rows(hot, a_row[...])
    driver_out[0, B:, :] = tail_rows(shut, b_row[...])


def place(far, slot):
    yl, x = lax.axis_index("yl"), lax.axis_index("x")
    first, second = slot % 2, slot // 2
    x = x + far * (3 - 2 * x)
    x = x + second * (1 - 2 * (x % 2))
    return (yl + first * (1 - 2 * yl)) * 4 + x


def block_of(r):
    c = lax.axis_index("c")
    other = r % 2
    return 2 * place(r // 8, r // 2 % 4) + c + other * (1 - 2 * c)


def ring(j):
    return (lax.axis_index("z") + j) % DB


def widen(messages, wide):
    for k, message in enumerate(messages):
        wide[k * B : (k + 1) * B] = with_zone(message, zone_rows(message))


def rider_part(own, other, drivers, rows, left):
    widen([driver[0] for driver in drivers], left)

    def pair(slot, carry):
        mine, theirs = own[slot], other[slot]
        right = jnp.concatenate(
            [with_zone(mine, zone_rows(mine)), with_zone(theirs, zone_rows(theirs))], axis=0
        )
        cost = product(left[...], right)
        pieces = [cost[z * B : (z + 1) * B] for z in range(DB)]
        low = tree([fold(piece, jnp.minimum) for piece in pieces], jnp.minimum)
        low = jnp.min(low, axis=0, keepdims=True)
        mass = tree([fold(jnp.exp(low - piece), jnp.add) for piece in pieces], jnp.add)
        total = jnp.log(jnp.sum(mass, axis=0, keepdims=True)) - low
        rows[pl.ds(2 * slot, 1), :] = total[:, :B]
        rows[pl.ds(2 * slot + 1, 1), :] = total[:, B:]
        return carry

    lax.fori_loop(0, 4, pair, 0)


def rider_near_body(own, other, *rest):
    *drivers, rows, left = rest
    rider_part(own, other, drivers, rows, left)


def rider_far_body(own, other, near, *rest):
    *drivers, out, rows, left = rest
    rider_part(own, other, drivers, rows, left)
    for r in range(RB):
        out[pl.ds(block_of(r), 1), :] = (rows if r >= 8 else near)[r % 8 : r % 8 + 1]


def log_total(sums):
    parts = [sums[k] for k in range(DB)]
    peak = tree(parts, jnp.maximum)
    return peak + jnp.log(tree([jnp.exp(part - peak) for part in parts], jnp.add))


def total_of(sums):
    return tree([sums[k] for k in range(DB)], jnp.add)


def driver_first_body(sums, own_near, own_far, other_near, other_far, *rest):
    *drivers, out, kernel, peaks, pots, ucol, left, right = rest
    riders = ((own_near, other_near), (own_far, other_far))
    messages = [riders[r // 8][r % 2][r // 2 % 4] for r in range(RB)]
    widen(messages, left)
    widen([driver[0] for driver in drivers], right)
    for r in range(RB):
        pots[pl.ds(RB + block_of(r), 1), :] = weight_row(messages[r])
    for j in range(DB):
        peaks[pl.ds(DB + ring(j), 1), :] = weight_row(drivers[j][0])
    pots[0:RB] = pots[RB:] - (sums[...] - LOG_DRIVERS)
    for r in range(RB):
        ucol[r * B : (r + 1) * B, :] = column(pots[pl.ds(block_of(r), 1), :])

    def pair(h, carry):
        lanes = pl.ds(pl.multiple_of(h * 2 * B, 2 * B), 2 * B)
        cost = product(left[...], right[lanes, :])
        high = jnp.full((8, 2 * B), FLOOR, F32)
        for r in range(RB):
            u = ucol[r * B : (r + 1) * B, :]
            score = jnp.concatenate([u, u], axis=1) - cost[r * B : (r + 1) * B]
            kernel[r * B : (r + 1) * B, lanes] = score
            high = jnp.maximum(high, fold(score, jnp.maximum))
        top = jnp.max(high, axis=0, keepdims=True)
        total = jnp.zeros((8, 2 * B), F32)
        for r in range(RB):
            term = jnp.exp(kernel[r * B : (r + 1) * B, lanes] - top)
            kernel[r * B : (r + 1) * B, lanes] = term
            total = total + fold(term, jnp.add)
        total = top + jnp.log(jnp.maximum(jnp.sum(total, axis=0, keepdims=True), TINY))
        for k in range(2):
            peaks[pl.ds(ring(2 * h + k), 1), :] = top[:, k * B : (k + 1) * B]
            out[0, pl.ds(ring(2 * h + k), 1), :] = total[:, k * B : (k + 1) * B]
        return carry

    lax.fori_loop(0, DB // 2, pair, 0)
    for k in range(1, DB):
        out[k] = out[0]


def row_sums(kernel, scale, out):
    weight = [scale[pl.ds(ring(j), 1), :] for j in range(DB)]
    for r in range(RB):
        rows = slice(r * B, (r + 1) * B)
        acc = kernel[rows, 0:B] * weight[0]
        for k in range(1, DB):
            acc = acc + kernel[rows, k * B : (k + 1) * B] * weight[k]
        out[pl.ds(block_of(r), 1), :] = jnp.sum(acc.T, axis=0, keepdims=True)


def column_sums(kernel, f, state, fcol, hold):
    hold[...] = f
    for r in range(RB):
        fcol[r * B : (r + 1) * B, :] = column(hold[pl.ds(block_of(r), 1), :])

    def block(r, acc):
        for k in range(B // 8):
            rows = pl.ds(pl.multiple_of(r * B + 8 * k, 8), 8)
            f = fcol[rows, :]
            acc = tuple(a + kernel[rows, j * B : (j + 1) * B] * f for j, a in enumerate(acc))
        return acc

    acc = lax.fori_loop(0, RB, block, tuple(jnp.zeros((8, B), F32) for _ in range(DB)))
    for j in range(DB):
        hold[pl.ds(ring(j), 1), :] = jnp.sum(acc[j], axis=0, keepdims=True)
    return hold[0:DB] * state[2 * DB : 3 * DB]


def rider_second_body(sums, peaks, kernel, out, state):
    log_b = peaks[DB:]
    pot = log_b - (log_total(sums) - LOG_RIDERS)
    state[0:DB] = pot
    state[DB : 2 * DB] = log_b
    state[2 * DB :] = jnp.exp(pot + peaks[0:DB])
    row_sums(kernel, state.at[pl.ds(2 * DB, DB)], out)


def driver_next_body(sums, pots, state, kernel, out, fcol, hold):
    rows = column_sums(kernel, jnp.exp(pots[RB:] + LOG_DRIVERS) / sums[...], state, fcol, hold)
    for k in range(DB):
        out[k] = rows


def rider_next_body(sums, state, kernel, out, scale):
    scale[...] = state[2 * DB :] * (jnp.exp(state[DB : 2 * DB] + LOG_RIDERS) / total_of(sums))
    row_sums(kernel, scale, out)


def driver_last_body(sums, pots, state, kernel, out, rider_pot, fcol, hold):
    log_a = pots[RB:]
    hold[...] = pots[0:RB] + (log_a + LOG_DRIVERS - jnp.log(sums[...]))
    block = lax.axis_index("yl") * 4 + lax.axis_index("x")
    rider_pot[0:1] = hold[pl.ds(2 * block, 1), :]
    rider_pot[1:2] = hold[pl.ds(2 * block + 1, 1), :]
    rows = column_sums(kernel, jnp.exp(log_a + LOG_DRIVERS) / sums[...], state, fcol, hold)
    for k in range(DB):
        out[k] = jnp.broadcast_to(rows[k : k + 1], (8, B))


def finish_body(sums, state, driver_pot):
    z = lax.axis_index("z")
    pot = state[pl.ds(z, 1), :]
    log_b = state[pl.ds(DB + z, 1), :]
    driver_pot[...] = pot + (log_b + LOG_RIDERS - jnp.log(total_of(sums)[0:1]))


def exchange(message):
    return lax.all_to_all(message, "z", 0, 0, tiled=True)


def swap(value, axes, partner):
    count = math.prod(SIZES[AXES.index(axis)] for axis in axes)
    return lax.ppermute(value, axes, [(k, partner(k)) for k in range(count)])


def gather(rider, driver):
    held = {0: driver, DB: driver}
    near, far, other = rider, None, None
    for k in range(1, DB // 2 + 1):
        held[k] = swap(held[k - 1], ("z",), lambda i: (i - 1) % DB)
        if k < DB // 2:
            held[DB - k] = swap(held[DB - k + 1], ("z",), lambda i: (i + 1) % DB)
        if k == 1:
            near = jnp.concatenate([near, swap(near, ("yl",), lambda i: 1 - i)], axis=0)
        elif k == 2:
            near = jnp.concatenate([near, swap(near, ("x",), lambda i: i ^ 1)], axis=0)
        elif k == 3:
            far = swap(near, ("x",), lambda i: 3 - i)
            other = swap(near, ("c",), lambda i: 1 - i)
        if k < 3:
            near, held[k], held[DB - k] = lax.optimization_barrier((near, held[k], held[DB - k]))
        elif k == 3:
            far, held[k], held[DB - k] = lax.optimization_barrier((far, held[k], held[DB - k]))
    return (near, far, other, swap(far, ("c",), lambda i: 1 - i)), [held[k] for k in range(DB)]


def log_add(a, b):
    peak = jnp.maximum(a, b)
    return peak + jnp.log(jnp.exp(a - peak) + jnp.exp(b - peak))


def close(value, op):
    for axes, partner in (
        (("c",), lambda k: 1 - k),
        (("x",), lambda k: k ^ 1),
        (("x",), lambda k: 3 - k),
        (("yl",), lambda k: 1 - k),
        (("yl", "yh"), lambda k: 3 - k),
    ):
        value = op(value, swap(value, axes, partner))
    return value


def matmul_cost(riders, drivers):
    return pl.CostEstimate(flops=2 * riders * drivers * 2 * B, transcendentals=riders * drivers,
                           bytes_accessed=4 * riders * drivers)


def per_device(rider_emb, driver_emb, log_a, log_b, rider_zone, driver_zone, zone_table):
    message = pltpu.VMEM((1, PAY, B), BF16)
    rider_msg, driver_msg = call(
        pack_body,
        [message, message],
        [FAR] * 7,
        [
            pltpu.VMEM((1, B), F32),
            pltpu.VMEM((1, B), F32),
            pltpu.SMEM((2,), jnp.int32),
            pltpu.SMEM((1,), jnp.int32),
            pltpu.SMEM((16, 16), jnp.int32),
            pltpu.SemaphoreType.DMA((7,)),
        ],
        limit=60,
    )(
        rider_emb.reshape(2, B, B), driver_emb, log_a.reshape(2, B), log_b.reshape(1, B),
        rider_zone, driver_zone, zone_table,
    )
    riders, drivers = gather(rider_msg, driver_msg)
    own_near, own_far, other_near, other_far = riders
    half = matmul_cost(RB * B // 2, DB * B)
    left = pltpu.VMEM((DB * B, 2 * B), BF16)
    (near,) = call(rider_near_body, [f32(8, B)], [VM] * 10, [left], cost=half)(
        own_near, other_near, *drivers
    )
    (sums,) = call(
        rider_far_body, [f32(RB, B)], [VM] * 11, [pltpu.VMEM((8, B), F32), left], cost=half
    )(own_far, other_far, near, *drivers)
    sums = close(sums, log_add)
    columns = pltpu.VMEM((RB * B, B), F32)
    sums, kernel, peaks, pots = call(
        driver_first_body,
        [f32(DB, DB, B), f32(RB * B, DB * B), f32(2 * DB, B), f32(2 * RB, B)],
        [VM] * 13,
        [columns, pltpu.VMEM((RB * B, 2 * B), BF16), left],
    )(sums, *riders, *drivers)
    sums = exchange(sums)
    columns = [columns, pltpu.VMEM((RB, B), F32)]
    sums, state = call(rider_second_body, [f32(RB, B), f32(3 * DB, B)], [VM] * 3)(
        sums, peaks, kernel
    )
    sums = close(sums, jnp.add)
    for _ in range(ITERS - 2):
        (sums,) = call(driver_next_body, [f32(DB, DB, B)], [VM] * 4, columns)(
            sums, pots, state, kernel
        )
        sums = exchange(sums)
        (sums,) = call(rider_next_body, [f32(RB, B)], [VM] * 3, [pltpu.VMEM((DB, B), F32)])(
            sums, state, kernel
        )
        sums = close(sums, jnp.add)
    sums, rider_pot = call(driver_last_body, [f32(DB, 8, B), f32(2, B)], [VM] * 4, columns)(
        sums, pots, state, kernel
    )
    sums = exchange(sums)
    (driver_pot,) = call(finish_body, [f32(1, B)], [VM] * 2)(sums, state)
    return rider_pot.reshape(2 * B), driver_pot.reshape(B)


def solution(mesh):
    fine = Mesh(mesh.devices.reshape(SIZES), AXES)
    row, every = ("z", "yl", "x"), AXES
    placed = (
        P(row, None),
        P(every, None),
        P(row),
        P(every),
        P(row),
        P(every),
        P(),
    )
    return jax.shard_map(
        per_device,
        mesh=fine,
        in_specs=placed,
        out_specs=(P(row), P(every)),
        check_vma=False,
    )
```

```python
import math

import jax
import jax.numpy as jnp
from jax import lax
from jax.experimental import pallas as pl
from jax.experimental.pallas import tpu as pltpu
from jax.sharding import Mesh, PartitionSpec as P

AXES = ("z", "yl", "x", "yh", "c")
SIZES = (8, 2, 4, 2, 2)
PLANE = ("yl", "x", "yh")
PEERS = 16

B = 128
RB = 16
DB = 8
PAY = B + 16
ITERS = 3
LOG_DRIVERS = math.log(32768)
LOG_RIDERS = math.log(16384)
PENALTY = 1e30
FLOOR = -1e29
TINY = 1e-37

F32 = jnp.float32
BF16 = jnp.bfloat16
VM = pl.BlockSpec(memory_space=pltpu.VMEM)
FAR = pl.BlockSpec(memory_space=pltpu.HBM)


def call(body, outs, ins, scratch=(), limit=40, cost=None):
    return pl.pallas_call(
        body,
        out_shape=outs,
        in_specs=ins,
        out_specs=[VM] * len(outs),
        cost_estimate=cost,
        scratch_shapes=list(scratch),
        compiler_params=pltpu.CompilerParams(vmem_limit_bytes=limit * 2**20),
    )


def f32(*shape):
    return jax.ShapeDtypeStruct(shape, F32)


def bf16(*shape):
    return jax.ShapeDtypeStruct(shape, BF16)


def product(left, right):
    return lax.dot_general(left, right, (((1,), (1,)), ((), ())), preferred_element_type=F32)


def tree(parts, op):
    while len(parts) > 1:
        parts = [op(parts[2 * k], parts[2 * k + 1]) for k in range(len(parts) // 2)]
    return parts[0]


def fold(block, op):
    return tree([block[8 * k : 8 * k + 8] for k in range(B // 8)], op)


def column(row):
    return jnp.broadcast_to(row, (B, B)).T


def three_parts(value):
    high = value.astype(BF16)
    rest = value - high.astype(F32)
    middle = rest.astype(BF16)
    return high, middle, (rest - middle.astype(F32)).astype(BF16)


def zone_rows(message):
    return jnp.broadcast_to(message[B : B + 1].astype(F32), (16, B)).astype(BF16)


def weight_row(message):
    tail = message[B:].astype(F32)
    return (tail[1:2] + tail[2:3]) + tail[3:4]


def with_zone(message, zone):
    return jnp.concatenate([message[:B], jnp.concatenate([zone] * (B // 16), axis=0)], axis=1)


def tail_rows(zone_row, log_row):
    row = lax.broadcasted_iota(jnp.int32, (16, B), 0)
    tail = jnp.where(row == 0, zone_row, 0.0)
    for k, part in enumerate(three_parts(log_row)):
        tail = jnp.where(row == k + 1, part.astype(F32), tail)
    return tail.astype(BF16)


def pack_body(rider, driver, log_a, log_b, rzone, dzone, table, rider_out, driver_out,
              a_row, b_row, rz, dz, tab, sems):
    c = lax.axis_index("c")
    copies = [
        pltpu.make_async_copy(rider.at[c], rider_out.at[0, pl.ds(0, B)], sems.at[0]),
        pltpu.make_async_copy(driver, driver_out.at[0, pl.ds(0, B)], sems.at[1]),
        pltpu.make_async_copy(log_a.at[pl.ds(c, 1)], a_row, sems.at[2]),
        pltpu.make_async_copy(log_b, b_row, sems.at[3]),
        pltpu.make_async_copy(rzone, rz, sems.at[4]),
        pltpu.make_async_copy(dzone, dz, sems.at[5]),
        pltpu.make_async_copy(table, tab, sems.at[6]),
    ]
    for copy in copies:
        copy.start()
    for copy in copies:
        copy.wait()
    lane = lax.broadcasted_iota(jnp.int32, (16, B), 1)
    hot = jnp.where(lane == rz[c], 1.0, 0.0)
    zone = dz[0]
    shut = jnp.zeros((16, B), F32)
    for k in range(16):
        shut = jnp.where((lane == k) & (tab[k, zone] != 1), PENALTY, shut)
    rider_out[0, B:, :] = tail_rows(hot, a_row[...])
    driver_out[0, B:, :] = tail_rows(shut, b_row[...])
    for k in range(1, DB):
        driver_out[k] = driver_out[0]


def place(far, slot):
    yl, x = lax.axis_index("yl"), lax.axis_index("x")
    first, second = slot % 2, slot // 2
    x = x + far * (3 - 2 * x)
    x = x + second * (1 - 2 * (x % 2))
    return (yl + first * (1 - 2 * yl)) * 4 + x


def block_of(r):
    c = lax.axis_index("c")
    other = r % 2
    return 2 * place(r // 8, r // 2 % 4) + c + other * (1 - 2 * c)


def block_of(r):
    c = lax.axis_index("c")
    other = r % 2
    return 2 * place(r // 8, r // 2 % 4) + c + other * (1 - 2 * c)


def widen(messages, wide):
    for k, message in enumerate(messages):
        wide[k * B : (k + 1) * B] = with_zone(message, zone_rows(message))


def rider_rows(riders, drivers, rows, first):
    def pair(h, carry):
        one, two = riders[2 * h], riders[2 * h + 1]
        right = jnp.concatenate(
            [with_zone(one, zone_rows(one)), with_zone(two, zone_rows(two))], axis=0
        )
        cost = product(drivers[...], right)
        pieces = [cost[z * B : (z + 1) * B] for z in range(DB)]
        low = tree([fold(piece, jnp.minimum) for piece in pieces], jnp.minimum)
        low = jnp.min(low, axis=0, keepdims=True)
        mass = tree([fold(jnp.exp(low - piece), jnp.add) for piece in pieces], jnp.add)
        total = jnp.log(jnp.sum(mass, axis=0, keepdims=True)) - low
        rows[pl.ds(first + 2 * h, 1), :] = total[:, :B]
        rows[pl.ds(first + 2 * h + 1, 1), :] = total[:, B:]
        return carry

    lax.fori_loop(0, 2, pair, 0)


def rider_near_body(near, driver, rows, wide):
    widen([driver[z] for z in range(DB)], wide)
    rider_rows(near, wide, rows, 0)


def rider_far_body(far, wide, rows):
    rider_rows(far, wide, rows, 0)


def rider_other_body(near, far, wide, own_near, own_far, out, rows):
    rider_rows(near, wide, rows, 0)
    rider_rows(far, wide, rows, 4)
    for r in range(RB):
        slot = r // 2 % 4
        if r % 2:
            row = rows[4 * (r // 8) + slot : 4 * (r // 8) + slot + 1]
        else:
            row = (own_far if r >= 8 else own_near)[slot : slot + 1]
        out[pl.ds(block_of(r), 1), :] = row


def log_total(sums):
    parts = [sums[k] for k in range(sums.shape[0])]
    peak = tree(parts, jnp.maximum)
    return peak + jnp.log(tree([jnp.exp(part - peak) for part in parts], jnp.add))


def total_of(sums):
    return tree([sums[k] for k in range(sums.shape[0])], jnp.add)


def driver_first_body(sums, own_near, own_far, other_near, other_far, driver, right,
                      out, kernel, peaks, pots, ucol, left):
    riders = ((own_near, other_near), (own_far, other_far))
    messages = [riders[r // 8][r % 2][r // 2 % 4] for r in range(RB)]
    widen(messages, left)
    for r in range(RB):
        pots[pl.ds(RB + block_of(r), 1), :] = weight_row(messages[r])
    for j in range(DB):
        peaks[DB + j : DB + j + 1, :] = weight_row(driver[j])
    pots[0:RB] = pots[RB:] - (log_total(sums) - LOG_DRIVERS)
    for r in range(RB):
        ucol[r * B : (r + 1) * B, :] = column(pots[pl.ds(block_of(r), 1), :])

    def pair(h, carry):
        lanes = pl.ds(pl.multiple_of(h * 2 * B, 2 * B), 2 * B)
        cost = product(left[...], right[lanes, :])
        high = jnp.full((8, 2 * B), FLOOR, F32)
        for r in range(RB):
            u = ucol[r * B : (r + 1) * B, :]
            score = jnp.concatenate([u, u], axis=1) - cost[r * B : (r + 1) * B]
            kernel[r * B : (r + 1) * B, lanes] = score
            high = jnp.maximum(high, fold(score, jnp.maximum))
        top = jnp.max(high, axis=0, keepdims=True)
        total = jnp.zeros((8, 2 * B), F32)
        for r in range(RB):
            term = jnp.exp(kernel[r * B : (r + 1) * B, lanes] - top)
            kernel[r * B : (r + 1) * B, lanes] = term
            total = total + fold(term, jnp.add)
        total = top + jnp.log(jnp.maximum(jnp.sum(total, axis=0, keepdims=True), TINY))
        for k in range(2):
            peaks[pl.ds(2 * h + k, 1), :] = top[:, k * B : (k + 1) * B]
            out[0, pl.ds(2 * h + k, 1), :] = total[:, k * B : (k + 1) * B]
        return carry

    lax.fori_loop(0, DB // 2, pair, 0)
    for k in range(1, DB):
        out[k] = out[0]


def row_sums(kernel, scale, out):
    for r in range(RB):
        rows = slice(r * B, (r + 1) * B)
        acc = kernel[rows, 0:B] * scale[0:1]
        for k in range(1, DB):
            acc = acc + kernel[rows, k * B : (k + 1) * B] * scale[k : k + 1]
        out[pl.ds(block_of(r), 1), :] = jnp.sum(acc.T, axis=0, keepdims=True)


def column_sums(kernel, f, state, fcol, hold):
    hold[...] = f
    for r in range(RB):
        fcol[r * B : (r + 1) * B, :] = column(hold[pl.ds(block_of(r), 1), :])

    def block(r, acc):
        for k in range(B // 8):
            rows = pl.ds(pl.multiple_of(r * B + 8 * k, 8), 8)
            f = fcol[rows, :]
            acc = tuple(a + kernel[rows, j * B : (j + 1) * B] * f for j, a in enumerate(acc))
        return acc

    acc = lax.fori_loop(0, RB, block, tuple(jnp.zeros((8, B), F32) for _ in range(DB)))
    for j in range(DB):
        hold[j : j + 1, :] = jnp.sum(acc[j], axis=0, keepdims=True)
    return hold[0:DB] * state[2 * DB : 3 * DB]


def rider_second_body(sums, peaks, kernel, out, state):
    log_b = peaks[DB:]
    pot = log_b - (log_total(sums) - LOG_RIDERS)
    state[0:DB] = pot
    state[DB : 2 * DB] = log_b
    state[2 * DB :] = jnp.exp(pot + peaks[0:DB])
    row_sums(kernel, state.at[pl.ds(2 * DB, DB)], out)


def driver_next_body(sums, pots, state, kernel, out, fcol, hold):
    rows = column_sums(kernel, jnp.exp(pots[RB:] + LOG_DRIVERS) / total_of(sums), state, fcol, hold)
    for k in range(DB):
        out[k] = rows


def rider_next_body(sums, state, kernel, out, scale):
    scale[...] = state[2 * DB :] * (jnp.exp(state[DB : 2 * DB] + LOG_RIDERS) / total_of(sums))
    row_sums(kernel, scale, out)


def driver_last_body(sums, pots, state, kernel, out, fcol, hold):
    f = jnp.exp(pots[RB:] + LOG_DRIVERS) / total_of(sums)
    rows = column_sums(kernel, f, state, fcol, hold)
    for k in range(DB):
        out[k] = jnp.broadcast_to(rows[k : k + 1], (8, B))


def finish_body(sums, state, rider_sums, pots, rider_pot, driver_pot, hold):
    z = lax.axis_index("z")
    pot = state[pl.ds(z, 1), :]
    log_b = state[pl.ds(DB + z, 1), :]
    driver_pot[...] = pot + (log_b + LOG_RIDERS - jnp.log(total_of(sums)[0:1]))
    hold[...] = pots[0:RB] + (pots[RB:] + LOG_DRIVERS - jnp.log(total_of(rider_sums)))
    block = lax.axis_index("yl") * 4 + lax.axis_index("x")
    rider_pot[0:1] = hold[pl.ds(2 * block, 1), :]
    rider_pot[1:2] = hold[pl.ds(2 * block + 1, 1), :]


def exchange(message, axes):
    return lax.all_to_all(message, axes, 0, 0, tiled=True)


def swap(value, axis, partner):
    return lax.ppermute(value, axis, [(k, partner(k)) for k in range(SIZES[AXES.index(axis)])])


def log_add(a, b):
    peak = jnp.maximum(a, b)
    return peak + jnp.log(jnp.exp(a - peak) + jnp.exp(b - peak))


def close(value, op):
    value = op(value, swap(value, "c", lambda k: 1 - k))
    return exchange(jnp.broadcast_to(value[None], (PEERS, RB, B)), PLANE)


def rider_first(message, drivers):
    near = jnp.concatenate([message, swap(message, "yl", lambda k: 1 - k)], axis=0)
    near, drivers = lax.optimization_barrier((near, drivers))
    drivers = exchange(drivers, "z")
    near = jnp.concatenate([near, swap(near, "x", lambda k: k ^ 1)], axis=0)
    far = swap(near, "x", lambda k: 3 - k)
    quarter = pl.CostEstimate(flops=2**30, transcendentals=2**19, bytes_accessed=2**21)
    near_rows, wide = call(
        rider_near_body, [f32(4, B), bf16(DB * B, 2 * B)], [VM] * 2, cost=quarter
    )(near, drivers)
    near, far, near_rows = lax.optimization_barrier((near, far, near_rows))
    other_near, other_far = (swap(value, "c", lambda k: 1 - k) for value in (near, far))
    (far_rows,) = call(rider_far_body, [f32(4, B)], [VM] * 2, cost=quarter)(far, wide)
    (sums,) = call(rider_other_body, [f32(RB, B)], [VM] * 5, [pltpu.VMEM((8, B), F32)])(
        other_near, other_far, wide, near_rows, far_rows
    )
    return sums, (near, far, other_near, other_far, drivers, wide)


def per_device(rider_emb, driver_emb, log_a, log_b, rider_zone, driver_zone, zone_table):
    rider_msg, driver_msg = call(
        pack_body,
        [pltpu.VMEM((1, PAY, B), BF16), pltpu.VMEM((DB, PAY, B), BF16)],
        [FAR] * 7,
        [
            pltpu.VMEM((1, B), F32),
            pltpu.VMEM((1, B), F32),
            pltpu.SMEM((2,), jnp.int32),
            pltpu.SMEM((1,), jnp.int32),
            pltpu.SMEM((16, 16), jnp.int32),
            pltpu.SemaphoreType.DMA((7,)),
        ],
        limit=60,
    )(
        rider_emb.reshape(2, B, B), driver_emb, log_a.reshape(2, B), log_b.reshape(1, B),
        rider_zone, driver_zone, zone_table,
    )
    sums, gathered = rider_first(rider_msg, driver_msg)
    sums = close(sums, log_add)
    columns = pltpu.VMEM((RB * B, B), F32)
    sums, kernel, peaks, pots = call(
        driver_first_body,
        [f32(DB, DB, B), f32(RB * B, DB * B), f32(2 * DB, B), f32(2 * RB, B)],
        [VM] * 7,
        [columns, pltpu.VMEM((RB * B, 2 * B), BF16)],
    )(sums, *gathered)
    sums = exchange(sums, "z")
    columns = [columns, pltpu.VMEM((RB, B), F32)]
    sums, state = call(rider_second_body, [f32(RB, B), f32(3 * DB, B)], [VM] * 3)(
        sums, peaks, kernel
    )
    sums = close(sums, jnp.add)
    for _ in range(ITERS - 2):
        (sums,) = call(driver_next_body, [f32(DB, DB, B)], [VM] * 4, columns)(
            sums, pots, state, kernel
        )
        sums = exchange(sums, "z")
        (sums,) = call(rider_next_body, [f32(RB, B)], [VM] * 3, [pltpu.VMEM((DB, B), F32)])(
            sums, state, kernel
        )
        sums = close(sums, jnp.add)
    rider_sums = sums
    (sums,) = call(driver_last_body, [f32(DB, 8, B)], [VM] * 4, columns)(
        rider_sums, pots, state, kernel
    )
    sums = exchange(sums, "z")
    rider_pot, driver_pot = call(
        finish_body, [f32(2, B), f32(1, B)], [VM] * 4, [pltpu.VMEM((RB, B), F32)]
    )(sums, state, rider_sums, pots)
    return rider_pot.reshape(2 * B), driver_pot.reshape(B)


def solution(mesh):
    fine = Mesh(mesh.devices.reshape(SIZES), AXES)
    row, every = ("z", "yl", "x"), AXES
    placed = (
        P(row, None),
        P(every, None),
        P(row),
        P(every),
        P(row),
        P(every),
        P(),
    )
    return jax.shard_map(
        per_device,
        mesh=fine,
        in_specs=placed,
        out_specs=(P(row), P(every)),
        check_vma=False,
    )
```

```python
import math

import jax
import jax.numpy as jnp
from jax import lax
from jax.experimental import pallas as pl
from jax.experimental.pallas import tpu as pltpu
from jax.sharding import Mesh, PartitionSpec as P

AXES = ("z", "yl", "x", "yh", "c")
SIZES = (8, 2, 4, 2, 2)
PLANE = ("yl", "x", "yh")
PEERS = 16

B = 128
RB = 16
DB = 8
PAY = B + 16
ITERS = 3
LOG_DRIVERS = math.log(32768)
LOG_RIDERS = math.log(16384)
PENALTY = 1e30
FLOOR = -1e29
TINY = 1e-37

F32 = jnp.float32
BF16 = jnp.bfloat16
VM = pl.BlockSpec(memory_space=pltpu.VMEM)
FAR = pl.BlockSpec(memory_space=pltpu.HBM)


def call(body, outs, ins, scratch=(), limit=40, cost=None):
    return pl.pallas_call(
        body,
        out_shape=outs,
        in_specs=ins,
        out_specs=[VM] * len(outs),
        cost_estimate=cost,
        scratch_shapes=list(scratch),
        compiler_params=pltpu.CompilerParams(vmem_limit_bytes=limit * 2**20),
    )


def f32(*shape):
    return jax.ShapeDtypeStruct(shape, F32)


def bf16(*shape):
    return jax.ShapeDtypeStruct(shape, BF16)


def product(left, right):
    return lax.dot_general(left, right, (((1,), (1,)), ((), ())), preferred_element_type=F32)


def tree(parts, op):
    while len(parts) > 1:
        parts = [op(parts[2 * k], parts[2 * k + 1]) for k in range(len(parts) // 2)]
    return parts[0]


def fold(block, op):
    return tree([block[8 * k : 8 * k + 8] for k in range(B // 8)], op)


def column(row):
    return jnp.broadcast_to(row, (B, B)).T


def three_parts(value):
    high = value.astype(BF16)
    rest = value - high.astype(F32)
    middle = rest.astype(BF16)
    return high, middle, (rest - middle.astype(F32)).astype(BF16)


def zone_rows(message):
    return jnp.broadcast_to(message[B : B + 1].astype(F32), (16, B)).astype(BF16)


def weight_row(message):
    tail = message[B:].astype(F32)
    return (tail[1:2] + tail[2:3]) + tail[3:4]


def with_zone(message, zone):
    return jnp.concatenate([message[:B], jnp.concatenate([zone] * (B // 16), axis=0)], axis=1)


def tail_rows(zone_row, log_row):
    row = lax.broadcasted_iota(jnp.int32, (16, B), 0)
    tail = jnp.where(row == 0, zone_row, 0.0)
    for k, part in enumerate(three_parts(log_row)):
        tail = jnp.where(row == k + 1, part.astype(F32), tail)
    return tail.astype(BF16)


def pack_body(rider, driver, log_a, log_b, rzone, dzone, table, rider_out, driver_out,
              a_row, b_row, rz, dz, tab, sems):
    c = lax.axis_index("c")
    copies = [
        pltpu.make_async_copy(rider.at[c], rider_out.at[0, pl.ds(0, B)], sems.at[0]),
        pltpu.make_async_copy(driver, driver_out.at[0, pl.ds(0, B)], sems.at[1]),
        pltpu.make_async_copy(log_a.at[pl.ds(c, 1)], a_row, sems.at[2]),
        pltpu.make_async_copy(log_b, b_row, sems.at[3]),
        pltpu.make_async_copy(rzone, rz, sems.at[4]),
        pltpu.make_async_copy(dzone, dz, sems.at[5]),
        pltpu.make_async_copy(table, tab, sems.at[6]),
    ]
    for copy in copies:
        copy.start()
    for copy in copies:
        copy.wait()
    lane = lax.broadcasted_iota(jnp.int32, (16, B), 1)
    hot = jnp.where(lane == rz[c], 1.0, 0.0)
    zone = dz[0]
    shut = jnp.zeros((16, B), F32)
    for k in range(16):
        shut = jnp.where((lane == k) & (tab[k, zone] != 1), PENALTY, shut)
    rider_out[0, B:, :] = tail_rows(hot, a_row[...])
    driver_out[0, B:, :] = tail_rows(shut, b_row[...])
    for k in range(1, DB):
        driver_out[k] = driver_out[0]


def place(far, slot):
    yl, x = lax.axis_index("yl"), lax.axis_index("x")
    first, second = slot % 2, slot // 2
    x = x + far * (3 - 2 * x)
    x = x + second * (1 - 2 * (x % 2))
    return (yl + first * (1 - 2 * yl)) * 4 + x


def block_of(r):
    c = lax.axis_index("c")
    other = r % 2
    return 2 * place(r // 8, r // 2 % 4) + c + other * (1 - 2 * c)


def block_of(r):
    c = lax.axis_index("c")
    other = r % 2
    return 2 * place(r // 8, r // 2 % 4) + c + other * (1 - 2 * c)


def widen(messages, wide):
    for k, message in enumerate(messages):
        wide[k * B : (k + 1) * B] = with_zone(message, zone_rows(message))


def rider_rows(riders, drivers, rows, first):
    def pair(h, carry):
        one, two = riders[2 * h], riders[2 * h + 1]
        right = jnp.concatenate(
            [with_zone(one, zone_rows(one)), with_zone(two, zone_rows(two))], axis=0
        )
        cost = product(drivers[...], right)
        pieces = [cost[z * B : (z + 1) * B] for z in range(DB)]
        low = tree([fold(piece, jnp.minimum) for piece in pieces], jnp.minimum)
        low = jnp.min(low, axis=0, keepdims=True)
        mass = tree([fold(jnp.exp(low - piece), jnp.add) for piece in pieces], jnp.add)
        total = jnp.log(jnp.sum(mass, axis=0, keepdims=True)) - low
        rows[pl.ds(first + 2 * h, 1), :] = total[:, :B]
        rows[pl.ds(first + 2 * h + 1, 1), :] = total[:, B:]
        return carry

    lax.fori_loop(0, 2, pair, 0)


def rider_near_body(near, driver, rows, wide):
    widen([driver[z] for z in range(DB)], wide)
    rider_rows(near, wide, rows, 0)


def rider_far_body(far, wide, rows):
    rider_rows(far, wide, rows, 0)


def rider_other_body(near, far, wide, own_near, own_far, out, rows):
    rider_rows(near, wide, rows, 0)
    rider_rows(far, wide, rows, 4)
    for r in range(RB):
        slot = r // 2 % 4
        if r % 2:
            row = rows[4 * (r // 8) + slot : 4 * (r // 8) + slot + 1]
        else:
            row = (own_far if r >= 8 else own_near)[slot : slot + 1]
        out[pl.ds(block_of(r), 1), :] = row


def log_total(sums):
    parts = [sums[k] for k in range(sums.shape[0])]
    peak = tree(parts, jnp.maximum)
    return peak + jnp.log(tree([jnp.exp(part - peak) for part in parts], jnp.add))


def total_of(sums):
    return tree([sums[k] for k in range(sums.shape[0])], jnp.add)


def driver_first_body(sums, own_near, own_far, other_near, other_far, driver, right,
                      out, kernel, peaks, pots, ucol, left):
    riders = ((own_near, other_near), (own_far, other_far))
    messages = [riders[r // 8][r % 2][r // 2 % 4] for r in range(RB)]
    widen(messages, left)
    for r in range(RB):
        pots[pl.ds(RB + block_of(r), 1), :] = weight_row(messages[r])
    for j in range(DB):
        peaks[DB + j : DB + j + 1, :] = weight_row(driver[j])
    pots[0:RB] = pots[RB:] - (log_total(sums) - LOG_DRIVERS)
    for r in range(RB):
        ucol[r * B : (r + 1) * B, :] = column(pots[pl.ds(block_of(r), 1), :])

    def four(h, carry):
        lanes = pl.ds(pl.multiple_of(h * 4 * B, 4 * B), 4 * B)
        cost = product(left[...], right[lanes, :])
        high = jnp.full((8, 4 * B), FLOOR, F32)
        for r in range(RB):
            u = ucol[r * B : (r + 1) * B, :]
            score = jnp.concatenate([u] * 4, axis=1) - cost[r * B : (r + 1) * B]
            kernel[r * B : (r + 1) * B, lanes] = score
            high = jnp.maximum(high, fold(score, jnp.maximum))
        top = jnp.max(high, axis=0, keepdims=True)
        total = jnp.zeros((8, 4 * B), F32)
        for r in range(RB):
            term = jnp.exp(kernel[r * B : (r + 1) * B, lanes] - top)
            kernel[r * B : (r + 1) * B, lanes] = term
            total = total + fold(term, jnp.add)
        total = top + jnp.log(jnp.maximum(jnp.sum(total, axis=0, keepdims=True), TINY))
        for k in range(4):
            peaks[pl.ds(4 * h + k, 1), :] = top[:, k * B : (k + 1) * B]
            out[0, pl.ds(4 * h + k, 1), :] = total[:, k * B : (k + 1) * B]
        return carry

    lax.fori_loop(0, DB // 4, four, 0)
    for k in range(1, DB):
        out[k] = out[0]


def row_sums(kernel, scale, out):
    for r in range(RB):
        rows = slice(r * B, (r + 1) * B)
        acc = kernel[rows, 0:B] * scale[0:1]
        for k in range(1, DB):
            acc = acc + kernel[rows, k * B : (k + 1) * B] * scale[k : k + 1]
        out[pl.ds(block_of(r), 1), :] = jnp.sum(acc.T, axis=0, keepdims=True)


def column_sums(kernel, f, state, fcol, hold):
    hold[...] = f
    for r in range(RB):
        fcol[r * B : (r + 1) * B, :] = column(hold[pl.ds(block_of(r), 1), :])

    def block(r, acc):
        for k in range(B // 8):
            rows = pl.ds(pl.multiple_of(r * B + 8 * k, 8), 8)
            f = fcol[rows, :]
            acc = tuple(a + kernel[rows, j * B : (j + 1) * B] * f for j, a in enumerate(acc))
        return acc

    acc = lax.fori_loop(0, RB, block, tuple(jnp.zeros((8, B), F32) for _ in range(DB)))
    for j in range(DB):
        hold[j : j + 1, :] = jnp.sum(acc[j], axis=0, keepdims=True)
    return hold[0:DB] * state[2 * DB : 3 * DB]


def rider_second_body(sums, peaks, kernel, out, state):
    log_b = peaks[DB:]
    pot = log_b - (log_total(sums) - LOG_RIDERS)
    state[0:DB] = pot
    state[DB : 2 * DB] = log_b
    state[2 * DB :] = jnp.exp(pot + peaks[0:DB])
    row_sums(kernel, state.at[pl.ds(2 * DB, DB)], out)


def driver_next_body(sums, pots, state, kernel, out, fcol, hold):
    rows = column_sums(kernel, jnp.exp(pots[RB:] + LOG_DRIVERS) / total_of(sums), state, fcol, hold)
    for k in range(DB):
        out[k] = rows


def rider_next_body(sums, state, kernel, out, scale):
    scale[...] = state[2 * DB :] * (jnp.exp(state[DB : 2 * DB] + LOG_RIDERS) / total_of(sums))
    row_sums(kernel, scale, out)


def driver_last_body(sums, pots, state, kernel, out, fcol, hold):
    f = jnp.exp(pots[RB:] + LOG_DRIVERS) / total_of(sums)
    rows = column_sums(kernel, f, state, fcol, hold)
    for k in range(DB):
        out[k] = jnp.broadcast_to(rows[k : k + 1], (8, B))


def finish_body(sums, state, rider_sums, pots, rider_pot, driver_pot, hold):
    z = lax.axis_index("z")
    pot = state[pl.ds(z, 1), :]
    log_b = state[pl.ds(DB + z, 1), :]
    driver_pot[...] = pot + (log_b + LOG_RIDERS - jnp.log(total_of(sums)[0:1]))
    hold[...] = pots[0:RB] + (pots[RB:] + LOG_DRIVERS - jnp.log(total_of(rider_sums)))
    block = lax.axis_index("yl") * 4 + lax.axis_index("x")
    rider_pot[0:1] = hold[pl.ds(2 * block, 1), :]
    rider_pot[1:2] = hold[pl.ds(2 * block + 1, 1), :]


def exchange(message, axes):
    return lax.all_to_all(message, axes, 0, 0, tiled=True)


def swap(value, axis, partner):
    return lax.ppermute(value, axis, [(k, partner(k)) for k in range(SIZES[AXES.index(axis)])])


def log_add(a, b):
    peak = jnp.maximum(a, b)
    return peak + jnp.log(jnp.exp(a - peak) + jnp.exp(b - peak))


def close(value, op):
    value = op(value, swap(value, "c", lambda k: 1 - k))
    return exchange(jnp.broadcast_to(value[None], (PEERS, RB, B)), PLANE)


def rider_first(message, drivers):
    near = jnp.concatenate([message, swap(message, "yl", lambda k: 1 - k)], axis=0)
    drivers = exchange(drivers, "z")
    near = jnp.concatenate([near, swap(near, "x", lambda k: k ^ 1)], axis=0)
    far = swap(near, "x", lambda k: 3 - k)
    quarter = pl.CostEstimate(flops=2**30, transcendentals=2**19, bytes_accessed=2**21)
    near_rows, wide = call(
        rider_near_body, [f32(4, B), bf16(DB * B, 2 * B)], [VM] * 2, cost=quarter
    )(near, drivers)
    near, far, near_rows = lax.optimization_barrier((near, far, near_rows))
    other_near, other_far = (swap(value, "c", lambda k: 1 - k) for value in (near, far))
    (far_rows,) = call(rider_far_body, [f32(4, B)], [VM] * 2, cost=quarter)(far, wide)
    (sums,) = call(rider_other_body, [f32(RB, B)], [VM] * 5, [pltpu.VMEM((8, B), F32)])(
        other_near, other_far, wide, near_rows, far_rows
    )
    return sums, (near, far, other_near, other_far, drivers, wide)


def per_device(rider_emb, driver_emb, log_a, log_b, rider_zone, driver_zone, zone_table):
    rider_msg, driver_msg = call(
        pack_body,
        [pltpu.VMEM((1, PAY, B), BF16), pltpu.VMEM((DB, PAY, B), BF16)],
        [FAR] * 7,
        [
            pltpu.VMEM((1, B), F32),
            pltpu.VMEM((1, B), F32),
            pltpu.SMEM((2,), jnp.int32),
            pltpu.SMEM((1,), jnp.int32),
            pltpu.SMEM((16, 16), jnp.int32),
            pltpu.SemaphoreType.DMA((7,)),
        ],
        limit=60,
    )(
        rider_emb.reshape(2, B, B), driver_emb, log_a.reshape(2, B), log_b.reshape(1, B),
        rider_zone, driver_zone, zone_table,
    )
    sums, gathered = rider_first(rider_msg, driver_msg)
    sums = close(sums, log_add)
    columns = pltpu.VMEM((RB * B, B), F32)
    sums, kernel, peaks, pots = call(
        driver_first_body,
        [f32(DB, DB, B), f32(RB * B, DB * B), f32(2 * DB, B), f32(2 * RB, B)],
        [VM] * 7,
        [columns, pltpu.VMEM((RB * B, 2 * B), BF16)],
    )(sums, *gathered)
    sums = exchange(sums, "z")
    columns = [columns, pltpu.VMEM((RB, B), F32)]
    sums, state = call(rider_second_body, [f32(RB, B), f32(3 * DB, B)], [VM] * 3)(
        sums, peaks, kernel
    )
    sums = close(sums, jnp.add)
    for _ in range(ITERS - 2):
        (sums,) = call(driver_next_body, [f32(DB, DB, B)], [VM] * 4, columns)(
            sums, pots, state, kernel
        )
        sums = exchange(sums, "z")
        (sums,) = call(rider_next_body, [f32(RB, B)], [VM] * 3, [pltpu.VMEM((DB, B), F32)])(
            sums, state, kernel
        )
        sums = close(sums, jnp.add)
    rider_sums = sums
    (sums,) = call(driver_last_body, [f32(DB, 8, B)], [VM] * 4, columns)(
        rider_sums, pots, state, kernel
    )
    sums = exchange(sums, "z")
    rider_pot, driver_pot = call(
        finish_body, [f32(2, B), f32(1, B)], [VM] * 4, [pltpu.VMEM((RB, B), F32)]
    )(sums, state, rider_sums, pots)
    return rider_pot.reshape(2 * B), driver_pot.reshape(B)


def solution(mesh):
    fine = Mesh(mesh.devices.reshape(SIZES), AXES)
    row, every = ("z", "yl", "x"), AXES
    placed = (
        P(row, None),
        P(every, None),
        P(row),
        P(every),
        P(row),
        P(every),
        P(),
    )
    return jax.shard_map(
        per_device,
        mesh=fine,
        in_specs=placed,
        out_specs=(P(row), P(every)),
        check_vma=False,
    )
```

```python
import math

import jax
import jax.numpy as jnp
from jax import lax
from jax.experimental import pallas as pl
from jax.experimental.pallas import tpu as pltpu
from jax.sharding import Mesh, PartitionSpec as P

AXES = ("z", "yl", "x", "yh", "c")
SIZES = (8, 2, 4, 2, 2)
PLANE = ("yl", "x", "yh")
PEERS = 16

B = 128
RB = 16
DB = 8
PAY = B + 16
ITERS = 3
LOG_DRIVERS = math.log(32768)
LOG_RIDERS = math.log(16384)
PENALTY = 1e30
FLOOR = -1e29
TINY = 1e-37

F32 = jnp.float32
BF16 = jnp.bfloat16
VM = pl.BlockSpec(memory_space=pltpu.VMEM)
FAR = pl.BlockSpec(memory_space=pltpu.HBM)


def call(body, outs, ins, scratch=(), limit=20, cost=None):
    return pl.pallas_call(
        body,
        out_shape=outs,
        in_specs=ins,
        out_specs=[VM] * len(outs),
        cost_estimate=cost,
        scratch_shapes=list(scratch),
        compiler_params=pltpu.CompilerParams(vmem_limit_bytes=limit * 2**20),
    )


def f32(*shape):
    return jax.ShapeDtypeStruct(shape, F32)


def bf16(*shape):
    return jax.ShapeDtypeStruct(shape, BF16)


def product(left, right):
    return lax.dot_general(left, right, (((1,), (1,)), ((), ())), preferred_element_type=F32)


def tree(parts, op):
    while len(parts) > 1:
        parts = [op(parts[2 * k], parts[2 * k + 1]) for k in range(len(parts) // 2)]
    return parts[0]


def fold(block, op):
    return tree([block[8 * k : 8 * k + 8] for k in range(B // 8)], op)


def column(row):
    return jnp.broadcast_to(row, (B, B)).T


def three_parts(value):
    high = value.astype(BF16)
    rest = value - high.astype(F32)
    middle = rest.astype(BF16)
    return high, middle, (rest - middle.astype(F32)).astype(BF16)


def zone_rows(message):
    return jnp.broadcast_to(message[B : B + 1].astype(F32), (16, B)).astype(BF16)


def weight_row(message):
    tail = message[B:].astype(F32)
    return (tail[1:2] + tail[2:3]) + tail[3:4]


def with_zone(message, zone):
    return jnp.concatenate([message[:B], jnp.concatenate([zone] * (B // 16), axis=0)], axis=1)


def tail_rows(zone_row, log_row):
    row = lax.broadcasted_iota(jnp.int32, (16, B), 0)
    tail = jnp.where(row == 0, zone_row, 0.0)
    for k, part in enumerate(three_parts(log_row)):
        tail = jnp.where(row == k + 1, part.astype(F32), tail)
    return tail.astype(BF16)


def pack_body(rider, driver, log_a, log_b, rzone, dzone, table, rider_out, driver_out,
              a_row, b_row, rz, dz, tab, sems):
    c = lax.axis_index("c")
    copies = [
        pltpu.make_async_copy(rider.at[c], rider_out.at[0, pl.ds(0, B)], sems.at[0]),
        pltpu.make_async_copy(driver, driver_out.at[0, pl.ds(0, B)], sems.at[1]),
        pltpu.make_async_copy(log_a.at[pl.ds(c, 1)], a_row, sems.at[2]),
        pltpu.make_async_copy(log_b, b_row, sems.at[3]),
        pltpu.make_async_copy(rzone, rz, sems.at[4]),
        pltpu.make_async_copy(dzone, dz, sems.at[5]),
        pltpu.make_async_copy(table, tab, sems.at[6]),
    ]
    for copy in copies:
        copy.start()
    for copy in copies:
        copy.wait()
    lane = lax.broadcasted_iota(jnp.int32, (16, B), 1)
    hot = jnp.where(lane == rz[c], 1.0, 0.0)
    zone = dz[0]
    shut = jnp.zeros((16, B), F32)
    for k in range(16):
        shut = jnp.where((lane == k) & (tab[k, zone] != 1), PENALTY, shut)
    rider_out[0, B:, :] = tail_rows(hot, a_row[...])
    driver_out[0, B:, :] = tail_rows(shut, b_row[...])
    for k in range(1, DB):
        driver_out[k] = driver_out[0]


def place(far, slot):
    yl, x = lax.axis_index("yl"), lax.axis_index("x")
    first, second = slot % 2, slot // 2
    x = x + far * (3 - 2 * x)
    x = x + second * (1 - 2 * (x % 2))
    return (yl + first * (1 - 2 * yl)) * 4 + x


def block_of(r):
    c = lax.axis_index("c")
    return 2 * place(r // 4 % 2, r % 4) + c + r // 8 * (1 - 2 * c)


def widen(messages, wide):
    for k, message in enumerate(messages):
        wide[k * B : (k + 1) * B] = with_zone(message, zone_rows(message))


def rider_rows(riders, drivers, cost, rows, first, left):
    widen([riders[k] for k in range(4)], left)
    for h in range(DB // 2):
        lanes = slice(2 * h * B, 2 * (h + 1) * B)
        cost[:, lanes] = product(left[...], drivers[lanes, :])
    for k in range(4):
        pieces = [cost[k * B : (k + 1) * B, j * B : (j + 1) * B] for j in range(DB)]
        low = tree(pieces, jnp.minimum)
        mass = tree([jnp.exp(low - piece) for piece in pieces], jnp.add).T
        low = low.T
        least = jnp.min(low, axis=0, keepdims=True)
        mass = jnp.sum(mass * jnp.exp(least - low), axis=0, keepdims=True)
        rows[first + k : first + k + 1, :] = jnp.log(mass) - least


def rider_near_body(near, driver, cost, rows, wide, left):
    widen([driver[z] for z in range(DB)], wide)
    rider_rows(near, wide, cost, rows, 0, left)


def rider_far_body(far, wide, cost, rows, left):
    rider_rows(far, wide, cost, rows, 0, left)


def rider_other_body(near, far, wide, own_near, own_far, near_cost, far_cost, out, rows, left):
    rows[0:4] = own_near[...]
    rows[4:8] = own_far[...]
    rider_rows(near, wide, near_cost, rows, 8, left)
    rider_rows(far, wide, far_cost, rows, 12, left)
    for r in range(RB):
        out[pl.ds(block_of(r), 1), :] = rows[r : r + 1]


def log_total(sums):
    parts = [sums[k] for k in range(sums.shape[0])]
    peak = tree(parts, jnp.maximum)
    return peak + jnp.log(tree([jnp.exp(part - peak) for part in parts], jnp.add))


def total_of(sums):
    return tree([sums[k] for k in range(sums.shape[0])], jnp.add)


def driver_first_body(sums, own_near, own_far, other_near, other_far, driver, *rest):
    *costs, out, kernel, peaks, pots, ucol = rest
    messages = (own_near, own_far, other_near, other_far)
    for r in range(RB):
        pots[pl.ds(RB + block_of(r), 1), :] = weight_row(messages[r // 4][r % 4])
    for j in range(DB):
        peaks[DB + j : DB + j + 1, :] = weight_row(driver[j])
    pots[0:RB] = pots[RB:] - (log_total(sums) - LOG_DRIVERS)
    for r in range(RB):
        ucol[r * B : (r + 1) * B, :] = column(pots[pl.ds(block_of(r), 1), :])

    def scores(r):
        u = ucol[r * B : (r + 1) * B, :]
        rows = slice(r % 4 * B, (r % 4 + 1) * B)
        return [u - costs[r // 4][rows, j * B : (j + 1) * B] for j in range(DB)]

    high = [jnp.full((8, B), FLOOR, F32)] * DB
    for r in range(RB):
        high = [jnp.maximum(h, fold(score, jnp.maximum)) for h, score in zip(high, scores(r))]
    top = [jnp.max(h, axis=0, keepdims=True) for h in high]
    total = [jnp.zeros((8, B), F32)] * DB
    for r in range(RB):
        for j, score in enumerate(scores(r)):
            term = jnp.exp(score - top[j])
            kernel[r * B : (r + 1) * B, j * B : (j + 1) * B] = term
            total[j] = total[j] + fold(term, jnp.add)
    for j in range(DB):
        mass = jnp.maximum(jnp.sum(total[j], axis=0, keepdims=True), TINY)
        peaks[j : j + 1] = top[j]
        out[0, j : j + 1] = top[j] + jnp.log(mass)
    for k in range(1, DB):
        out[k] = out[0]


def row_sums(kernel, scale, out):
    for r in range(RB):
        rows = slice(r * B, (r + 1) * B)
        acc = kernel[rows, 0:B] * scale[0:1]
        for k in range(1, DB):
            acc = acc + kernel[rows, k * B : (k + 1) * B] * scale[k : k + 1]
        out[pl.ds(block_of(r), 1), :] = jnp.sum(acc.T, axis=0, keepdims=True)


def column_sums(kernel, f, state, fcol, hold):
    hold[...] = f
    for r in range(RB):
        fcol[r * B : (r + 1) * B, :] = column(hold[pl.ds(block_of(r), 1), :])

    def block(r, acc):
        for k in range(B // 8):
            rows = pl.ds(pl.multiple_of(r * B + 8 * k, 8), 8)
            f = fcol[rows, :]
            acc = tuple(a + kernel[rows, j * B : (j + 1) * B] * f for j, a in enumerate(acc))
        return acc

    acc = lax.fori_loop(0, RB, block, tuple(jnp.zeros((8, B), F32) for _ in range(DB)))
    for j in range(DB):
        hold[j : j + 1, :] = jnp.sum(acc[j], axis=0, keepdims=True)
    return hold[0:DB] * state[2 * DB : 3 * DB]


def rider_second_body(sums, peaks, kernel, out, state):
    log_b = peaks[DB:]
    pot = log_b - (log_total(sums) - LOG_RIDERS)
    state[0:DB] = pot
    state[DB : 2 * DB] = log_b
    state[2 * DB :] = jnp.exp(pot + peaks[0:DB])
    row_sums(kernel, state.at[pl.ds(2 * DB, DB)], out)


def driver_next_body(sums, pots, state, kernel, out, fcol, hold):
    rows = column_sums(kernel, jnp.exp(pots[RB:] + LOG_DRIVERS) / total_of(sums), state, fcol, hold)
    for k in range(DB):
        out[k] = rows


def rider_next_body(sums, state, kernel, out, scale):
    scale[...] = state[2 * DB :] * (jnp.exp(state[DB : 2 * DB] + LOG_RIDERS) / total_of(sums))
    row_sums(kernel, scale, out)


def driver_last_body(sums, pots, state, kernel, out, fcol, hold):
    f = jnp.exp(pots[RB:] + LOG_DRIVERS) / total_of(sums)
    rows = column_sums(kernel, f, state, fcol, hold)
    for k in range(DB):
        out[k] = jnp.broadcast_to(rows[k : k + 1], (8, B))


def finish_body(sums, state, rider_sums, pots, rider_pot, driver_pot, hold):
    z = lax.axis_index("z")
    pot = state[pl.ds(z, 1), :]
    log_b = state[pl.ds(DB + z, 1), :]
    driver_pot[...] = pot + (log_b + LOG_RIDERS - jnp.log(total_of(sums)[0:1]))
    hold[...] = pots[0:RB] + (pots[RB:] + LOG_DRIVERS - jnp.log(total_of(rider_sums)))
    block = lax.axis_index("yl") * 4 + lax.axis_index("x")
    rider_pot[0:1] = hold[pl.ds(2 * block, 1), :]
    rider_pot[1:2] = hold[pl.ds(2 * block + 1, 1), :]


def exchange(message, axes):
    return lax.all_to_all(message, axes, 0, 0, tiled=True)


def swap(value, axis, partner):
    return lax.ppermute(value, axis, [(k, partner(k)) for k in range(SIZES[AXES.index(axis)])])


def log_add(a, b):
    peak = jnp.maximum(a, b)
    return peak + jnp.log(jnp.exp(a - peak) + jnp.exp(b - peak))


def close(value, op):
    value = op(value, swap(value, "c", lambda k: 1 - k))
    return exchange(jnp.broadcast_to(value[None], (PEERS, RB, B)), PLANE)


def rider_first(message, drivers):
    near = jnp.concatenate([message, swap(message, "yl", lambda k: 1 - k)], axis=0)
    drivers = exchange(drivers, "z")
    near = jnp.concatenate([near, swap(near, "x", lambda k: k ^ 1)], axis=0)
    far = swap(near, "x", lambda k: 3 - k)
    quarter = pl.CostEstimate(flops=2**30, transcendentals=2**19, bytes_accessed=2**21)
    cost, rows, left = f32(4 * B, DB * B), f32(4, B), pltpu.VMEM((4 * B, 2 * B), BF16)
    own_near_cost, near_rows, wide = call(
        rider_near_body, [cost, rows, bf16(DB * B, 2 * B)], [VM] * 2, [left], cost=quarter
    )(near, drivers)
    near, far, near_rows = lax.optimization_barrier((near, far, near_rows))
    other_near, other_far = (swap(value, "c", lambda k: 1 - k) for value in (near, far))
    own_far_cost, far_rows = call(rider_far_body, [cost, rows], [VM] * 2, [left], cost=quarter)(far, wide)
    other_near_cost, other_far_cost, sums = call(
        rider_other_body, [cost, cost, f32(RB, B)], [VM] * 5, [pltpu.VMEM((RB, B), F32), left]
    )(other_near, other_far, wide, near_rows, far_rows)
    costs = own_near_cost, own_far_cost, other_near_cost, other_far_cost
    return sums, (near, far, other_near, other_far, drivers, *costs)


def per_device(rider_emb, driver_emb, log_a, log_b, rider_zone, driver_zone, zone_table):
    rider_msg, driver_msg = call(
        pack_body,
        [pltpu.VMEM((1, PAY, B), BF16), pltpu.VMEM((DB, PAY, B), BF16)],
        [FAR] * 7,
        [
            pltpu.VMEM((1, B), F32),
            pltpu.VMEM((1, B), F32),
            pltpu.SMEM((2,), jnp.int32),
            pltpu.SMEM((1,), jnp.int32),
            pltpu.SMEM((16, 16), jnp.int32),
            pltpu.SemaphoreType.DMA((7,)),
        ],
        limit=60,
    )(
        rider_emb.reshape(2, B, B), driver_emb, log_a.reshape(2, B), log_b.reshape(1, B),
        rider_zone, driver_zone, zone_table,
    )
    sums, gathered = rider_first(rider_msg, driver_msg)
    sums = close(sums, log_add)
    columns = pltpu.VMEM((RB * B, B), F32)
    sums, kernel, peaks, pots = call(
        driver_first_body,
        [f32(DB, DB, B), f32(RB * B, DB * B), f32(2 * DB, B), f32(2 * RB, B)],
        [VM] * 10,
        [columns],
    )(sums, *gathered)
    sums = exchange(sums, "z")
    columns = [columns, pltpu.VMEM((RB, B), F32)]
    sums, state = call(rider_second_body, [f32(RB, B), f32(3 * DB, B)], [VM] * 3)(
        sums, peaks, kernel
    )
    sums = close(sums, jnp.add)
    for _ in range(ITERS - 2):
        (sums,) = call(driver_next_body, [f32(DB, DB, B)], [VM] * 4, columns)(
            sums, pots, state, kernel
        )
        sums = exchange(sums, "z")
        (sums,) = call(rider_next_body, [f32(RB, B)], [VM] * 3, [pltpu.VMEM((DB, B), F32)])(
            sums, state, kernel
        )
        sums = close(sums, jnp.add)
    rider_sums = sums
    (sums,) = call(driver_last_body, [f32(DB, 8, B)], [VM] * 4, columns)(
        rider_sums, pots, state, kernel
    )
    sums = exchange(sums, "z")
    rider_pot, driver_pot = call(
        finish_body, [f32(2, B), f32(1, B)], [VM] * 4, [pltpu.VMEM((RB, B), F32)]
    )(sums, state, rider_sums, pots)
    return rider_pot.reshape(2 * B), driver_pot.reshape(B)


def solution(mesh):
    fine = Mesh(mesh.devices.reshape(SIZES), AXES)
    row, every = ("z", "yl", "x"), AXES
    placed = (
        P(row, None),
        P(every, None),
        P(row),
        P(every),
        P(row),
        P(every),
        P(),
    )
    return jax.shard_map(
        per_device,
        mesh=fine,
        in_specs=placed,
        out_specs=(P(row), P(every)),
        check_vma=False,
    )
```

```python
import math

import jax
import jax.numpy as jnp
from jax import lax
from jax.experimental import pallas as pl
from jax.experimental.pallas import tpu as pltpu
from jax.sharding import Mesh, PartitionSpec as P

AXES = ("z", "yl", "x", "yh", "c")
SIZES = (8, 2, 4, 2, 2)
PLANE = ("yl", "x", "yh")
PEERS = 16

B = 128
RB = 16
DB = 8
PAY = B + 16
ITERS = 3
LOG_DRIVERS = math.log(32768)
LOG_RIDERS = math.log(16384)
PENALTY = 1e30
FLOOR = -1e29
TINY = 1e-37

F32 = jnp.float32
BF16 = jnp.bfloat16
VM = pl.BlockSpec(memory_space=pltpu.VMEM)
FAR = pl.BlockSpec(memory_space=pltpu.HBM)


def call(body, outs, ins, scratch=(), limit=20, cost=None):
    return pl.pallas_call(
        body,
        out_shape=outs,
        in_specs=ins,
        out_specs=[VM] * len(outs),
        cost_estimate=cost,
        scratch_shapes=list(scratch),
        compiler_params=pltpu.CompilerParams(vmem_limit_bytes=limit * 2**20),
    )


def f32(*shape):
    return jax.ShapeDtypeStruct(shape, F32)


def bf16(*shape):
    return jax.ShapeDtypeStruct(shape, BF16)


def product(left, right):
    return lax.dot_general(left, right, (((1,), (1,)), ((), ())), preferred_element_type=F32)


def tree(parts, op):
    while len(parts) > 1:
        parts = [op(parts[2 * k], parts[2 * k + 1]) for k in range(len(parts) // 2)]
    return parts[0]


def fold(block, op):
    return tree([block[8 * k : 8 * k + 8] for k in range(B // 8)], op)


def column(row):
    return jnp.broadcast_to(row, (B, B)).T


def three_parts(value):
    high = value.astype(BF16)
    rest = value - high.astype(F32)
    middle = rest.astype(BF16)
    return high, middle, (rest - middle.astype(F32)).astype(BF16)


def zone_rows(message):
    return jnp.broadcast_to(message[B : B + 1].astype(F32), (16, B)).astype(BF16)


def weight_row(message):
    tail = message[B:].astype(F32)
    return (tail[1:2] + tail[2:3]) + tail[3:4]


def with_zone(message, zone):
    return jnp.concatenate([message[:B], jnp.concatenate([zone] * (B // 16), axis=0)], axis=1)


def tail_rows(zone_row, log_row):
    row = lax.broadcasted_iota(jnp.int32, (16, B), 0)
    tail = jnp.where(row == 0, zone_row, 0.0)
    for k, part in enumerate(three_parts(log_row)):
        tail = jnp.where(row == k + 1, part.astype(F32), tail)
    return tail.astype(BF16)


def pack_body(rider, driver, log_a, log_b, rzone, dzone, table, rider_out, driver_out,
              a_row, b_row, rz, dz, tab, sems):
    c = lax.axis_index("c")
    copies = [
        pltpu.make_async_copy(rider.at[c], rider_out.at[0, pl.ds(0, B)], sems.at[0]),
        pltpu.make_async_copy(driver, driver_out.at[0, pl.ds(0, B)], sems.at[1]),
        pltpu.make_async_copy(log_a.at[pl.ds(c, 1)], a_row, sems.at[2]),
        pltpu.make_async_copy(log_b, b_row, sems.at[3]),
        pltpu.make_async_copy(rzone, rz, sems.at[4]),
        pltpu.make_async_copy(dzone, dz, sems.at[5]),
        pltpu.make_async_copy(table, tab, sems.at[6]),
    ]
    for copy in copies:
        copy.start()
    for copy in copies:
        copy.wait()
    lane = lax.broadcasted_iota(jnp.int32, (16, B), 1)
    hot = jnp.where(lane == rz[c], 1.0, 0.0)
    zone = dz[0]
    shut = jnp.zeros((16, B), F32)
    for k in range(16):
        shut = jnp.where((lane == k) & (tab[k, zone] != 1), PENALTY, shut)
    rider_out[0, B:, :] = tail_rows(hot, a_row[...])
    driver_out[0, B:, :] = tail_rows(shut, b_row[...])
    for k in range(1, DB):
        driver_out[k] = driver_out[0]


def place(far, slot):
    yl, x = lax.axis_index("yl"), lax.axis_index("x")
    x = x + slot // 2 * (3 - 2 * x)
    x = x + slot % 2 * (1 - 2 * (x % 2))
    return (yl + far * (1 - 2 * yl)) * 4 + x


def block_of(r):
    c = lax.axis_index("c")
    return 2 * place(r // 4 % 2, r % 4) + c + r // 8 * (1 - 2 * c)


def widen(messages, wide):
    for k, message in enumerate(messages):
        wide[k * B : (k + 1) * B] = with_zone(message, zone_rows(message))


def rider_rows(riders, drivers, cost, rows, first, left):
    widen([riders[k] for k in range(4)], left)
    for h in range(DB // 2):
        lanes = slice(2 * h * B, 2 * (h + 1) * B)
        cost[:, lanes] = product(left[...], drivers[lanes, :])
    for k in range(4):
        pieces = [cost[k * B : (k + 1) * B, j * B : (j + 1) * B] for j in range(DB)]
        low = tree(pieces, jnp.minimum)
        mass = tree([jnp.exp(low - piece) for piece in pieces], jnp.add).T
        low = low.T
        least = jnp.min(low, axis=0, keepdims=True)
        mass = jnp.sum(mass * jnp.exp(least - low), axis=0, keepdims=True)
        rows[first + k : first + k + 1, :] = jnp.log(mass) - least


def rider_near_body(near, driver, cost, rows, wide, left):
    widen([driver[z] for z in range(DB)], wide)
    rider_rows(near, wide, cost, rows, 0, left)


def rider_far_body(far, wide, cost, rows, left):
    rider_rows(far, wide, cost, rows, 0, left)


def rider_other_body(near, far, wide, own_near, own_far, near_cost, far_cost, out, rows, left):
    rows[0:4] = own_near[...]
    rows[4:8] = own_far[...]
    rider_rows(near, wide, near_cost, rows, 8, left)
    rider_rows(far, wide, far_cost, rows, 12, left)
    for r in range(RB):
        out[pl.ds(block_of(r), 1), :] = rows[r : r + 1]


def log_total(sums):
    parts = [sums[k] for k in range(sums.shape[0])]
    peak = tree(parts, jnp.maximum)
    return peak + jnp.log(tree([jnp.exp(part - peak) for part in parts], jnp.add))


def total_of(sums):
    return tree([sums[k] for k in range(sums.shape[0])], jnp.add)


def driver_first_body(sums, own_near, own_far, other_near, other_far, driver, *rest):
    *costs, out, kernel, peaks, pots, ucol = rest
    messages = (own_near, own_far, other_near, other_far)
    for r in range(RB):
        pots[pl.ds(RB + block_of(r), 1), :] = weight_row(messages[r // 4][r % 4])
    for j in range(DB):
        peaks[DB + j : DB + j + 1, :] = weight_row(driver[j])
    pots[0:RB] = pots[RB:] - (log_total(sums) - LOG_DRIVERS)
    for r in range(RB):
        ucol[r * B : (r + 1) * B, :] = column(pots[pl.ds(block_of(r), 1), :])

    def scores(r):
        u = ucol[r * B : (r + 1) * B, :]
        rows = slice(r % 4 * B, (r % 4 + 1) * B)
        return [u - costs[r // 4][rows, j * B : (j + 1) * B] for j in range(DB)]

    high = [jnp.full((8, B), FLOOR, F32)] * DB
    for r in range(RB):
        high = [jnp.maximum(h, fold(score, jnp.maximum)) for h, score in zip(high, scores(r))]
    top = [jnp.max(h, axis=0, keepdims=True) for h in high]
    total = [jnp.zeros((8, B), F32)] * DB
    for r in range(RB):
        for j, score in enumerate(scores(r)):
            term = jnp.exp(score - top[j])
            kernel[r * B : (r + 1) * B, j * B : (j + 1) * B] = term
            total[j] = total[j] + fold(term, jnp.add)
    for j in range(DB):
        mass = jnp.maximum(jnp.sum(total[j], axis=0, keepdims=True), TINY)
        peaks[j : j + 1] = top[j]
        out[0, j : j + 1] = top[j] + jnp.log(mass)
    for k in range(1, DB):
        out[k] = out[0]


def row_sums(kernel, scale, out):
    for r in range(RB):
        rows = slice(r * B, (r + 1) * B)
        acc = kernel[rows, 0:B] * scale[0:1]
        for k in range(1, DB):
            acc = acc + kernel[rows, k * B : (k + 1) * B] * scale[k : k + 1]
        out[pl.ds(block_of(r), 1), :] = jnp.sum(acc.T, axis=0, keepdims=True)


def column_sums(kernel, f, state, fcol, hold):
    hold[...] = f
    for r in range(RB):
        fcol[r * B : (r + 1) * B, :] = column(hold[pl.ds(block_of(r), 1), :])

    def block(r, acc):
        for k in range(B // 8):
            rows = pl.ds(pl.multiple_of(r * B + 8 * k, 8), 8)
            f = fcol[rows, :]
            acc = tuple(a + kernel[rows, j * B : (j + 1) * B] * f for j, a in enumerate(acc))
        return acc

    acc = lax.fori_loop(0, RB, block, tuple(jnp.zeros((8, B), F32) for _ in range(DB)))
    for j in range(DB):
        hold[j : j + 1, :] = jnp.sum(acc[j], axis=0, keepdims=True)
    return hold[0:DB] * state[2 * DB : 3 * DB]


def rider_second_body(sums, peaks, kernel, out, state):
    log_b = peaks[DB:]
    pot = log_b - (log_total(sums) - LOG_RIDERS)
    state[0:DB] = pot
    state[DB : 2 * DB] = log_b
    state[2 * DB :] = jnp.exp(pot + peaks[0:DB])
    row_sums(kernel, state.at[pl.ds(2 * DB, DB)], out)


def driver_next_body(sums, pots, state, kernel, out, fcol, hold):
    rows = column_sums(kernel, jnp.exp(pots[RB:] + LOG_DRIVERS) / total_of(sums), state, fcol, hold)
    for k in range(DB):
        out[k] = rows


def rider_next_body(sums, state, kernel, out, scale):
    scale[...] = state[2 * DB :] * (jnp.exp(state[DB : 2 * DB] + LOG_RIDERS) / total_of(sums))
    row_sums(kernel, scale, out)


def driver_last_body(sums, pots, state, kernel, out, fcol, hold):
    f = jnp.exp(pots[RB:] + LOG_DRIVERS) / total_of(sums)
    rows = column_sums(kernel, f, state, fcol, hold)
    for k in range(DB):
        out[k] = jnp.broadcast_to(rows[k : k + 1], (8, B))


def finish_body(sums, state, rider_sums, pots, rider_pot, driver_pot, hold):
    z = lax.axis_index("z")
    pot = state[pl.ds(z, 1), :]
    log_b = state[pl.ds(DB + z, 1), :]
    driver_pot[...] = pot + (log_b + LOG_RIDERS - jnp.log(total_of(sums)[0:1]))
    hold[...] = pots[0:RB] + (pots[RB:] + LOG_DRIVERS - jnp.log(total_of(rider_sums)))
    block = lax.axis_index("yl") * 4 + lax.axis_index("x")
    rider_pot[0:1] = hold[pl.ds(2 * block, 1), :]
    rider_pot[1:2] = hold[pl.ds(2 * block + 1, 1), :]


def exchange(message, axes):
    return lax.all_to_all(message, axes, 0, 0, tiled=True)


def swap(value, axis, partner):
    return lax.ppermute(value, axis, [(k, partner(k)) for k in range(SIZES[AXES.index(axis)])])


def from_y(value, step):
    place_of = lambda y: y % 2 * 2 + y // 2
    return lax.ppermute(
        value, ("yl", "yh"), [(place_of(y), place_of((y - step) % 4)) for y in range(4)]
    )


def log_add(a, b):
    peak = jnp.maximum(a, b)
    return peak + jnp.log(jnp.exp(a - peak) + jnp.exp(b - peak))


def close(value, op):
    value = op(value, swap(value, "c", lambda k: 1 - k))
    return exchange(jnp.broadcast_to(value[None], (PEERS, RB, B)), PLANE)


def rider_first(message, drivers):
    two = jnp.concatenate([message, swap(message, "x", lambda k: k ^ 1)], axis=0)
    two, drivers = lax.optimization_barrier((two, drivers))
    drivers = exchange(drivers, "z")
    mirror = swap(two, "x", lambda k: 3 - k)
    near = jnp.concatenate([two, mirror], axis=0)
    far = jnp.concatenate([from_y(two, 1), from_y(mirror, -1)], axis=0)
    quarter = pl.CostEstimate(flops=2**30, transcendentals=2**19, bytes_accessed=2**21)
    cost, rows, left = f32(4 * B, DB * B), f32(4, B), pltpu.VMEM((4 * B, 2 * B), BF16)
    own_near_cost, near_rows, wide = call(
        rider_near_body, [cost, rows, bf16(DB * B, 2 * B)], [VM] * 2, [left], cost=quarter
    )(near, drivers)
    near, far, near_rows = lax.optimization_barrier((near, far, near_rows))
    other_near, other_far = (swap(value, "c", lambda k: 1 - k) for value in (near, far))
    own_far_cost, far_rows = call(rider_far_body, [cost, rows], [VM] * 2, [left], cost=quarter)(far, wide)
    other_near_cost, other_far_cost, sums = call(
        rider_other_body, [cost, cost, f32(RB, B)], [VM] * 5, [pltpu.VMEM((RB, B), F32), left]
    )(other_near, other_far, wide, near_rows, far_rows)
    costs = own_near_cost, own_far_cost, other_near_cost, other_far_cost
    return sums, (near, far, other_near, other_far, drivers, *costs)


def per_device(rider_emb, driver_emb, log_a, log_b, rider_zone, driver_zone, zone_table):
    rider_msg, driver_msg = call(
        pack_body,
        [pltpu.VMEM((1, PAY, B), BF16), pltpu.VMEM((DB, PAY, B), BF16)],
        [FAR] * 7,
        [
            pltpu.VMEM((1, B), F32),
            pltpu.VMEM((1, B), F32),
            pltpu.SMEM((2,), jnp.int32),
            pltpu.SMEM((1,), jnp.int32),
            pltpu.SMEM((16, 16), jnp.int32),
            pltpu.SemaphoreType.DMA((7,)),
        ],
        limit=60,
    )(
        rider_emb.reshape(2, B, B), driver_emb, log_a.reshape(2, B), log_b.reshape(1, B),
        rider_zone, driver_zone, zone_table,
    )
    sums, gathered = rider_first(rider_msg, driver_msg)
    sums = close(sums, log_add)
    columns = pltpu.VMEM((RB * B, B), F32)
    sums, kernel, peaks, pots = call(
        driver_first_body,
        [f32(DB, DB, B), f32(RB * B, DB * B), f32(2 * DB, B), f32(2 * RB, B)],
        [VM] * 10,
        [columns],
    )(sums, *gathered)
    sums = exchange(sums, "z")
    columns = [columns, pltpu.VMEM((RB, B), F32)]
    sums, state = call(rider_second_body, [f32(RB, B), f32(3 * DB, B)], [VM] * 3)(
        sums, peaks, kernel
    )
    sums = close(sums, jnp.add)
    for _ in range(ITERS - 2):
        (sums,) = call(driver_next_body, [f32(DB, DB, B)], [VM] * 4, columns)(
            sums, pots, state, kernel
        )
        sums = exchange(sums, "z")
        (sums,) = call(rider_next_body, [f32(RB, B)], [VM] * 3, [pltpu.VMEM((DB, B), F32)])(
            sums, state, kernel
        )
        sums = close(sums, jnp.add)
    rider_sums = sums
    (sums,) = call(driver_last_body, [f32(DB, 8, B)], [VM] * 4, columns)(
        rider_sums, pots, state, kernel
    )
    sums = exchange(sums, "z")
    rider_pot, driver_pot = call(
        finish_body, [f32(2, B), f32(1, B)], [VM] * 4, [pltpu.VMEM((RB, B), F32)]
    )(sums, state, rider_sums, pots)
    return rider_pot.reshape(2 * B), driver_pot.reshape(B)


def solution(mesh):
    fine = Mesh(mesh.devices.reshape(SIZES), AXES)
    row, every = ("z", "yl", "x"), AXES
    placed = (
        P(row, None),
        P(every, None),
        P(row),
        P(every),
        P(row),
        P(every),
        P(),
    )
    return jax.shard_map(
        per_device,
        mesh=fine,
        in_specs=placed,
        out_specs=(P(row), P(every)),
        check_vma=False,
    )
```

```python
import math

import jax
import jax.numpy as jnp
from jax import lax
from jax.experimental import pallas as pl
from jax.experimental.pallas import tpu as pltpu
from jax.sharding import Mesh, PartitionSpec as P

AXES = ("z", "yl", "x", "yh", "c")
SIZES = (8, 2, 4, 2, 2)
PLANE = ("yl", "x", "yh")
PEERS = 16

B = 128
RB = 16
DB = 8
PAY = B + 16
ITERS = 3
LOG_DRIVERS = math.log(32768)
LOG_RIDERS = math.log(16384)
PENALTY = 1e30
FLOOR = -1e29
TINY = 1e-37

F32 = jnp.float32
BF16 = jnp.bfloat16
VM = pl.BlockSpec(memory_space=pltpu.VMEM)
FAR = pl.BlockSpec(memory_space=pltpu.HBM)


def call(body, outs, ins, scratch=(), limit=20, cost=None):
    return pl.pallas_call(
        body,
        out_shape=outs,
        in_specs=ins,
        out_specs=[VM] * len(outs),
        cost_estimate=cost,
        scratch_shapes=list(scratch),
        compiler_params=pltpu.CompilerParams(vmem_limit_bytes=limit * 2**20),
    )


def f32(*shape):
    return jax.ShapeDtypeStruct(shape, F32)


def bf16(*shape):
    return jax.ShapeDtypeStruct(shape, BF16)


def product(left, right):
    return lax.dot_general(left, right, (((1,), (1,)), ((), ())), preferred_element_type=F32)


def tree(parts, op):
    while len(parts) > 1:
        parts = [op(parts[2 * k], parts[2 * k + 1]) for k in range(len(parts) // 2)]
    return parts[0]


def fold(block, op):
    return tree([block[8 * k : 8 * k + 8] for k in range(B // 8)], op)


def column(row):
    return jnp.broadcast_to(row, (B, B)).T


def three_parts(value):
    high = value.astype(BF16)
    rest = value - high.astype(F32)
    middle = rest.astype(BF16)
    return high, middle, (rest - middle.astype(F32)).astype(BF16)


def zone_rows(message):
    return jnp.broadcast_to(message[B : B + 1].astype(F32), (16, B)).astype(BF16)


def weight_row(message):
    tail = message[B:].astype(F32)
    return (tail[1:2] + tail[2:3]) + tail[3:4]


def with_zone(message, zone):
    return jnp.concatenate([message[:B], jnp.concatenate([zone] * (B // 16), axis=0)], axis=1)


def tail_rows(zone_row, log_row):
    row = lax.broadcasted_iota(jnp.int32, (16, B), 0)
    tail = jnp.where(row == 0, zone_row, 0.0)
    for k, part in enumerate(three_parts(log_row)):
        tail = jnp.where(row == k + 1, part.astype(F32), tail)
    return tail.astype(BF16)


def pack_body(rider, driver, log_a, log_b, rzone, dzone, table, rider_out, driver_out,
              a_row, b_row, rz, dz, tab, sems):
    c = lax.axis_index("c")
    copies = [
        pltpu.make_async_copy(rider.at[c], rider_out.at[0, pl.ds(0, B)], sems.at[0]),
        pltpu.make_async_copy(driver, driver_out.at[0, pl.ds(0, B)], sems.at[1]),
        pltpu.make_async_copy(log_a.at[pl.ds(c, 1)], a_row, sems.at[2]),
        pltpu.make_async_copy(log_b, b_row, sems.at[3]),
        pltpu.make_async_copy(rzone, rz, sems.at[4]),
        pltpu.make_async_copy(dzone, dz, sems.at[5]),
        pltpu.make_async_copy(table, tab, sems.at[6]),
    ]
    for copy in copies:
        copy.start()
    for copy in copies:
        copy.wait()
    lane = lax.broadcasted_iota(jnp.int32, (16, B), 1)
    hot = jnp.where(lane == rz[c], 1.0, 0.0)
    zone = dz[0]
    shut = jnp.zeros((16, B), F32)
    for k in range(16):
        shut = jnp.where((lane == k) & (tab[k, zone] != 1), PENALTY, shut)
    rider_out[0, B:, :] = tail_rows(hot, a_row[...])
    driver_out[0, B:, :] = tail_rows(shut, b_row[...])
    for k in range(1, DB):
        driver_out[k] = driver_out[0]


def place(far, slot):
    yl, x = lax.axis_index("yl"), lax.axis_index("x")
    x = x + slot // 2 * (3 - 2 * x)
    x = x + slot % 2 * (1 - 2 * (x % 2))
    return (yl + far * (1 - 2 * yl)) * 4 + x


def block_of(r):
    c = lax.axis_index("c")
    return 2 * place(r // 4 % 2, r % 4) + c + r // 8 * (1 - 2 * c)


def widen(messages, wide):
    for k, message in enumerate(messages):
        wide[k * B : (k + 1) * B] = with_zone(message, zone_rows(message))


def rider_rows(riders, drivers, cost, rows, first, left):
    widen([riders[k] for k in range(4)], left)
    for h in range(DB // 2):
        lanes = slice(2 * h * B, 2 * (h + 1) * B)
        cost[:, lanes] = product(left[...], drivers[lanes, :])
    for k in range(4):
        pieces = [cost[k * B : (k + 1) * B, j * B : (j + 1) * B] for j in range(DB)]
        low = tree(pieces, jnp.minimum)
        mass = tree([jnp.exp(low - piece) for piece in pieces], jnp.add).T
        low = low.T
        least = jnp.min(low, axis=0, keepdims=True)
        mass = jnp.sum(mass * jnp.exp(least - low), axis=0, keepdims=True)
        rows[first + k : first + k + 1, :] = jnp.log(mass) - least


def rider_near_body(near, driver, cost, rows, wide, left):
    widen([driver[z] for z in range(DB)], wide)
    rider_rows(near, wide, cost, rows, 0, left)


def rider_far_body(far, wide, cost, rows, left):
    rider_rows(far, wide, cost, rows, 0, left)


def rider_other_body(near, far, wide, own_near, own_far, near_cost, far_cost, out, rows, left):
    rows[0:4] = own_near[...]
    rows[4:8] = own_far[...]
    rider_rows(near, wide, near_cost, rows, 8, left)
    rider_rows(far, wide, far_cost, rows, 12, left)
    for r in range(RB):
        out[pl.ds(block_of(r), 1), :] = rows[r : r + 1]


def log_total(sums):
    parts = [sums[k] for k in range(sums.shape[0])]
    peak = tree(parts, jnp.maximum)
    return peak + jnp.log(tree([jnp.exp(part - peak) for part in parts], jnp.add))


def total_of(sums):
    return tree([sums[k] for k in range(sums.shape[0])], jnp.add)


def driver_first_body(sums, own_near, own_far, other_near, other_far, driver, *rest):
    *costs, out, kernel, peaks, pots, ucol = rest
    messages = (own_near, own_far, other_near, other_far)
    for r in range(RB):
        pots[pl.ds(RB + block_of(r), 1), :] = weight_row(messages[r // 4][r % 4])
    for j in range(DB):
        peaks[DB + j : DB + j + 1, :] = weight_row(driver[j])
    pots[0:RB] = pots[RB:] - (log_total(sums) - LOG_DRIVERS)
    for r in range(RB):
        ucol[r * B : (r + 1) * B, :] = column(pots[pl.ds(block_of(r), 1), :])

    def scores(r):
        u = ucol[r * B : (r + 1) * B, :]
        rows = slice(r % 4 * B, (r % 4 + 1) * B)
        return [u - costs[r // 4][rows, j * B : (j + 1) * B] for j in range(DB)]

    high = [jnp.full((8, B), FLOOR, F32)] * DB
    for r in range(RB):
        high = [jnp.maximum(h, fold(score, jnp.maximum)) for h, score in zip(high, scores(r))]
    top = [jnp.max(h, axis=0, keepdims=True) for h in high]
    total = [jnp.zeros((8, B), F32)] * DB
    for r in range(RB):
        for j, score in enumerate(scores(r)):
            term = jnp.exp(score - top[j])
            kernel[r * B : (r + 1) * B, j * B : (j + 1) * B] = term
            total[j] = total[j] + fold(term, jnp.add)
    for j in range(DB):
        mass = jnp.maximum(jnp.sum(total[j], axis=0, keepdims=True), TINY)
        peaks[j : j + 1] = top[j]
        out[0, j : j + 1] = top[j] + jnp.log(mass)
    for k in range(1, DB):
        out[k] = out[0]


def row_sums(kernel, scale, out):
    for r in range(RB):
        rows = slice(r * B, (r + 1) * B)
        acc = kernel[rows, 0:B] * scale[0:1]
        for k in range(1, DB):
            acc = acc + kernel[rows, k * B : (k + 1) * B] * scale[k : k + 1]
        out[pl.ds(block_of(r), 1), :] = jnp.sum(acc.T, axis=0, keepdims=True)


def column_sums(kernel, f, state, fcol, hold):
    hold[...] = f
    for r in range(RB):
        fcol[r * B : (r + 1) * B, :] = column(hold[pl.ds(block_of(r), 1), :])

    def block(r, acc):
        for k in range(B // 8):
            rows = pl.ds(pl.multiple_of(r * B + 8 * k, 8), 8)
            f = fcol[rows, :]
            acc = tuple(a + kernel[rows, j * B : (j + 1) * B] * f for j, a in enumerate(acc))
        return acc

    acc = lax.fori_loop(0, RB, block, tuple(jnp.zeros((8, B), F32) for _ in range(DB)))
    for j in range(DB):
        hold[j : j + 1, :] = jnp.sum(acc[j], axis=0, keepdims=True)
    return hold[0:DB] * state[2 * DB : 3 * DB]


def rider_second_body(sums, peaks, kernel, out, state):
    log_b = peaks[DB:]
    pot = log_b - (log_total(sums) - LOG_RIDERS)
    state[0:DB] = pot
    state[DB : 2 * DB] = log_b
    state[2 * DB :] = jnp.exp(pot + peaks[0:DB])
    row_sums(kernel, state.at[pl.ds(2 * DB, DB)], out)


def driver_next_body(sums, pots, state, kernel, out, fcol, hold):
    rows = column_sums(kernel, jnp.exp(pots[RB:] + LOG_DRIVERS) / total_of(sums), state, fcol, hold)
    for k in range(DB):
        out[k] = rows


def rider_next_body(sums, state, kernel, out, scale):
    scale[...] = state[2 * DB :] * (jnp.exp(state[DB : 2 * DB] + LOG_RIDERS) / total_of(sums))
    row_sums(kernel, scale, out)


def driver_last_body(sums, pots, state, kernel, out, fcol, hold):
    f = jnp.exp(pots[RB:] + LOG_DRIVERS) / total_of(sums)
    rows = column_sums(kernel, f, state, fcol, hold)
    for k in range(DB):
        out[k] = jnp.broadcast_to(rows[k : k + 1], (8, B))


def finish_body(sums, state, rider_sums, pots, rider_pot, driver_pot, hold):
    z = lax.axis_index("z")
    pot = state[pl.ds(z, 1), :]
    log_b = state[pl.ds(DB + z, 1), :]
    driver_pot[...] = pot + (log_b + LOG_RIDERS - jnp.log(total_of(sums)[0:1]))
    hold[...] = pots[0:RB] + (pots[RB:] + LOG_DRIVERS - jnp.log(total_of(rider_sums)))
    block = lax.axis_index("yl") * 4 + lax.axis_index("x")
    rider_pot[0:1] = hold[pl.ds(2 * block, 1), :]
    rider_pot[1:2] = hold[pl.ds(2 * block + 1, 1), :]


def exchange(message, axes):
    return lax.all_to_all(message, axes, 0, 0, tiled=True)


def swap(value, axis, partner):
    return lax.ppermute(value, axis, [(k, partner(k)) for k in range(SIZES[AXES.index(axis)])])


def from_y(value, step):
    place_of = lambda y: y % 2 * 2 + y // 2
    return lax.ppermute(
        value, ("yl", "yh"), [(place_of(y), place_of((y - step) % 4)) for y in range(4)]
    )


def log_add(a, b):
    peak = jnp.maximum(a, b)
    return peak + jnp.log(jnp.exp(a - peak) + jnp.exp(b - peak))


def close(value, op):
    value = op(value, swap(value, "c", lambda k: 1 - k))
    return exchange(jnp.broadcast_to(value[None], (PEERS, RB, B)), PLANE)


def rider_first(message, drivers):
    two = jnp.concatenate([message, swap(message, "x", lambda k: k ^ 1)], axis=0)
    drivers = exchange(drivers, "z")
    mirror = swap(two, "x", lambda k: 3 - k)
    near = jnp.concatenate([two, mirror], axis=0)
    far = jnp.concatenate([from_y(two, 1), from_y(mirror, -1)], axis=0)
    quarter = pl.CostEstimate(flops=2**30, transcendentals=2**19, bytes_accessed=2**21)
    cost, rows, left = f32(4 * B, DB * B), f32(4, B), pltpu.VMEM((4 * B, 2 * B), BF16)
    own_near_cost, near_rows, wide = call(
        rider_near_body, [cost, rows, bf16(DB * B, 2 * B)], [VM] * 2, [left], cost=quarter
    )(near, drivers)
    near, far, near_rows = lax.optimization_barrier((near, far, near_rows))
    other_near, other_far = (swap(value, "c", lambda k: 1 - k) for value in (near, far))
    own_far_cost, far_rows = call(rider_far_body, [cost, rows], [VM] * 2, [left], cost=quarter)(far, wide)
    other_near_cost, other_far_cost, sums = call(
        rider_other_body, [cost, cost, f32(RB, B)], [VM] * 5, [pltpu.VMEM((RB, B), F32), left]
    )(other_near, other_far, wide, near_rows, far_rows)
    costs = own_near_cost, own_far_cost, other_near_cost, other_far_cost
    return sums, (near, far, other_near, other_far, drivers, *costs)


def per_device(rider_emb, driver_emb, log_a, log_b, rider_zone, driver_zone, zone_table):
    rider_msg, driver_msg = call(
        pack_body,
        [pltpu.VMEM((1, PAY, B), BF16), pltpu.VMEM((DB, PAY, B), BF16)],
        [FAR] * 7,
        [
            pltpu.VMEM((1, B), F32),
            pltpu.VMEM((1, B), F32),
            pltpu.SMEM((2,), jnp.int32),
            pltpu.SMEM((1,), jnp.int32),
            pltpu.SMEM((16, 16), jnp.int32),
            pltpu.SemaphoreType.DMA((7,)),
        ],
        limit=60,
    )(
        rider_emb.reshape(2, B, B), driver_emb, log_a.reshape(2, B), log_b.reshape(1, B),
        rider_zone, driver_zone, zone_table,
    )
    sums, gathered = rider_first(rider_msg, driver_msg)
    sums = close(sums, log_add)
    columns = pltpu.VMEM((RB * B, B), F32)
    sums, kernel, peaks, pots = call(
        driver_first_body,
        [f32(DB, DB, B), f32(RB * B, DB * B), f32(2 * DB, B), f32(2 * RB, B)],
        [VM] * 10,
        [columns],
    )(sums, *gathered)
    sums = exchange(sums, "z")
    columns = [columns, pltpu.VMEM((RB, B), F32)]
    sums, state = call(rider_second_body, [f32(RB, B), f32(3 * DB, B)], [VM] * 3)(
        sums, peaks, kernel
    )
    sums = close(sums, jnp.add)
    for _ in range(ITERS - 2):
        (sums,) = call(driver_next_body, [f32(DB, DB, B)], [VM] * 4, columns)(
            sums, pots, state, kernel
        )
        sums = exchange(sums, "z")
        (sums,) = call(rider_next_body, [f32(RB, B)], [VM] * 3, [pltpu.VMEM((DB, B), F32)])(
            sums, state, kernel
        )
        sums = close(sums, jnp.add)
    rider_sums = sums
    (sums,) = call(driver_last_body, [f32(DB, 8, B)], [VM] * 4, columns)(
        rider_sums, pots, state, kernel
    )
    sums = exchange(sums, "z")
    rider_pot, driver_pot = call(
        finish_body, [f32(2, B), f32(1, B)], [VM] * 4, [pltpu.VMEM((RB, B), F32)]
    )(sums, state, rider_sums, pots)
    return rider_pot.reshape(2 * B), driver_pot.reshape(B)


def solution(mesh):
    fine = Mesh(mesh.devices.reshape(SIZES), AXES)
    row, every = ("z", "yl", "x"), AXES
    placed = (
        P(row, None),
        P(every, None),
        P(row),
        P(every),
        P(row),
        P(every),
        P(),
    )
    return jax.shard_map(
        per_device,
        mesh=fine,
        in_specs=placed,
        out_specs=(P(row), P(every)),
        check_vma=False,
    )
```

```python
import math

import jax
import jax.numpy as jnp
from jax import lax
from jax.experimental import pallas as pl
from jax.experimental.pallas import tpu as pltpu
from jax.sharding import Mesh, PartitionSpec as P

AXES = ("z", "yl", "x", "yh", "c")
SIZES = (8, 2, 4, 2, 2)
PLANE = ("yl", "x", "yh")
PEERS = 16

B = 128
RB = 16
DB = 8
PAY = B + 16
ITERS = 3
LOG_DRIVERS = math.log(32768)
LOG_RIDERS = math.log(16384)
PENALTY = 1e30
FLOOR = -1e29
TINY = 1e-37

F32 = jnp.float32
BF16 = jnp.bfloat16
VM = pl.BlockSpec(memory_space=pltpu.VMEM)
FAR = pl.BlockSpec(memory_space=pltpu.HBM)


def call(body, outs, ins, scratch=(), limit=20, cost=None):
    return pl.pallas_call(
        body,
        out_shape=outs,
        in_specs=ins,
        out_specs=[VM] * len(outs),
        cost_estimate=cost,
        scratch_shapes=list(scratch),
        compiler_params=pltpu.CompilerParams(vmem_limit_bytes=limit * 2**20),
    )


def f32(*shape):
    return jax.ShapeDtypeStruct(shape, F32)


def bf16(*shape):
    return jax.ShapeDtypeStruct(shape, BF16)


def product(left, right):
    return lax.dot_general(left, right, (((1,), (1,)), ((), ())), preferred_element_type=F32)


def tree(parts, op):
    while len(parts) > 1:
        parts = [op(parts[2 * k], parts[2 * k + 1]) for k in range(len(parts) // 2)]
    return parts[0]


def fold(block, op):
    return tree([block[8 * k : 8 * k + 8] for k in range(B // 8)], op)


def column(row):
    return jnp.broadcast_to(row, (B, B)).T


def three_parts(value):
    high = value.astype(BF16)
    rest = value - high.astype(F32)
    middle = rest.astype(BF16)
    return high, middle, (rest - middle.astype(F32)).astype(BF16)


def zone_rows(message):
    return jnp.broadcast_to(message[B : B + 1].astype(F32), (16, B)).astype(BF16)


def weight_row(message):
    tail = message[B:].astype(F32)
    return (tail[1:2] + tail[2:3]) + tail[3:4]


def with_zone(message, zone):
    return jnp.concatenate([message[:B], jnp.concatenate([zone] * (B // 16), axis=0)], axis=1)


def tail_rows(zone_row, log_row):
    row = lax.broadcasted_iota(jnp.int32, (16, B), 0)
    tail = jnp.where(row == 0, zone_row, 0.0)
    for k, part in enumerate(three_parts(log_row)):
        tail = jnp.where(row == k + 1, part.astype(F32), tail)
    return tail.astype(BF16)


def pack_body(rider, driver, log_a, log_b, rzone, dzone, table, rider_out, driver_out,
              a_row, b_row, rz, dz, tab, sems):
    c = lax.axis_index("c")
    copies = [
        pltpu.make_async_copy(rider.at[c], rider_out.at[0, pl.ds(0, B)], sems.at[0]),
        pltpu.make_async_copy(driver, driver_out.at[0, pl.ds(0, B)], sems.at[1]),
        pltpu.make_async_copy(log_a.at[pl.ds(c, 1)], a_row, sems.at[2]),
        pltpu.make_async_copy(log_b, b_row, sems.at[3]),
        pltpu.make_async_copy(rzone, rz, sems.at[4]),
        pltpu.make_async_copy(dzone, dz, sems.at[5]),
        pltpu.make_async_copy(table, tab, sems.at[6]),
    ]
    for copy in copies:
        copy.start()
    for copy in copies:
        copy.wait()
    lane = lax.broadcasted_iota(jnp.int32, (16, B), 1)
    hot = jnp.where(lane == rz[c], 1.0, 0.0)
    zone = dz[0]
    shut = jnp.zeros((16, B), F32)
    for k in range(16):
        shut = jnp.where((lane == k) & (tab[k, zone] != 1), PENALTY, shut)
    rider_out[0, B:, :] = tail_rows(hot, a_row[...])
    driver_out[0, B:, :] = tail_rows(shut, b_row[...])
    for k in range(1, DB):
        driver_out[k] = driver_out[0]


def place(far, slot):
    yl, x = lax.axis_index("yl"), lax.axis_index("x")
    x = x + slot // 2 * (3 - 2 * x)
    x = x + slot % 2 * (1 - 2 * (x % 2))
    return (yl + far * (1 - 2 * yl)) * 4 + x


def block_of(r):
    c = lax.axis_index("c")
    return 2 * place(r // 4 % 2, r % 4) + c + r // 8 * (1 - 2 * c)


def widen(messages, wide):
    for k, message in enumerate(messages):
        wide[k * B : (k + 1) * B] = with_zone(message, zone_rows(message))


def rider_rows(riders, drivers, cost, rows, first, left):
    widen([riders[k] for k in range(4)], left)
    for h in range(DB // 2):
        lanes = slice(2 * h * B, 2 * (h + 1) * B)
        cost[:, lanes] = product(left[...], drivers[lanes, :])
    for k in range(4):
        pieces = [cost[k * B : (k + 1) * B, j * B : (j + 1) * B] for j in range(DB)]
        low = tree(pieces, jnp.minimum)
        mass = tree([jnp.exp(low - piece) for piece in pieces], jnp.add).T
        low = low.T
        least = jnp.min(low, axis=0, keepdims=True)
        mass = jnp.sum(mass * jnp.exp(least - low), axis=0, keepdims=True)
        rows[first + k : first + k + 1, :] = jnp.log(mass) - least


def rider_near_body(near, driver, cost, rows, wide, left):
    widen([driver[z] for z in range(DB)], wide)
    rider_rows(near, wide, cost, rows, 0, left)


def rider_far_body(far, wide, cost, rows, left):
    rider_rows(far, wide, cost, rows, 0, left)


def rider_other_body(near, far, wide, own_near, own_far, near_cost, far_cost, out, rows, left):
    rows[0:4] = own_near[...]
    rows[4:8] = own_far[...]
    rider_rows(near, wide, near_cost, rows, 8, left)
    rider_rows(far, wide, far_cost, rows, 12, left)
    for r in range(RB):
        out[pl.ds(block_of(r), 1), :] = rows[r : r + 1]


def log_total(sums):
    parts = [sums[k] for k in range(sums.shape[0])]
    peak = tree(parts, jnp.maximum)
    return peak + jnp.log(tree([jnp.exp(part - peak) for part in parts], jnp.add))


def total_of(sums):
    return tree([sums[k] for k in range(sums.shape[0])], jnp.add)


def driver_first_body(sums, own_near, own_far, other_near, other_far, driver, *rest):
    *costs, out, kernel, peaks, pots, ucol = rest
    messages = (own_near, own_far, other_near, other_far)
    for r in range(RB):
        pots[pl.ds(RB + block_of(r), 1), :] = weight_row(messages[r // 4][r % 4])
    for j in range(DB):
        peaks[DB + j : DB + j + 1, :] = weight_row(driver[j])
    pots[0:RB] = pots[RB:] - (log_total(sums) - LOG_DRIVERS)
    for r in range(RB):
        ucol[r * B : (r + 1) * B, :] = column(pots[pl.ds(block_of(r), 1), :])

    def scores(r):
        u = ucol[r * B : (r + 1) * B, :]
        rows = slice(r % 4 * B, (r % 4 + 1) * B)
        return [u - costs[r // 4][rows, j * B : (j + 1) * B] for j in range(DB)]

    high = [jnp.full((8, B), FLOOR, F32)] * DB
    for r in range(RB):
        high = [jnp.maximum(h, fold(score, jnp.maximum)) for h, score in zip(high, scores(r))]
    top = [jnp.max(h, axis=0, keepdims=True) for h in high]
    total = [jnp.zeros((8, B), F32)] * DB
    for r in range(RB):
        for j, score in enumerate(scores(r)):
            term = jnp.exp(score - top[j])
            kernel[r * B : (r + 1) * B, j * B : (j + 1) * B] = term
            total[j] = total[j] + fold(term, jnp.add)
    for j in range(DB):
        mass = jnp.maximum(jnp.sum(total[j], axis=0, keepdims=True), TINY)
        peaks[j : j + 1] = top[j]
        out[0, j : j + 1] = top[j] + jnp.log(mass)
    for k in range(1, DB):
        out[k] = out[0]


def row_sums(kernel, scale, out):
    for r in range(RB):
        rows = slice(r * B, (r + 1) * B)
        acc = kernel[rows, 0:B] * scale[0:1]
        for k in range(1, DB):
            acc = acc + kernel[rows, k * B : (k + 1) * B] * scale[k : k + 1]
        out[pl.ds(block_of(r), 1), :] = jnp.sum(acc.T, axis=0, keepdims=True)


def column_sums(kernel, f, state, fcol, hold):
    hold[...] = f
    for r in range(RB):
        fcol[r * B : (r + 1) * B, :] = column(hold[pl.ds(block_of(r), 1), :])

    def block(r, acc):
        for k in range(B // 8):
            rows = pl.ds(pl.multiple_of(r * B + 8 * k, 8), 8)
            f = fcol[rows, :]
            acc = tuple(a + kernel[rows, j * B : (j + 1) * B] * f for j, a in enumerate(acc))
        return acc

    acc = lax.fori_loop(0, RB, block, tuple(jnp.zeros((8, B), F32) for _ in range(DB)))
    for j in range(DB):
        hold[j : j + 1, :] = jnp.sum(acc[j], axis=0, keepdims=True)
    return hold[0:DB] * state[2 * DB : 3 * DB]


def rider_second_body(sums, peaks, kernel, out, state):
    log_b = peaks[DB:]
    pot = log_b - (log_total(sums) - LOG_RIDERS)
    state[0:DB] = pot
    state[DB : 2 * DB] = log_b
    state[2 * DB :] = jnp.exp(pot + peaks[0:DB])
    row_sums(kernel, state.at[pl.ds(2 * DB, DB)], out)


def driver_next_body(sums, pots, state, kernel, out, fcol, hold):
    rows = column_sums(kernel, jnp.exp(pots[RB:] + LOG_DRIVERS) / total_of(sums), state, fcol, hold)
    for k in range(DB):
        out[k] = rows


def rider_next_body(sums, state, kernel, out, scale):
    scale[...] = state[2 * DB :] * (jnp.exp(state[DB : 2 * DB] + LOG_RIDERS) / total_of(sums))
    row_sums(kernel, scale, out)


def driver_last_body(sums, pots, state, kernel, out, fcol, hold):
    f = jnp.exp(pots[RB:] + LOG_DRIVERS) / total_of(sums)
    rows = column_sums(kernel, f, state, fcol, hold)
    for k in range(DB):
        out[k] = jnp.broadcast_to(rows[k : k + 1], (8, B))


def finish_body(sums, state, rider_sums, pots, rider_pot, driver_pot, hold):
    z = lax.axis_index("z")
    pot = state[pl.ds(z, 1), :]
    log_b = state[pl.ds(DB + z, 1), :]
    driver_pot[...] = pot + (log_b + LOG_RIDERS - jnp.log(total_of(sums)[0:1]))
    hold[...] = pots[0:RB] + (pots[RB:] + LOG_DRIVERS - jnp.log(total_of(rider_sums)))
    block = lax.axis_index("yl") * 4 + lax.axis_index("x")
    rider_pot[0:1] = hold[pl.ds(2 * block, 1), :]
    rider_pot[1:2] = hold[pl.ds(2 * block + 1, 1), :]


def exchange(message, axes):
    return lax.all_to_all(message, axes, 0, 0, tiled=True)


def swap(value, axis, partner):
    return lax.ppermute(value, axis, [(k, partner(k)) for k in range(SIZES[AXES.index(axis)])])


def from_y(value, step):
    place_of = lambda y: y % 2 * 2 + y // 2
    return lax.ppermute(
        value, ("yl", "yh"), [(place_of(y), place_of((y - step) % 4)) for y in range(4)]
    )


def log_add(a, b):
    peak = jnp.maximum(a, b)
    return peak + jnp.log(jnp.exp(a - peak) + jnp.exp(b - peak))


def close(value, op):
    value = op(value, swap(value, "c", lambda k: 1 - k))
    return exchange(jnp.broadcast_to(value[None], (PEERS, RB, B)), PLANE)


def rider_first(message, drivers):
    beside, across, behind = (
        swap(message, "x", partner)
        for partner in (lambda k: k ^ 1, lambda k: 3 - k, lambda k: k ^ 2)
    )
    two = jnp.concatenate([message, beside], axis=0)
    drivers = exchange(drivers, "z")
    mirror = jnp.concatenate([across, behind], axis=0)
    near = jnp.concatenate([two, mirror], axis=0)
    far = jnp.concatenate([from_y(two, 1), from_y(mirror, -1)], axis=0)
    quarter = pl.CostEstimate(flops=2**30, transcendentals=2**19, bytes_accessed=2**21)
    cost, rows, left = f32(4 * B, DB * B), f32(4, B), pltpu.VMEM((4 * B, 2 * B), BF16)
    own_near_cost, near_rows, wide = call(
        rider_near_body, [cost, rows, bf16(DB * B, 2 * B)], [VM] * 2, [left], cost=quarter
    )(near, drivers)
    near, far, near_rows = lax.optimization_barrier((near, far, near_rows))
    other_near, other_far = (swap(value, "c", lambda k: 1 - k) for value in (near, far))
    own_far_cost, far_rows = call(rider_far_body, [cost, rows], [VM] * 2, [left], cost=quarter)(far, wide)
    other_near_cost, other_far_cost, sums = call(
        rider_other_body, [cost, cost, f32(RB, B)], [VM] * 5, [pltpu.VMEM((RB, B), F32), left]
    )(other_near, other_far, wide, near_rows, far_rows)
    costs = own_near_cost, own_far_cost, other_near_cost, other_far_cost
    return sums, (near, far, other_near, other_far, drivers, *costs)


def per_device(rider_emb, driver_emb, log_a, log_b, rider_zone, driver_zone, zone_table):
    rider_msg, driver_msg = call(
        pack_body,
        [pltpu.VMEM((1, PAY, B), BF16), pltpu.VMEM((DB, PAY, B), BF16)],
        [FAR] * 7,
        [
            pltpu.VMEM((1, B), F32),
            pltpu.VMEM((1, B), F32),
            pltpu.SMEM((2,), jnp.int32),
            pltpu.SMEM((1,), jnp.int32),
            pltpu.SMEM((16, 16), jnp.int32),
            pltpu.SemaphoreType.DMA((7,)),
        ],
        limit=60,
    )(
        rider_emb.reshape(2, B, B), driver_emb, log_a.reshape(2, B), log_b.reshape(1, B),
        rider_zone, driver_zone, zone_table,
    )
    sums, gathered = rider_first(rider_msg, driver_msg)
    sums = close(sums, log_add)
    columns = pltpu.VMEM((RB * B, B), F32)
    sums, kernel, peaks, pots = call(
        driver_first_body,
        [f32(DB, DB, B), f32(RB * B, DB * B), f32(2 * DB, B), f32(2 * RB, B)],
        [VM] * 10,
        [columns],
    )(sums, *gathered)
    sums = exchange(sums, "z")
    columns = [columns, pltpu.VMEM((RB, B), F32)]
    sums, state = call(rider_second_body, [f32(RB, B), f32(3 * DB, B)], [VM] * 3)(
        sums, peaks, kernel
    )
    sums = close(sums, jnp.add)
    for _ in range(ITERS - 2):
        (sums,) = call(driver_next_body, [f32(DB, DB, B)], [VM] * 4, columns)(
            sums, pots, state, kernel
        )
        sums = exchange(sums, "z")
        (sums,) = call(rider_next_body, [f32(RB, B)], [VM] * 3, [pltpu.VMEM((DB, B), F32)])(
            sums, state, kernel
        )
        sums = close(sums, jnp.add)
    rider_sums = sums
    (sums,) = call(driver_last_body, [f32(DB, 8, B)], [VM] * 4, columns)(
        rider_sums, pots, state, kernel
    )
    sums = exchange(sums, "z")
    rider_pot, driver_pot = call(
        finish_body, [f32(2, B), f32(1, B)], [VM] * 4, [pltpu.VMEM((RB, B), F32)]
    )(sums, state, rider_sums, pots)
    return rider_pot.reshape(2 * B), driver_pot.reshape(B)


def solution(mesh):
    fine = Mesh(mesh.devices.reshape(SIZES), AXES)
    row, every = ("z", "yl", "x"), AXES
    placed = (
        P(row, None),
        P(every, None),
        P(row),
        P(every),
        P(row),
        P(every),
        P(),
    )
    return jax.shard_map(
        per_device,
        mesh=fine,
        in_specs=placed,
        out_specs=(P(row), P(every)),
        check_vma=False,
    )
```

```python
import math

import jax
import jax.numpy as jnp
from jax import lax
from jax.experimental import pallas as pl
from jax.experimental.pallas import tpu as pltpu
from jax.sharding import Mesh, PartitionSpec as P

AXES = ("z", "yl", "x", "yh", "c")
SIZES = (8, 2, 4, 2, 2)
PLANE = ("yl", "x", "yh")
PEERS = 16

B = 128
RB = 16
DB = 8
PAY = B + 16
ITERS = 3
LOG_DRIVERS = math.log(32768)
LOG_RIDERS = math.log(16384)
PENALTY = 1e30
FLOOR = -1e29
TINY = 1e-37

F32 = jnp.float32
BF16 = jnp.bfloat16
VM = pl.BlockSpec(memory_space=pltpu.VMEM)
FAR = pl.BlockSpec(memory_space=pltpu.HBM)


def call(body, outs, ins, scratch=(), limit=20):
    return pl.pallas_call(
        body,
        out_shape=outs,
        in_specs=ins,
        out_specs=[VM] * len(outs),
        scratch_shapes=list(scratch),
        compiler_params=pltpu.CompilerParams(vmem_limit_bytes=limit * 2**20),
    )


def f32(*shape):
    return jax.ShapeDtypeStruct(shape, F32)


def bf16(*shape):
    return jax.ShapeDtypeStruct(shape, BF16)


def product(left, right):
    return lax.dot_general(left, right, (((1,), (1,)), ((), ())), preferred_element_type=F32)


def tree(parts, op):
    while len(parts) > 1:
        parts = [op(parts[2 * k], parts[2 * k + 1]) for k in range(len(parts) // 2)]
    return parts[0]


def fold(block, op):
    return tree([block[8 * k : 8 * k + 8] for k in range(B // 8)], op)


def column(row):
    return jnp.broadcast_to(row, (B, B)).T


def three_parts(value):
    high = value.astype(BF16)
    rest = value - high.astype(F32)
    middle = rest.astype(BF16)
    return high, middle, (rest - middle.astype(F32)).astype(BF16)


def zone_rows(message):
    return jnp.broadcast_to(message[B : B + 1].astype(F32), (16, B)).astype(BF16)


def weight_row(message):
    tail = message[B:].astype(F32)
    return (tail[1:2] + tail[2:3]) + tail[3:4]


def with_zone(message, zone):
    return jnp.concatenate([message[:B], jnp.concatenate([zone] * (B // 16), axis=0)], axis=1)


def tail_rows(zone_row, log_row):
    row = lax.broadcasted_iota(jnp.int32, (16, B), 0)
    tail = jnp.where(row == 0, zone_row, 0.0)
    for k, part in enumerate(three_parts(log_row)):
        tail = jnp.where(row == k + 1, part.astype(F32), tail)
    return tail.astype(BF16)


def pack_body(rider, driver, log_a, log_b, rzone, dzone, table, rider_out, driver_out,
              a_row, b_row, rz, dz, tab, sems):
    c = lax.axis_index("c")
    copies = [
        pltpu.make_async_copy(rider.at[c], rider_out.at[0, pl.ds(0, B)], sems.at[0]),
        pltpu.make_async_copy(driver, driver_out.at[0, pl.ds(0, B)], sems.at[1]),
        pltpu.make_async_copy(log_a.at[pl.ds(c, 1)], a_row, sems.at[2]),
        pltpu.make_async_copy(log_b, b_row, sems.at[3]),
        pltpu.make_async_copy(rzone, rz, sems.at[4]),
        pltpu.make_async_copy(dzone, dz, sems.at[5]),
        pltpu.make_async_copy(table, tab, sems.at[6]),
    ]
    for copy in copies:
        copy.start()
    for copy in copies:
        copy.wait()
    lane = lax.broadcasted_iota(jnp.int32, (16, B), 1)
    hot = jnp.where(lane == rz[c], 1.0, 0.0)
    zone = dz[0]
    shut = jnp.zeros((16, B), F32)
    for k in range(16):
        shut = jnp.where((lane == k) & (tab[k, zone] != 1), PENALTY, shut)
    rider_out[0, B:, :] = tail_rows(hot, a_row[...])
    driver_out[0, B:, :] = tail_rows(shut, b_row[...])
    for k in range(1, DB):
        driver_out[k] = driver_out[0]


def place(far, slot):
    yl, x = lax.axis_index("yl"), lax.axis_index("x")
    x = x + slot // 2 * (3 - 2 * x)
    x = x + slot % 2 * (1 - 2 * (x % 2))
    return (yl + far * (1 - 2 * yl)) * 4 + x


def block_of(r):
    c = lax.axis_index("c")
    return 2 * place(r // 4 % 2, r % 4) + c + r // 8 * (1 - 2 * c)


def widen(messages, wide):
    for k, message in enumerate(messages):
        wide[k * B : (k + 1) * B] = with_zone(message, zone_rows(message))


def rider_rows(riders, drivers, cost, rows, first, left):
    widen([riders[k] for k in range(4)], left)
    for h in range(DB // 2):
        lanes = slice(2 * h * B, 2 * (h + 1) * B)
        cost[:, lanes] = product(left[...], drivers[lanes, :])
    for k in range(4):
        pieces = [cost[k * B : (k + 1) * B, j * B : (j + 1) * B] for j in range(DB)]
        low = tree(pieces, jnp.minimum)
        mass = tree([jnp.exp(low - piece) for piece in pieces], jnp.add).T
        low = low.T
        least = jnp.min(low, axis=0, keepdims=True)
        mass = jnp.sum(mass * jnp.exp(least - low), axis=0, keepdims=True)
        rows[first + k : first + k + 1, :] = jnp.log(mass) - least


def rider_first_body(own_near, own_far, other_near, other_far, driver, *rest):
    *costs, out, rows, wide, left = rest
    widen([driver[z] for z in range(DB)], wide)
    for k, riders in enumerate((own_near, own_far, other_near, other_far)):
        rider_rows(riders, wide, costs[k], rows, 4 * k, left)
    for r in range(RB):
        out[pl.ds(block_of(r), 1), :] = rows[r : r + 1]


def log_total(sums):
    parts = [sums[k] for k in range(sums.shape[0])]
    peak = tree(parts, jnp.maximum)
    return peak + jnp.log(tree([jnp.exp(part - peak) for part in parts], jnp.add))


def total_of(sums):
    return tree([sums[k] for k in range(sums.shape[0])], jnp.add)


def driver_first_body(sums, own_near, own_far, other_near, other_far, driver, *rest):
    *costs, out, kernel, peaks, pots, ucol = rest
    messages = (own_near, own_far, other_near, other_far)
    for r in range(RB):
        pots[pl.ds(RB + block_of(r), 1), :] = weight_row(messages[r // 4][r % 4])
    for j in range(DB):
        peaks[DB + j : DB + j + 1, :] = weight_row(driver[j])
    pots[0:RB] = pots[RB:] - (log_total(sums) - LOG_DRIVERS)
    for r in range(RB):
        ucol[r * B : (r + 1) * B, :] = column(pots[pl.ds(block_of(r), 1), :])

    def scores(r):
        u = ucol[r * B : (r + 1) * B, :]
        rows = slice(r % 4 * B, (r % 4 + 1) * B)
        return [u - costs[r // 4][rows, j * B : (j + 1) * B] for j in range(DB)]

    high = [jnp.full((8, B), FLOOR, F32)] * DB
    for r in range(RB):
        high = [jnp.maximum(h, fold(score, jnp.maximum)) for h, score in zip(high, scores(r))]
    top = [jnp.max(h, axis=0, keepdims=True) for h in high]
    total = [jnp.zeros((8, B), F32)] * DB
    for r in range(RB):
        for j, score in enumerate(scores(r)):
            term = jnp.exp(score - top[j])
            kernel[r * B : (r + 1) * B, j * B : (j + 1) * B] = term
            total[j] = total[j] + fold(term, jnp.add)
    for j in range(DB):
        mass = jnp.maximum(jnp.sum(total[j], axis=0, keepdims=True), TINY)
        peaks[j : j + 1] = top[j]
        out[0, j : j + 1] = top[j] + jnp.log(mass)
    for k in range(1, DB):
        out[k] = out[0]


def row_sums(kernel, scale, out):
    for r in range(RB):
        rows = slice(r * B, (r + 1) * B)
        acc = kernel[rows, 0:B] * scale[0:1]
        for k in range(1, DB):
            acc = acc + kernel[rows, k * B : (k + 1) * B] * scale[k : k + 1]
        out[pl.ds(block_of(r), 1), :] = jnp.sum(acc.T, axis=0, keepdims=True)


def column_sums(kernel, f, state, fcol, hold):
    hold[...] = f
    for r in range(RB):
        fcol[r * B : (r + 1) * B, :] = column(hold[pl.ds(block_of(r), 1), :])

    def block(r, acc):
        for k in range(B // 8):
            rows = pl.ds(pl.multiple_of(r * B + 8 * k, 8), 8)
            f = fcol[rows, :]
            acc = tuple(a + kernel[rows, j * B : (j + 1) * B] * f for j, a in enumerate(acc))
        return acc

    acc = lax.fori_loop(0, RB, block, tuple(jnp.zeros((8, B), F32) for _ in range(DB)))
    for j in range(DB):
        hold[j : j + 1, :] = jnp.sum(acc[j], axis=0, keepdims=True)
    return hold[0:DB] * state[2 * DB : 3 * DB]


def rider_second_body(sums, peaks, kernel, out, state):
    log_b = peaks[DB:]
    pot = log_b - (log_total(sums) - LOG_RIDERS)
    state[0:DB] = pot
    state[DB : 2 * DB] = log_b
    state[2 * DB :] = jnp.exp(pot + peaks[0:DB])
    row_sums(kernel, state.at[pl.ds(2 * DB, DB)], out)


def driver_next_body(sums, pots, state, kernel, out, fcol, hold):
    rows = column_sums(kernel, jnp.exp(pots[RB:] + LOG_DRIVERS) / total_of(sums), state, fcol, hold)
    for k in range(DB):
        out[k] = rows


def rider_next_body(sums, state, kernel, out, scale):
    scale[...] = state[2 * DB :] * (jnp.exp(state[DB : 2 * DB] + LOG_RIDERS) / total_of(sums))
    row_sums(kernel, scale, out)


def driver_last_body(sums, pots, state, kernel, out, fcol, hold):
    f = jnp.exp(pots[RB:] + LOG_DRIVERS) / total_of(sums)
    rows = column_sums(kernel, f, state, fcol, hold)
    for k in range(DB):
        out[k] = jnp.broadcast_to(rows[k : k + 1], (8, B))


def finish_body(sums, state, rider_sums, pots, rider_pot, driver_pot, hold):
    z = lax.axis_index("z")
    pot = state[pl.ds(z, 1), :]
    log_b = state[pl.ds(DB + z, 1), :]
    driver_pot[...] = pot + (log_b + LOG_RIDERS - jnp.log(total_of(sums)[0:1]))
    hold[...] = pots[0:RB] + (pots[RB:] + LOG_DRIVERS - jnp.log(total_of(rider_sums)))
    block = lax.axis_index("yl") * 4 + lax.axis_index("x")
    rider_pot[0:1] = hold[pl.ds(2 * block, 1), :]
    rider_pot[1:2] = hold[pl.ds(2 * block + 1, 1), :]


def exchange(message, axes):
    return lax.all_to_all(message, axes, 0, 0, tiled=True)


def swap(value, axis, partner):
    return lax.ppermute(value, axis, [(k, partner(k)) for k in range(SIZES[AXES.index(axis)])])


def from_y(value, step):
    place_of = lambda y: y % 2 * 2 + y // 2
    return lax.ppermute(
        value, ("yl", "yh"), [(place_of(y), place_of((y - step) % 4)) for y in range(4)]
    )


def log_add(a, b):
    peak = jnp.maximum(a, b)
    return peak + jnp.log(jnp.exp(a - peak) + jnp.exp(b - peak))


def close(value, op):
    value = op(value, swap(value, "c", lambda k: 1 - k))
    return exchange(jnp.broadcast_to(value[None], (PEERS, RB, B)), PLANE)


def gather(message, drivers):
    drivers = exchange(drivers, "z")
    beside, across, behind = (
        swap(message, "x", partner)
        for partner in (lambda k: k ^ 1, lambda k: 3 - k, lambda k: k ^ 2)
    )
    two = jnp.concatenate([message, beside], axis=0)
    mirror = jnp.concatenate([across, behind], axis=0)
    near = jnp.concatenate([two, mirror], axis=0)
    far = jnp.concatenate([from_y(two, 1), from_y(mirror, -1)], axis=0)
    other_near, other_far = (swap(value, "c", lambda k: 1 - k) for value in (near, far))
    return near, far, other_near, other_far, drivers


def per_device(rider_emb, driver_emb, log_a, log_b, rider_zone, driver_zone, zone_table):
    rider_msg, driver_msg = call(
        pack_body,
        [pltpu.VMEM((1, PAY, B), BF16), pltpu.VMEM((DB, PAY, B), BF16)],
        [FAR] * 7,
        [
            pltpu.VMEM((1, B), F32),
            pltpu.VMEM((1, B), F32),
            pltpu.SMEM((2,), jnp.int32),
            pltpu.SMEM((1,), jnp.int32),
            pltpu.SMEM((16, 16), jnp.int32),
            pltpu.SemaphoreType.DMA((7,)),
        ],
        limit=60,
    )(
        rider_emb.reshape(2, B, B), driver_emb, log_a.reshape(2, B), log_b.reshape(1, B),
        rider_zone, driver_zone, zone_table,
    )
    messages = gather(rider_msg, driver_msg)
    *costs, sums = call(
        rider_first_body,
        [f32(4 * B, DB * B)] * 4 + [f32(RB, B)],
        [VM] * 5,
        [
            pltpu.VMEM((RB, B), F32),
            pltpu.VMEM((DB * B, 2 * B), BF16),
            pltpu.VMEM((4 * B, 2 * B), BF16),
        ],
    )(*messages)
    sums = close(sums, log_add)
    columns = pltpu.VMEM((RB * B, B), F32)
    sums, kernel, peaks, pots = call(
        driver_first_body,
        [f32(DB, DB, B), f32(RB * B, DB * B), f32(2 * DB, B), f32(2 * RB, B)],
        [VM] * 10,
        [columns],
    )(sums, *messages, *costs)
    sums = exchange(sums, "z")
    columns = [columns, pltpu.VMEM((RB, B), F32)]
    sums, state = call(rider_second_body, [f32(RB, B), f32(3 * DB, B)], [VM] * 3)(
        sums, peaks, kernel
    )
    sums = close(sums, jnp.add)
    for _ in range(ITERS - 2):
        (sums,) = call(driver_next_body, [f32(DB, DB, B)], [VM] * 4, columns)(
            sums, pots, state, kernel
        )
        sums = exchange(sums, "z")
        (sums,) = call(rider_next_body, [f32(RB, B)], [VM] * 3, [pltpu.VMEM((DB, B), F32)])(
            sums, state, kernel
        )
        sums = close(sums, jnp.add)
    rider_sums = sums
    (sums,) = call(driver_last_body, [f32(DB, 8, B)], [VM] * 4, columns)(
        rider_sums, pots, state, kernel
    )
    sums = exchange(sums, "z")
    rider_pot, driver_pot = call(
        finish_body, [f32(2, B), f32(1, B)], [VM] * 4, [pltpu.VMEM((RB, B), F32)]
    )(sums, state, rider_sums, pots)
    return rider_pot.reshape(2 * B), driver_pot.reshape(B)


def solution(mesh):
    fine = Mesh(mesh.devices.reshape(SIZES), AXES)
    row, every = ("z", "yl", "x"), AXES
    placed = (
        P(row, None),
        P(every, None),
        P(row),
        P(every),
        P(row),
        P(every),
        P(),
    )
    return jax.shard_map(
        per_device,
        mesh=fine,
        in_specs=placed,
        out_specs=(P(row), P(every)),
        check_vma=False,
    )
```

```python
import math

import jax
import jax.numpy as jnp
from jax import lax
from jax.experimental import pallas as pl
from jax.experimental.pallas import tpu as pltpu
from jax.sharding import Mesh, PartitionSpec as P

AXES = ("z", "yl", "x", "yh", "c")
SIZES = (8, 2, 4, 2, 2)
PLANE = ("yl", "x", "yh")
PEERS = 16

B = 128
RB = 16
DB = 8
PAY = B + 16
ITERS = 3
LOG_DRIVERS = math.log(32768)
LOG_RIDERS = math.log(16384)
PENALTY = 1e30
FLOOR = -1e29
TINY = 1e-37

F32 = jnp.float32
BF16 = jnp.bfloat16
VM = pl.BlockSpec(memory_space=pltpu.VMEM)
FAR = pl.BlockSpec(memory_space=pltpu.HBM)


def call(body, outs, ins, scratch=(), limit=20):
    return pl.pallas_call(
        body,
        out_shape=outs,
        in_specs=ins,
        out_specs=[VM] * len(outs),
        scratch_shapes=list(scratch),
        compiler_params=pltpu.CompilerParams(vmem_limit_bytes=limit * 2**20),
    )


def f32(*shape):
    return jax.ShapeDtypeStruct(shape, F32)


def bf16(*shape):
    return jax.ShapeDtypeStruct(shape, BF16)


def product(left, right):
    return lax.dot_general(left, right, (((1,), (1,)), ((), ())), preferred_element_type=F32)


def tree(parts, op):
    while len(parts) > 1:
        parts = [op(parts[2 * k], parts[2 * k + 1]) for k in range(len(parts) // 2)]
    return parts[0]


def fold(block, op):
    return tree([block[8 * k : 8 * k + 8] for k in range(B // 8)], op)


def column(row):
    return jnp.broadcast_to(row, (B, B)).T


def three_parts(value):
    high = value.astype(BF16)
    rest = value - high.astype(F32)
    middle = rest.astype(BF16)
    return high, middle, (rest - middle.astype(F32)).astype(BF16)


def zone_rows(message):
    return jnp.broadcast_to(message[B : B + 1].astype(F32), (16, B)).astype(BF16)


def weight_row(message):
    tail = message[B:].astype(F32)
    return (tail[1:2] + tail[2:3]) + tail[3:4]


def with_zone(message, zone):
    return jnp.concatenate([message[:B], jnp.concatenate([zone] * (B // 16), axis=0)], axis=1)


def tail_rows(zone_row, log_row):
    row = lax.broadcasted_iota(jnp.int32, (16, B), 0)
    tail = jnp.where(row == 0, zone_row, 0.0)
    for k, part in enumerate(three_parts(log_row)):
        tail = jnp.where(row == k + 1, part.astype(F32), tail)
    return tail.astype(BF16)


def pack_body(rider, driver, log_a, log_b, rzone, dzone, table, rider_out, driver_out,
              a_row, b_row, rz, dz, tab, sems):
    c = lax.axis_index("c")
    copies = [
        pltpu.make_async_copy(rider.at[c], rider_out.at[0, pl.ds(0, B)], sems.at[0]),
        pltpu.make_async_copy(driver, driver_out.at[0, pl.ds(0, B)], sems.at[1]),
        pltpu.make_async_copy(log_a.at[pl.ds(c, 1)], a_row, sems.at[2]),
        pltpu.make_async_copy(log_b, b_row, sems.at[3]),
        pltpu.make_async_copy(rzone, rz, sems.at[4]),
        pltpu.make_async_copy(dzone, dz, sems.at[5]),
        pltpu.make_async_copy(table, tab, sems.at[6]),
    ]
    for copy in copies:
        copy.start()
    for copy in copies:
        copy.wait()
    lane = lax.broadcasted_iota(jnp.int32, (16, B), 1)
    hot = jnp.where(lane == rz[c], 1.0, 0.0)
    zone = dz[0]
    shut = jnp.zeros((16, B), F32)
    for k in range(16):
        shut = jnp.where((lane == k) & (tab[k, zone] != 1), PENALTY, shut)
    rider_out[0, B:, :] = tail_rows(hot, a_row[...])
    driver_out[0, B:, :] = tail_rows(shut, b_row[...])
    for k in range(1, DB):
        driver_out[k] = driver_out[0]


def place(far, slot):
    yl, x = lax.axis_index("yl"), lax.axis_index("x")
    x = x + slot // 2 * (3 - 2 * x)
    x = x + slot % 2 * (1 - 2 * (x % 2))
    return (yl + far * (1 - 2 * yl)) * 4 + x


def block_of(r):
    c = lax.axis_index("c")
    return 2 * place(r // 4 % 2, r % 4) + c + r // 8 * (1 - 2 * c)


def widen(messages, wide):
    for k, message in enumerate(messages):
        wide[k * B : (k + 1) * B] = with_zone(message, zone_rows(message))


def rider_rows(riders, drivers, cost, rows, first, left):
    widen([riders[k] for k in range(4)], left)
    for h in range(DB // 2):
        lanes = slice(2 * h * B, 2 * (h + 1) * B)
        cost[:, lanes] = product(left[...], drivers[lanes, :])
    for k in range(4):
        pieces = [cost[k * B : (k + 1) * B, j * B : (j + 1) * B] for j in range(DB)]
        low = tree(pieces, jnp.minimum)
        mass = tree([jnp.exp(low - piece) for piece in pieces], jnp.add).T
        low = low.T
        least = jnp.min(low, axis=0, keepdims=True)
        mass = jnp.sum(mass * jnp.exp(least - low), axis=0, keepdims=True)
        rows[first + k : first + k + 1, :] = jnp.log(mass) - least


def rider_early_body(own_near, own_far, other_near, driver, *rest):
    *costs, rows, wide, left = rest
    widen([driver[z] for z in range(DB)], wide)
    for k, riders in enumerate((own_near, own_far, other_near)):
        rider_rows(riders, wide, costs[k], rows, 4 * k, left)


def rider_late_body(other_far, wide, early, cost, out, rows, left):
    rider_rows(other_far, wide, cost, rows, 0, left)
    for r in range(RB):
        row = early[r : r + 1] if r < 12 else rows[r - 12 : r - 11]
        out[pl.ds(block_of(r), 1), :] = row


def log_total(sums):
    parts = [sums[k] for k in range(sums.shape[0])]
    peak = tree(parts, jnp.maximum)
    return peak + jnp.log(tree([jnp.exp(part - peak) for part in parts], jnp.add))


def total_of(sums):
    return tree([sums[k] for k in range(sums.shape[0])], jnp.add)


def driver_first_body(sums, own_near, own_far, other_near, other_far, driver, *rest):
    *costs, out, kernel, peaks, pots, ucol = rest
    messages = (own_near, own_far, other_near, other_far)
    for r in range(RB):
        pots[pl.ds(RB + block_of(r), 1), :] = weight_row(messages[r // 4][r % 4])
    for j in range(DB):
        peaks[DB + j : DB + j + 1, :] = weight_row(driver[j])
    pots[0:RB] = pots[RB:] - (log_total(sums) - LOG_DRIVERS)
    for r in range(RB):
        ucol[r * B : (r + 1) * B, :] = column(pots[pl.ds(block_of(r), 1), :])

    def scores(r):
        u = ucol[r * B : (r + 1) * B, :]
        rows = slice(r % 4 * B, (r % 4 + 1) * B)
        return [u - costs[r // 4][rows, j * B : (j + 1) * B] for j in range(DB)]

    high = [jnp.full((8, B), FLOOR, F32)] * DB
    for r in range(RB):
        high = [jnp.maximum(h, fold(score, jnp.maximum)) for h, score in zip(high, scores(r))]
    top = [jnp.max(h, axis=0, keepdims=True) for h in high]
    total = [jnp.zeros((8, B), F32)] * DB
    for r in range(RB):
        for j, score in enumerate(scores(r)):
            term = jnp.exp(score - top[j])
            kernel[r * B : (r + 1) * B, j * B : (j + 1) * B] = term
            total[j] = total[j] + fold(term, jnp.add)
    for j in range(DB):
        mass = jnp.maximum(jnp.sum(total[j], axis=0, keepdims=True), TINY)
        peaks[j : j + 1] = top[j]
        out[0, j : j + 1] = top[j] + jnp.log(mass)
    for k in range(1, DB):
        out[k] = out[0]


def row_sums(kernel, scale, out):
    for r in range(RB):
        rows = slice(r * B, (r + 1) * B)
        acc = kernel[rows, 0:B] * scale[0:1]
        for k in range(1, DB):
            acc = acc + kernel[rows, k * B : (k + 1) * B] * scale[k : k + 1]
        out[pl.ds(block_of(r), 1), :] = jnp.sum(acc.T, axis=0, keepdims=True)


def column_sums(kernel, f, state, fcol, hold):
    hold[...] = f
    for r in range(RB):
        fcol[r * B : (r + 1) * B, :] = column(hold[pl.ds(block_of(r), 1), :])

    def block(r, acc):
        for k in range(B // 8):
            rows = pl.ds(pl.multiple_of(r * B + 8 * k, 8), 8)
            f = fcol[rows, :]
            acc = tuple(a + kernel[rows, j * B : (j + 1) * B] * f for j, a in enumerate(acc))
        return acc

    acc = lax.fori_loop(0, RB, block, tuple(jnp.zeros((8, B), F32) for _ in range(DB)))
    for j in range(DB):
        hold[j : j + 1, :] = jnp.sum(acc[j], axis=0, keepdims=True)
    return hold[0:DB] * state[2 * DB : 3 * DB]


def rider_second_body(sums, peaks, kernel, out, state):
    log_b = peaks[DB:]
    pot = log_b - (log_total(sums) - LOG_RIDERS)
    state[0:DB] = pot
    state[DB : 2 * DB] = log_b
    state[2 * DB :] = jnp.exp(pot + peaks[0:DB])
    row_sums(kernel, state.at[pl.ds(2 * DB, DB)], out)


def driver_next_body(sums, pots, state, kernel, out, fcol, hold):
    rows = column_sums(kernel, jnp.exp(pots[RB:] + LOG_DRIVERS) / total_of(sums), state, fcol, hold)
    for k in range(DB):
        out[k] = rows


def rider_next_body(sums, state, kernel, out, scale):
    scale[...] = state[2 * DB :] * (jnp.exp(state[DB : 2 * DB] + LOG_RIDERS) / total_of(sums))
    row_sums(kernel, scale, out)


def driver_last_body(sums, pots, state, kernel, out, fcol, hold):
    f = jnp.exp(pots[RB:] + LOG_DRIVERS) / total_of(sums)
    rows = column_sums(kernel, f, state, fcol, hold)
    for k in range(DB):
        out[k] = jnp.broadcast_to(rows[k : k + 1], (8, B))


def finish_body(sums, state, rider_sums, pots, rider_pot, driver_pot, hold):
    z = lax.axis_index("z")
    pot = state[pl.ds(z, 1), :]
    log_b = state[pl.ds(DB + z, 1), :]
    driver_pot[...] = pot + (log_b + LOG_RIDERS - jnp.log(total_of(sums)[0:1]))
    hold[...] = pots[0:RB] + (pots[RB:] + LOG_DRIVERS - jnp.log(total_of(rider_sums)))
    block = lax.axis_index("yl") * 4 + lax.axis_index("x")
    rider_pot[0:1] = hold[pl.ds(2 * block, 1), :]
    rider_pot[1:2] = hold[pl.ds(2 * block + 1, 1), :]


def exchange(message, axes):
    return lax.all_to_all(message, axes, 0, 0, tiled=True)


def swap(value, axis, partner):
    return lax.ppermute(value, axis, [(k, partner(k)) for k in range(SIZES[AXES.index(axis)])])


def from_y(value, step):
    place_of = lambda y: y % 2 * 2 + y // 2
    return lax.ppermute(
        value, ("yl", "yh"), [(place_of(y), place_of((y - step) % 4)) for y in range(4)]
    )


def log_add(a, b):
    peak = jnp.maximum(a, b)
    return peak + jnp.log(jnp.exp(a - peak) + jnp.exp(b - peak))


def close(value, op):
    value = op(value, swap(value, "c", lambda k: 1 - k))
    return exchange(jnp.broadcast_to(value[None], (PEERS, RB, B)), PLANE)


def gather(message, drivers):
    drivers = exchange(drivers, "z")
    beside, across, behind = (
        swap(message, "x", partner)
        for partner in (lambda k: k ^ 1, lambda k: 3 - k, lambda k: k ^ 2)
    )
    two = jnp.concatenate([message, beside], axis=0)
    mirror = jnp.concatenate([across, behind], axis=0)
    near = jnp.concatenate([two, mirror], axis=0)
    far = jnp.concatenate([from_y(two, 1), from_y(mirror, -1)], axis=0)
    other_near, other_far = (swap(value, "c", lambda k: 1 - k) for value in (near, far))
    return near, far, other_near, other_far, drivers


def per_device(rider_emb, driver_emb, log_a, log_b, rider_zone, driver_zone, zone_table):
    rider_msg, driver_msg = call(
        pack_body,
        [pltpu.VMEM((1, PAY, B), BF16), pltpu.VMEM((DB, PAY, B), BF16)],
        [FAR] * 7,
        [
            pltpu.VMEM((1, B), F32),
            pltpu.VMEM((1, B), F32),
            pltpu.SMEM((2,), jnp.int32),
            pltpu.SMEM((1,), jnp.int32),
            pltpu.SMEM((16, 16), jnp.int32),
            pltpu.SemaphoreType.DMA((7,)),
        ],
        limit=60,
    )(
        rider_emb.reshape(2, B, B), driver_emb, log_a.reshape(2, B), log_b.reshape(1, B),
        rider_zone, driver_zone, zone_table,
    )
    messages = gather(rider_msg, driver_msg)
    own_near, own_far, other_near, other_far, driver = messages
    cost, left = f32(4 * B, DB * B), pltpu.VMEM((4 * B, 2 * B), BF16)
    *costs, rows, wide = call(
        rider_early_body, [cost] * 3 + [f32(12, B), bf16(DB * B, 2 * B)], [VM] * 4, [left]
    )(own_near, own_far, other_near, driver)
    last, sums = call(
        rider_late_body, [cost, f32(RB, B)], [VM] * 3, [pltpu.VMEM((4, B), F32), left]
    )(other_far, wide, rows)
    costs.append(last)
    sums = close(sums, log_add)
    columns = pltpu.VMEM((RB * B, B), F32)
    sums, kernel, peaks, pots = call(
        driver_first_body,
        [f32(DB, DB, B), f32(RB * B, DB * B), f32(2 * DB, B), f32(2 * RB, B)],
        [VM] * 10,
        [columns],
    )(sums, *messages, *costs)
    sums = exchange(sums, "z")
    columns = [columns, pltpu.VMEM((RB, B), F32)]
    sums, state = call(rider_second_body, [f32(RB, B), f32(3 * DB, B)], [VM] * 3)(
        sums, peaks, kernel
    )
    sums = close(sums, jnp.add)
    for _ in range(ITERS - 2):
        (sums,) = call(driver_next_body, [f32(DB, DB, B)], [VM] * 4, columns)(
            sums, pots, state, kernel
        )
        sums = exchange(sums, "z")
        (sums,) = call(rider_next_body, [f32(RB, B)], [VM] * 3, [pltpu.VMEM((DB, B), F32)])(
            sums, state, kernel
        )
        sums = close(sums, jnp.add)
    rider_sums = sums
    (sums,) = call(driver_last_body, [f32(DB, 8, B)], [VM] * 4, columns)(
        rider_sums, pots, state, kernel
    )
    sums = exchange(sums, "z")
    rider_pot, driver_pot = call(
        finish_body, [f32(2, B), f32(1, B)], [VM] * 4, [pltpu.VMEM((RB, B), F32)]
    )(sums, state, rider_sums, pots)
    return rider_pot.reshape(2 * B), driver_pot.reshape(B)


def solution(mesh):
    fine = Mesh(mesh.devices.reshape(SIZES), AXES)
    row, every = ("z", "yl", "x"), AXES
    placed = (
        P(row, None),
        P(every, None),
        P(row),
        P(every),
        P(row),
        P(every),
        P(),
    )
    return jax.shard_map(
        per_device,
        mesh=fine,
        in_specs=placed,
        out_specs=(P(row), P(every)),
        check_vma=False,
    )
```

```python
import math

import jax
import jax.numpy as jnp
from jax import lax
from jax.experimental import pallas as pl
from jax.experimental.pallas import tpu as pltpu
from jax.sharding import Mesh, PartitionSpec as P

AXES = ("z", "yl", "x", "yh", "c")
SIZES = (8, 2, 4, 2, 2)
PLANE = ("yl", "x", "yh")
PEERS = 16

B = 128
RB = 16
DB = 8
PAY = B + 16
ITERS = 3
LOG_DRIVERS = math.log(32768)
LOG_RIDERS = math.log(16384)
PENALTY = 1e30
FLOOR = -1e29
TINY = 1e-37

F32 = jnp.float32
BF16 = jnp.bfloat16
VM = pl.BlockSpec(memory_space=pltpu.VMEM)
FAR = pl.BlockSpec(memory_space=pltpu.HBM)


def call(body, outs, ins, scratch=(), limit=20):
    return pl.pallas_call(
        body,
        out_shape=outs,
        in_specs=ins,
        out_specs=[VM] * len(outs),
        scratch_shapes=list(scratch),
        compiler_params=pltpu.CompilerParams(vmem_limit_bytes=limit * 2**20),
    )


def f32(*shape):
    return jax.ShapeDtypeStruct(shape, F32)


def bf16(*shape):
    return jax.ShapeDtypeStruct(shape, BF16)


def product(left, right):
    return lax.dot_general(left, right, (((1,), (1,)), ((), ())), preferred_element_type=F32)


def tree(parts, op):
    while len(parts) > 1:
        parts = [op(parts[2 * k], parts[2 * k + 1]) for k in range(len(parts) // 2)]
    return parts[0]


def fold(block, op):
    return tree([block[8 * k : 8 * k + 8] for k in range(B // 8)], op)


def column(row):
    return jnp.broadcast_to(row, (B, B)).T


def three_parts(value):
    high = value.astype(BF16)
    rest = value - high.astype(F32)
    middle = rest.astype(BF16)
    return high, middle, (rest - middle.astype(F32)).astype(BF16)


def zone_rows(message):
    return jnp.broadcast_to(message[B:].astype(F32)[0:1], (16, B)).astype(BF16)


def weight_row(message):
    tail = message[B:].astype(F32)
    return (tail[1:2] + tail[2:3]) + tail[3:4]


def with_zone(message, zone):
    return jnp.concatenate([message[:B], jnp.concatenate([zone] * (B // 16), axis=0)], axis=1)


def tail_rows(zone_row, log_row):
    row = lax.broadcasted_iota(jnp.int32, (16, B), 0)
    tail = jnp.where(row == 0, zone_row, 0.0)
    for k, part in enumerate(three_parts(log_row)):
        tail = jnp.where(row == k + 1, part.astype(F32), tail)
    return tail.astype(BF16)


def pack_body(rider, driver, log_a, log_b, rzone, dzone, table, rider_out, driver_out,
              a_row, b_row, rz, dz, tab, sems):
    c = lax.axis_index("c")
    copies = [
        pltpu.make_async_copy(rider.at[c], rider_out.at[0, pl.ds(0, B)], sems.at[0]),
        pltpu.make_async_copy(driver, driver_out.at[0, pl.ds(0, B)], sems.at[1]),
        pltpu.make_async_copy(log_a.at[pl.ds(c, 1)], a_row, sems.at[2]),
        pltpu.make_async_copy(log_b, b_row, sems.at[3]),
        pltpu.make_async_copy(rzone, rz, sems.at[4]),
        pltpu.make_async_copy(dzone, dz, sems.at[5]),
        pltpu.make_async_copy(table, tab, sems.at[6]),
    ]
    for copy in copies:
        copy.start()
    for copy in copies:
        copy.wait()
    lane = lax.broadcasted_iota(jnp.int32, (16, B), 1)
    hot = jnp.where(lane == rz[c], 1.0, 0.0)
    zone = dz[0]
    shut = jnp.zeros((16, B), F32)
    for k in range(16):
        shut = jnp.where((lane == k) & (tab[k, zone] != 1), PENALTY, shut)
    rider_out[0, B:, :] = tail_rows(hot, a_row[...])
    driver_out[0, B:, :] = tail_rows(shut, b_row[...])
    for k in range(1, DB):
        driver_out[k] = driver_out[0]


def place(far, slot):
    yl, x = lax.axis_index("yl"), lax.axis_index("x")
    x = x + slot // 2 * (3 - 2 * x)
    x = x + slot % 2 * (1 - 2 * (x % 2))
    return (yl + far * (1 - 2 * yl)) * 4 + x


def block_of(r):
    c = lax.axis_index("c")
    return 2 * place(r // 4 % 2, r % 4) + c + r // 8 * (1 - 2 * c)


def widen(messages, wide):
    for k, message in enumerate(messages):
        wide[k * B : (k + 1) * B] = with_zone(message, zone_rows(message))


def rider_rows(riders, drivers, cost, rows, first, left):
    widen([riders[k] for k in range(4)], left)
    for h in range(DB // 2):
        lanes = slice(2 * h * B, 2 * (h + 1) * B)
        cost[:, lanes] = product(left[...], drivers[lanes, :])
    for k in range(4):
        pieces = [cost[k * B : (k + 1) * B, j * B : (j + 1) * B] for j in range(DB)]
        low = tree(pieces, jnp.minimum)
        mass = tree([jnp.exp(low - piece) for piece in pieces], jnp.add).T
        low = low.T
        least = jnp.min(low, axis=0, keepdims=True)
        mass = jnp.sum(mass * jnp.exp(least - low), axis=0, keepdims=True)
        rows[first + k : first + k + 1, :] = jnp.log(mass) - least


def rider_first_body(own_near, own_far, other_near, other_far, driver, *rest):
    *costs, out, rows, wide, left = rest
    widen([driver[z] for z in range(DB)], wide)
    for k, riders in enumerate((own_near, own_far, other_near, other_far)):
        rider_rows(riders, wide, costs[k], rows, 4 * k, left)
    for r in range(RB):
        out[pl.ds(block_of(r), 1), :] = rows[r : r + 1]


def log_total(sums):
    parts = [sums[k] for k in range(sums.shape[0])]
    peak = tree(parts, jnp.maximum)
    return peak + jnp.log(tree([jnp.exp(part - peak) for part in parts], jnp.add))


def total_of(sums):
    return tree([sums[k] for k in range(sums.shape[0])], jnp.add)


def driver_first_body(sums, own_near, own_far, other_near, other_far, driver, *rest):
    *costs, out, kernel, peaks, pots, ucol = rest
    messages = (own_near, own_far, other_near, other_far)
    for r in range(RB):
        pots[pl.ds(RB + block_of(r), 1), :] = weight_row(messages[r // 4][r % 4])
    for j in range(DB):
        peaks[DB + j : DB + j + 1, :] = weight_row(driver[j])
    pots[0:RB] = pots[RB:] - (log_total(sums) - LOG_DRIVERS)
    for r in range(RB):
        ucol[r * B : (r + 1) * B, :] = column(pots[pl.ds(block_of(r), 1), :])

    def scores(r):
        u = ucol[r * B : (r + 1) * B, :]
        rows = slice(r % 4 * B, (r % 4 + 1) * B)
        return [u - costs[r // 4][rows, j * B : (j + 1) * B] for j in range(DB)]

    high = [jnp.full((8, B), FLOOR, F32)] * DB
    for r in range(RB):
        high = [jnp.maximum(h, fold(score, jnp.maximum)) for h, score in zip(high, scores(r))]
    top = [jnp.max(h, axis=0, keepdims=True) for h in high]
    total = [jnp.zeros((8, B), F32)] * DB
    for r in range(RB):
        for j, score in enumerate(scores(r)):
            term = jnp.exp(score - top[j])
            kernel[r * B : (r + 1) * B, j * B : (j + 1) * B] = term
            total[j] = total[j] + fold(term, jnp.add)
    for j in range(DB):
        mass = jnp.maximum(jnp.sum(total[j], axis=0, keepdims=True), TINY)
        peaks[j : j + 1] = top[j]
        out[0, j : j + 1] = top[j] + jnp.log(mass)
    for k in range(1, DB):
        out[k] = out[0]


def row_sums(kernel, scale, out):
    for r in range(RB):
        rows = slice(r * B, (r + 1) * B)
        acc = kernel[rows, 0:B] * scale[0:1]
        for k in range(1, DB):
            acc = acc + kernel[rows, k * B : (k + 1) * B] * scale[k : k + 1]
        out[pl.ds(block_of(r), 1), :] = jnp.sum(acc.T, axis=0, keepdims=True)


def column_sums(kernel, f, state, fcol, hold):
    hold[...] = f
    for r in range(RB):
        fcol[r * B : (r + 1) * B, :] = column(hold[pl.ds(block_of(r), 1), :])

    def block(r, acc):
        for k in range(B // 8):
            rows = pl.ds(pl.multiple_of(r * B + 8 * k, 8), 8)
            f = fcol[rows, :]
            acc = tuple(a + kernel[rows, j * B : (j + 1) * B] * f for j, a in enumerate(acc))
        return acc

    acc = lax.fori_loop(0, RB, block, tuple(jnp.zeros((8, B), F32) for _ in range(DB)))
    for j in range(DB):
        hold[j : j + 1, :] = jnp.sum(acc[j], axis=0, keepdims=True)
    return hold[0:DB] * state[2 * DB : 3 * DB]


def rider_second_body(sums, peaks, kernel, out, state):
    log_b = peaks[DB:]
    pot = log_b - (log_total(sums) - LOG_RIDERS)
    state[0:DB] = pot
    state[DB : 2 * DB] = log_b
    state[2 * DB :] = jnp.exp(pot + peaks[0:DB])
    row_sums(kernel, state.at[pl.ds(2 * DB, DB)], out)


def driver_next_body(sums, pots, state, kernel, out, fcol, hold):
    rows = column_sums(kernel, jnp.exp(pots[RB:] + LOG_DRIVERS) / total_of(sums), state, fcol, hold)
    for k in range(DB):
        out[k] = rows


def rider_next_body(sums, state, kernel, out, scale):
    scale[...] = state[2 * DB :] * (jnp.exp(state[DB : 2 * DB] + LOG_RIDERS) / total_of(sums))
    row_sums(kernel, scale, out)


def driver_last_body(sums, pots, state, kernel, out, fcol, hold):
    f = jnp.exp(pots[RB:] + LOG_DRIVERS) / total_of(sums)
    rows = column_sums(kernel, f, state, fcol, hold)
    for k in range(DB):
        out[k] = jnp.broadcast_to(rows[k : k + 1], (8, B))


def finish_body(sums, state, rider_sums, pots, rider_pot, driver_pot, hold):
    z = lax.axis_index("z")
    pot = state[pl.ds(z, 1), :]
    log_b = state[pl.ds(DB + z, 1), :]
    driver_pot[...] = pot + (log_b + LOG_RIDERS - jnp.log(total_of(sums)[0:1]))
    hold[...] = pots[0:RB] + (pots[RB:] + LOG_DRIVERS - jnp.log(total_of(rider_sums)))
    block = lax.axis_index("yl") * 4 + lax.axis_index("x")
    rider_pot[0:1] = hold[pl.ds(2 * block, 1), :]
    rider_pot[1:2] = hold[pl.ds(2 * block + 1, 1), :]


def exchange(message, axes):
    return lax.all_to_all(message, axes, 0, 0, tiled=True)


def swap(value, axis, partner):
    return lax.ppermute(value, axis, [(k, partner(k)) for k in range(SIZES[AXES.index(axis)])])


def from_y(value, step):
    place_of = lambda y: y % 2 * 2 + y // 2
    return lax.ppermute(
        value, ("yl", "yh"), [(place_of(y), place_of((y - step) % 4)) for y in range(4)]
    )


def log_add(a, b):
    peak = jnp.maximum(a, b)
    return peak + jnp.log(jnp.exp(a - peak) + jnp.exp(b - peak))


def close(value, op):
    value = op(value, swap(value, "c", lambda k: 1 - k))
    return exchange(jnp.broadcast_to(value[None], (PEERS, RB, B)), PLANE)


def gather(message, drivers):
    drivers = exchange(drivers, "z")
    beside, across, behind = (
        swap(message, "x", partner)
        for partner in (lambda k: k ^ 1, lambda k: 3 - k, lambda k: k ^ 2)
    )
    two = jnp.concatenate([message, beside], axis=0)
    mirror = jnp.concatenate([across, behind], axis=0)
    near = jnp.concatenate([two, mirror], axis=0)
    far = jnp.concatenate([from_y(two, 1), from_y(mirror, -1)], axis=0)
    other_near, other_far = (swap(value, "c", lambda k: 1 - k) for value in (near, far))
    return near, far, other_near, other_far, drivers


def per_device(rider_emb, driver_emb, log_a, log_b, rider_zone, driver_zone, zone_table):
    rider_msg, driver_msg = call(
        pack_body,
        [pltpu.VMEM((1, PAY, B), BF16), pltpu.VMEM((DB, PAY, B), BF16)],
        [FAR] * 7,
        [
            pltpu.VMEM((1, B), F32),
            pltpu.VMEM((1, B), F32),
            pltpu.SMEM((2,), jnp.int32),
            pltpu.SMEM((1,), jnp.int32),
            pltpu.SMEM((16, 16), jnp.int32),
            pltpu.SemaphoreType.DMA((7,)),
        ],
        limit=60,
    )(
        rider_emb.reshape(2, B, B), driver_emb, log_a.reshape(2, B), log_b.reshape(1, B),
        rider_zone, driver_zone, zone_table,
    )
    messages = gather(rider_msg, driver_msg)
    *costs, sums = call(
        rider_first_body,
        [f32(4 * B, DB * B)] * 4 + [f32(RB, B)],
        [VM] * 5,
        [
            pltpu.VMEM((RB, B), F32),
            pltpu.VMEM((DB * B, 2 * B), BF16),
            pltpu.VMEM((4 * B, 2 * B), BF16),
        ],
    )(*messages)
    sums = close(sums, log_add)
    columns = pltpu.VMEM((RB * B, B), F32)
    sums, kernel, peaks, pots = call(
        driver_first_body,
        [f32(DB, DB, B), f32(RB * B, DB * B), f32(2 * DB, B), f32(2 * RB, B)],
        [VM] * 10,
        [columns],
    )(sums, *messages, *costs)
    sums = exchange(sums, "z")
    columns = [columns, pltpu.VMEM((RB, B), F32)]
    sums, state = call(rider_second_body, [f32(RB, B), f32(3 * DB, B)], [VM] * 3)(
        sums, peaks, kernel
    )
    sums = close(sums, jnp.add)
    for _ in range(ITERS - 2):
        (sums,) = call(driver_next_body, [f32(DB, DB, B)], [VM] * 4, columns)(
            sums, pots, state, kernel
        )
        sums = exchange(sums, "z")
        (sums,) = call(rider_next_body, [f32(RB, B)], [VM] * 3, [pltpu.VMEM((DB, B), F32)])(
            sums, state, kernel
        )
        sums = close(sums, jnp.add)
    rider_sums = sums
    (sums,) = call(driver_last_body, [f32(DB, 8, B)], [VM] * 4, columns)(
        rider_sums, pots, state, kernel
    )
    sums = exchange(sums, "z")
    rider_pot, driver_pot = call(
        finish_body, [f32(2, B), f32(1, B)], [VM] * 4, [pltpu.VMEM((RB, B), F32)]
    )(sums, state, rider_sums, pots)
    return rider_pot.reshape(2 * B), driver_pot.reshape(B)


def solution(mesh):
    fine = Mesh(mesh.devices.reshape(SIZES), AXES)
    row, every = ("z", "yl", "x"), AXES
    placed = (
        P(row, None),
        P(every, None),
        P(row),
        P(every),
        P(row),
        P(every),
        P(),
    )
    return jax.shard_map(
        per_device,
        mesh=fine,
        in_specs=placed,
        out_specs=(P(row), P(every)),
        check_vma=False,
    )
```
